32 devices in a mesh: batch: 2 (over x), seq: 4 (over z), pool: 4 (over y, core).
Axes of the slice: x: 2, y: 2, z: 4, core: 2. Of those that a mesh axis runs over, the one named last changes fastest.
Arguments:
- tokens: bfloat16 [8, 1024, 1024], P(('batch', 'pool'), 'seq'), may hold values from -6 to 6
- w_in: bfloat16 [1024, 4096], replicated, may hold values from -0.1875 to 0.1875
- w_out: bfloat16 [1024, 1024], replicated, may hold values from -0.1875 to 0.1875
- w_proj: bfloat16 [1024, 256], replicated, may hold values from -0.1875 to 0.1875
- pos_embed: bfloat16 [8, 1024, 256], P(('batch', 'pool'), 'seq'), may hold values from -6 to 6
- pos_ids: int32 [8, 1024], P(('batch', 'pool'), 'seq'), may hold values from 0 to 1048575
- lengths: int32 [8], P(('batch', 'pool')), may hold values from 128 to 1024, as said below
- neg_embed: bfloat16 [2, 4096, 256], P('batch', 'pool'), may hold values from -0.375 to 0.375
- neg_ids: int32 [2, 4096], P('batch', 'pool'), may hold values from 0 to 1048575
Outputs:
- loss: float32 [8, 1024], P(('batch', 'pool'), 'seq')
- d_neg: float32 [2, 4096, 256], P('batch', 'pool', 'seq')
- d_proj: float32 [1024, 256], replicated
The draws below stay inside these ranges and needn't reach their ends.
Inputs may be any that keep to these rules, and one draw needn't show every extreme that they name: `lengths`: every history has at least one valid event; in every draw one history is valid over all 1024 events.
All inputs are finite; a program needn't handle non-finite values.
Results may differ from the reference program's by a relative error of at most 0.017.
Values may be sent and summed in bfloat16 or wider, within the bound.
No kernel may reach another device: no remote copies, remote signals or barrier semaphores. Data moves between devices by JAX's collectives and lax.ppermute only.
A program may use at most 128 MiB of HBM per device.

```python
import math
import jax
import jax.numpy as jnp
import numpy as np
from jax import lax

D = 1024
HEADS = 8
E = 256
NEG = 4096
ITEMS = 1048576
LEN = 1024
HIST = 8
N_BATCH = 2
N_POOL = 4


def draw_lengths(key, part):
    key = jax.random.fold_in(key, 11)
    key_len, key_top = jax.random.split(key)
    drawn = jax.random.randint(key_len, (HIST,), LEN // 8, LEN + 1)
    chosen = jax.random.randint(key_top, (), 0, HIST)
    return jnp.where(jnp.arange(HIST) == chosen, LEN, drawn).astype(jnp.int32)


def touch_ends(values, rng, smallest, largest):
    longest = values.shape.index(max(values.shape))
    spots = []
    for shift in (0, 1):
        where = [jax.random.randint(jax.random.fold_in(rng, axis), (), 0, length) for axis, length in enumerate(values.shape)]
        where[longest] = (where[longest] + shift) % values.shape[longest]
        spots.append(tuple(where))
    return values.at[spots[0]].set(smallest).at[spots[1]].set(largest)


def block_scale(key, shape, cuts, smallest, high):
    gain, own = 1.0, jax.random.fold_in(key, 6)
    for position, shards_of in cuts:
        draws = jnp.exp(jax.random.uniform(jax.random.fold_in(own, position), (shards_of,), jnp.float32, smallest / len(cuts), high / len(cuts)))
        gain = gain * jnp.repeat(draws, shape[position] // shards_of).reshape([-1 if axis == position else 1 for axis in range(len(shape))])
    return gain


def skewed_wide(rng, shape, amount, skew):
    loads = [min(1 << octave, amount + 1 - (1 << octave)) * (1 << 20) // math.isqrt((1 << octave) ** skew) + 1 for octave in range((amount + 1).bit_length()) if 1 << octave <= amount]
    scale = 1 + sum(loads) // (1 << 30)
    grid = np.cumsum(np.array([max(1, weight // scale) for weight in loads]))
    lot = jax.random.randint(jax.random.fold_in(rng, 1), shape, 0, int(grid[len(loads) - 1]))
    start = jnp.left_shift(1, jnp.searchsorted(jnp.asarray(grid, jnp.int32), lot, side="right").astype(jnp.int32))
    grade = start - 1 + jax.random.randint(jax.random.fold_in(rng, 4), shape, 0, 1 << 30) % jnp.minimum(start, amount + 1 - start)
    return jax.random.permutation(jax.random.fold_in(rng, 2), amount)[grade].astype(jnp.int32)


def normal_values(own_key, dims, deviation, reach, cuts=(), kind=jnp.bfloat16):
    gain = block_scale(own_key, dims, cuts, -0.22, 0.18) if cuts else 1.0
    entries = jax.random.normal(own_key, dims, jnp.float32) * deviation * gain
    return jnp.minimum(jnp.maximum(entries, -reach), reach).astype(kind)


def setup_inputs(seed: int = 0) -> dict:
    arg_keys = jax.random.split(jax.random.key(seed), 10)
    return {
        "tokens": normal_values(arg_keys[0], (HIST, LEN, D), 1.0, 6.0, ((0, 8), (1, 4))),
        "w_in": normal_values(arg_keys[1], (D, 4 * D), D ** -0.5, 0.1875),
        "w_out": normal_values(arg_keys[2], (D, D), D ** -0.5, 0.1875),
        "w_proj": normal_values(arg_keys[3], (D, E), D ** -0.5, 0.1875),
        "pos_embed": normal_values(arg_keys[4], (HIST, LEN, E), 1.0, 6.0, ((0, 8), (1, 4))),
        "pos_ids": touch_ends(skewed_wide(arg_keys[5], (HIST, LEN), ITEMS, 2), jax.random.fold_in(arg_keys[5], 3), 0, ITEMS - 1).astype(jnp.int32),
        "lengths": draw_lengths(jax.random.fold_in(arg_keys[9], 71), 0),
        "neg_embed": normal_values(arg_keys[7], (N_BATCH, NEG, E), E ** -0.5, 0.375, ((0, 2), (1, 4))),
        "neg_ids": touch_ends(skewed_wide(arg_keys[8], (N_BATCH, NEG), ITEMS, 2), jax.random.fold_in(arg_keys[8], 3), 0, ITEMS - 1).astype(jnp.int32),
    }


SOFTMAX_WARMTH = 0.02
NORM_EPSILON = 1e-05
UNIT_EPSILON = 1e-06

def layer_norm(inputs):
    center = inputs - lax.optimization_barrier(jnp.mean(inputs, axis=-1, keepdims=True))
    spread = lax.optimization_barrier(jnp.mean(center * center, axis=-1, keepdims=True))
    return center / jnp.sqrt(spread + NORM_EPSILON)

def unit_rows(inputs):
    norms = jnp.sqrt(lax.optimization_barrier(jnp.sum(inputs * inputs, axis=-1, keepdims=True)) + UNIT_EPSILON)
    return (inputs / norms, norms)

def log_sample_chance(item_ids):
    ranks = item_ids.astype(jnp.float32) + 1.0
    return jnp.log(jnp.log1p(1.0 / ranks)) - jnp.log(jnp.log(jnp.float32(ITEMS) + 1.0))

def head_split(block):
    return block.reshape(block.shape[0], HEADS, block.shape[1] // HEADS).transpose(1, 0, 2)

def attend(query_block, query_pos, key_block, value_block, key_pos, length):
    width = query_block.shape[1]
    head_width = width // HEADS
    allowed = (key_pos[None, :] <= query_pos[:, None]) & (key_pos[None, :] < length)

    def one_head(parts):
        query_head, key_head, value_head = parts
        scores = jnp.dot(query_head, key_head.T, preferred_element_type=jnp.float32) / math.sqrt(head_width)
        weights = jnp.where(allowed, jax.nn.silu(scores), 0.0).astype(jnp.bfloat16)
        return jnp.dot(weights, value_head, preferred_element_type=jnp.float32)
    result = lax.map(one_head, (head_split(query_block), head_split(key_block), head_split(value_block)))
    return result.transpose(1, 0, 2).reshape(query_block.shape[0], width)

def reference(tokens, w_in, w_out, w_proj, pos_embed, pos_ids, lengths, neg_embed, neg_ids):
    unit_negs, neg_norms = unit_rows(neg_embed.astype(jnp.float32))
    negative_estimate = unit_negs.astype(jnp.bfloat16)
    positions = jnp.arange(LEN, dtype=jnp.int32)
    groups = jnp.arange(HIST, dtype=jnp.int32) // N_POOL

    def per_history(parts):
        history, pos_rows, positive_targets, length, group = parts
        width = history.shape[1]
        normed = layer_norm(history.astype(jnp.float32)).astype(jnp.bfloat16)
        mixed = jax.nn.silu(jnp.dot(normed, w_in, preferred_element_type=jnp.float32))
        gate_u = mixed[:, :width].astype(jnp.bfloat16)
        values = mixed[:, width:2 * width].astype(jnp.bfloat16)
        queries = mixed[:, 2 * width:3 * width].astype(jnp.bfloat16)
        keys = mixed[:, 3 * width:].astype(jnp.bfloat16)
        attn = attend(queries, positions, keys, values, positions, length)
        gated = (layer_norm(attn) * gate_u.astype(jnp.float32)).astype(jnp.bfloat16)
        layer_out = (jnp.dot(gated, w_out, preferred_element_type=jnp.float32) + history.astype(jnp.float32)).astype(jnp.bfloat16)
        out_unit, out_norms = unit_rows(jnp.dot(layer_out, w_proj, preferred_element_type=jnp.float32))
        output_estimate = out_unit.astype(jnp.bfloat16)
        positive_direction = unit_rows(pos_rows.astype(jnp.float32))[0]
        valid = positions < length
        group_estimate = negative_estimate[group]
        group_labels = neg_ids[group]
        positive_score = lax.optimization_barrier(jnp.sum(output_estimate.astype(jnp.float32) * positive_direction, axis=-1)) / SOFTMAX_WARMTH - log_sample_chance(positive_targets)
        negative_score = jnp.dot(output_estimate, group_estimate.T, preferred_element_type=jnp.float32) / SOFTMAX_WARMTH - log_sample_chance(group_labels)[None, :]
        kept = jnp.where(group_labels[None, :] != positive_targets[:, None], jnp.exp(negative_score), 0.0)
        total = jnp.exp(positive_score) + lax.optimization_barrier(jnp.sum(kept, axis=-1))
        loss = jnp.where(valid, jnp.log(total) - positive_score, 0.0)
        negative_weights = (jnp.where(valid[:, None], kept / total[:, None], 0.0) / HIST).astype(jnp.bfloat16)
        positive_weight = jnp.where(valid, jnp.exp(positive_score) / total - 1.0, 0.0) / HIST
        negative_portion = jnp.dot(negative_weights.T, output_estimate, preferred_element_type=jnp.float32) / SOFTMAX_WARMTH
        unit_gradient = (positive_weight[:, None] * positive_direction + jnp.dot(negative_weights, group_estimate, preferred_element_type=jnp.float32)) / SOFTMAX_WARMTH
        d_out = ((unit_gradient - out_unit * lax.optimization_barrier(jnp.sum(out_unit * unit_gradient, axis=-1, keepdims=True))) / out_norms).astype(jnp.bfloat16)
        proj_part = jnp.dot(layer_out.T, d_out, preferred_element_type=jnp.float32)
        return (loss, negative_portion, proj_part)
    loss, neg_parts, proj_parts = lax.map(per_history, (tokens, pos_embed, pos_ids, lengths, groups))
    neg_sum = lax.optimization_barrier(jnp.sum(neg_parts.reshape(N_BATCH, N_POOL, NEG, E), axis=1))
    d_neg = (neg_sum - unit_negs * lax.optimization_barrier(jnp.sum(unit_negs * neg_sum, axis=-1, keepdims=True))) / neg_norms
    d_proj = lax.optimization_barrier(jnp.sum(proj_parts, axis=0))
    return (loss, d_neg, d_proj)
```

```python
import functools
import itertools
import math

import jax
import jax.numpy as jnp
from jax import lax
from jax.experimental import pallas as pl
from jax.experimental.pallas import tpu as pltpu
from jax.sharding import PartitionSpec as P

HEADS = 8
ITEMS = 1048576

SOFTMAX_WARMTH = 0.02
NORM_EPSILON = 1e-05
UNIT_EPSILON = 1e-06
LOG2E = math.log2(math.e)
SCORE_SCALE = LOG2E / SOFTMAX_WARMTH
FAR = 10000.0

F32 = jnp.float32
BF16 = jnp.bfloat16
MIB = 1 << 20


def log_sample_chance(item_ids):
    x = 1.0 / (item_ids + 1.0)
    series = x * (1.0 - x * (1 / 2 - x * (1 / 3 - x * (1 / 4 - x * (1 / 5 - x * (1 / 6))))))
    return jnp.log(jnp.where(x > 1 / 16, jnp.log(1.0 + x), series)) - math.log(math.log(ITEMS + 1.0))


def column(row):
    return jnp.broadcast_to(row, (128, row.shape[1])).T[:, :1]


def dot(a, b):
    return jnp.dot(a, b, preferred_element_type=F32)


def dot_t(a, b):
    return lax.dot_general(a, b, (((1,), (1,)), ((), ())), preferred_element_type=F32)


def t_dot(a, b):
    return lax.dot_general(a, b, (((0,), (0,)), ((), ())), preferred_element_type=F32)


def silu(v):
    half = 0.5 * v
    return half + half * jnp.tanh(half)


def row_norm(x, keep=None):
    center = x - jnp.mean(x, axis=-1, keepdims=True)
    scale = lax.rsqrt(jnp.mean(center * center, axis=-1, keepdims=True) + NORM_EPSILON)
    if keep is not None:
        scale = jnp.where(keep, scale, 0.0)
    return center * scale


def norm_of(x):
    return jnp.sqrt(jnp.sum(x * x, axis=-1, keepdims=True) + UNIT_EPSILON)


def kept_rows(first, rows, length):
    return first + lax.broadcasted_iota(jnp.int32, (rows, 1), 0) < length


def attend(q_ref, keys, values, acc_ref, before_ref, causal=None):
    rows, width = q_ref.shape
    head = width // HEADS
    for h in range(HEADS):
        cols = slice(h * head, (h + 1) * head)
        half = dot_t(q_ref[:, cols], keys[:, cols]) * (0.5 / math.sqrt(head))
        weights = half + half * jnp.tanh(half)
        if causal is not None:
            weights = jnp.where(causal, weights, 0.0)
        part = dot(weights.astype(BF16), values[:, cols])
        acc_ref[:, cols] = part if before_ref is None else before_ref[:, cols] + part


def project(normed, w_ref, block):
    width = normed.shape[1]
    return silu(dot(normed, w_ref[:, block * width : (block + 1) * width])).astype(BF16)


def causal_mask(rows):
    return lax.broadcasted_iota(jnp.int32, (rows, rows), 0) >= lax.broadcasted_iota(jnp.int32, (rows, rows), 1)


def own_kernel(info_ref, x_ref, w_ref, gate_ref, q_ref, k_ref, v_ref, acc_ref):
    rows = x_ref.shape[0]
    keep = kept_rows(info_ref[0], rows, info_ref[1])
    normed = row_norm(x_ref[...].astype(F32), keep).astype(BF16)
    gate_ref[...] = project(normed, w_ref, 0)
    q_ref[...] = project(normed, w_ref, 2)
    keys, values = project(normed, w_ref, 3), project(normed, w_ref, 1)
    k_ref[...] = keys
    v_ref[...] = values
    attend(q_ref, keys, values, acc_ref, None, causal_mask(rows))


def guest_kernel(info_ref, x_ref, w_ref, k_ref, v_ref, gate_ref, q_ref, acc_ref):
    rows = x_ref.shape[0]
    keep = kept_rows(info_ref[0] + rows, rows, info_ref[1])
    normed = row_norm(x_ref[...].astype(F32), keep).astype(BF16)
    gate_ref[...] = project(normed, w_ref, 0)
    q_ref[...] = project(normed, w_ref, 2)
    attend(q_ref, project(normed, w_ref, 3), project(normed, w_ref, 1), acc_ref, None, causal_mask(rows))
    attend(q_ref, k_ref[...], v_ref[...], acc_ref, acc_ref)


def add_block(info_ref, back, x_ref, w_ref, q_refs, acc_refs, before_refs):
    keep = kept_rows(info_ref[0] - back, x_ref.shape[0], info_ref[1])
    normed = row_norm(x_ref[...].astype(F32), keep).astype(BF16)
    keys, values = project(normed, w_ref, 3), project(normed, w_ref, 1)
    for q_ref, acc_ref, before_ref in zip(q_refs, acc_refs, before_refs):
        attend(q_ref, keys, values, acc_ref, before_ref)


def step_kernel(back, info_ref, x_ref, w_ref, *refs):
    add_block(info_ref, back, x_ref, w_ref, refs[:2], refs[4:], refs[2:4])


def last_kernel(back, info_ref, x_ref, w_ref, *refs):
    q_refs, before_refs, gate_refs, own_refs = refs[:2], refs[2:4], refs[4:6], refs[6:8]
    w_out_ref, w_proj_ref, layer_ref, out_ref, hat_ref, *acc_refs = refs[8:]
    add_block(info_ref, back, x_ref, w_ref, q_refs, acc_refs, before_refs)
    gated = [
        (row_norm(acc_ref[...]) * gate_ref[...].astype(F32)).astype(BF16)
        for acc_ref, gate_ref in zip(acc_refs, gate_refs)
    ]
    rest = jnp.concatenate([own_ref[...] for own_ref in own_refs], axis=0).astype(F32)
    layer = (dot(jnp.concatenate(gated, axis=0), w_out_ref[...]) + rest).astype(BF16)
    layer_ref[...] = layer
    out = dot(layer, w_proj_ref[...])
    out_ref[...] = out
    hat_ref[...] = (out / norm_of(out)).astype(BF16)


def split3(x):
    high = x.astype(BF16).astype(F32)
    mid = (x - high).astype(BF16).astype(F32)
    return [high, mid, x - high - mid]


def id_digits(ids):
    return [(ids >> 14).astype(F32), ((ids >> 7) & 127).astype(F32), (ids & 127).astype(F32)]


def of_digits(a, b, c):
    return a * 16384.0 + b * 128.0 + c


def padded_rows(count):
    return -(-count // 16) * 16


def table_kernel(x_ref, ids_ref, pos_ref, pos_ids_ref, table_ref, message_ref):
    count, embed = x_ref.shape
    x = x_ref[...].astype(F32)
    table_ref[:count, :] = (x / norm_of(x)).astype(BF16)
    ids = jnp.concatenate([ids_ref[:, i : i + embed] for i in range(0, count, embed)], axis=0)
    parts = split3(log_sample_chance(ids.astype(F32)) * LOG2E) + id_digits(ids)
    used = len(parts) * ids.shape[0]
    pad = jnp.zeros((table_ref.shape[0] - count - used, embed), F32)
    table_ref[count:, :] = jnp.concatenate(parts + [pad], axis=0).astype(BF16)
    rows = pos_ref.shape[0]
    parts = id_digits(pos_ids_ref[...])
    pad = jnp.zeros((message_ref.shape[0] - rows - len(parts), embed), F32)
    message_ref[:rows, :] = pos_ref[...]
    message_ref[rows:, :] = jnp.concatenate(parts + [pad], axis=0).astype(BF16)


def head_kernel(
    hist_count, info_ref, hat_ref, out_ref, layer_ref, pos_ref, ids_ref, guest_ref, *rest
):
    *table_refs, loss_ref, guest_loss_ref, message_ref, keep_ref, send_ref, proj_ref = rest
    rows, embed = hat_ref.shape
    block = rows // 2
    chunks = table_refs[0].shape[0] // (embed + 6)
    count = chunks * embed
    hat = hat_ref[...]
    guest_parts = guest_ref[block:, :].astype(F32)
    id_rows = [id_digits(ids_ref[...]), [guest_parts[i : i + 1, :] for i in range(3)]]
    id_row = jnp.concatenate([of_digits(*digits) for digits in id_rows], axis=1)
    pos_id = column(id_row)
    pos = jnp.concatenate([pos_ref[...], guest_ref[:block, :]], axis=0).astype(F32)
    pos_unit = pos / norm_of(pos)
    pos_score = (
        jnp.sum(hat.astype(F32) * pos_unit, axis=-1, keepdims=True) / SOFTMAX_WARMTH - column(log_sample_chance(id_row))
    )
    lanes = jnp.zeros((rows, 128), F32)
    grads = jnp.zeros((rows, embed), F32)
    for table_ref in table_refs:
        parts = table_ref[count:, :].astype(F32)
        for chunk in range(chunks):
            bias, ids = (
                [parts[(g + j) * chunks + chunk : (g + j) * chunks + chunk + 1, :] for j in range(3)]
                for g in (0, 3)
            )
            table = table_ref[chunk * embed : (chunk + 1) * embed, :]
            scores = dot_t(hat, table) * SCORE_SCALE - (bias[0] + bias[1] + bias[2])
            kept = jnp.where(of_digits(*ids) != pos_id, jnp.exp2(scores), 0.0)
            for lane in range(0, embed, 128):
                lanes = lanes + kept[:, lane : lane + 128]
            grads = grads + dot(kept.astype(BF16), table)
    pos_part = jnp.exp(pos_score)
    total = pos_part + jnp.sum(lanes, axis=-1, keepdims=True)
    log_total = jnp.log(total)
    at = lax.broadcasted_iota(jnp.int32, (rows, 1), 0)
    valid = info_ref[0] + at < jnp.where(at < block, info_ref[5], info_ref[6])
    loss = jnp.where(valid, log_total - pos_score, 0.0)
    shift = jnp.where(valid, (log_total + math.log(hist_count)) * LOG2E, FAR)
    loss = jnp.broadcast_to(loss, (rows, 128)).T
    loss_ref[...] = loss[:1, :block]
    guest_loss_ref[...] = loss[:1, block:]
    shift = jnp.broadcast_to(shift, (rows, 128)).T
    parts = []
    for i in range(2):
        parts += split3(shift[:1, i * block : (i + 1) * block]) + id_rows[i]
    pad = jnp.zeros((message_ref.shape[0] - rows - len(parts), embed), F32)
    message_ref[:rows, :] = hat
    message_ref[rows:, :] = jnp.concatenate(parts + [pad], axis=0).astype(BF16)
    share = jnp.where(valid, 1.0 / (total * hist_count), 0.0)
    pos_weight = jnp.where(valid, pos_part / total - 1.0, 0.0) / hist_count
    d_unit = (pos_weight * pos_unit + share * grads) / SOFTMAX_WARMTH
    out = out_ref[...]
    norms = norm_of(out)
    unit = out / norms
    d_out = ((d_unit - unit * jnp.sum(unit * d_unit, axis=-1, keepdims=True)) / norms).astype(BF16)
    proj_ref[...] = t_dot(layer_ref[...], d_out)
    half = keep_ref.shape[0]
    keep_ref[...] = proj_ref[part_at(info_ref[3], half), :]
    send_ref[...] = proj_ref[part_at(1 - info_ref[3], half), :].astype(BF16)


def part_at(index, rows):
    return pl.ds(pl.multiple_of(index * rows, rows), rows)


def halved_kernel(info_ref, keep_ref, got_ref, own_ref, *rest):
    *send_refs, sum_ref = rest
    rows = own_ref.shape[0]
    sum_ref[...] = keep_ref[...] + got_ref[...].astype(F32)
    own_ref[...] = sum_ref[part_at(info_ref[4], rows), :]
    for r, send_ref in enumerate(send_refs, 1):
        send_ref[...] = sum_ref[part_at(lax.bitwise_xor(info_ref[4], r), rows), :].astype(BF16)


def sum_kernel(*refs):
    parts = [ref[...].astype(F32) for ref in refs[:-1]]
    while len(parts) > 1:
        parts = [a + b for a, b in zip(parts[::2], parts[1::2])]
    refs[-1][...] = parts[0].astype(refs[-1].dtype)


def lay_kernel(slot, info_ref, *refs):
    *part_refs, out_ref = refs
    rows = part_refs[0].shape[0]
    for r, part_ref in enumerate(part_refs):
        at = part_at(lax.bitwise_xor(info_ref[slot], r), rows)
        out_ref[at, :] = part_ref[...].astype(out_ref.dtype)


def cut_blocks(values, keep_ref, send_ref, rows):
    for i in range(values.shape[0] // rows):
        to_ref = send_ref if i % 2 else keep_ref
        to_ref[i // 2 * rows : (i // 2 + 1) * rows, :] = values[i * rows : (i + 1) * rows, :].astype(to_ref.dtype)


def halving_kernel(rows, keep_ref, got_ref, next_keep_ref, next_send_ref):
    cut_blocks(keep_ref[...] + got_ref[: keep_ref.shape[0], :].astype(F32), next_keep_ref, next_send_ref, rows)


def loss_kernel(last, info_ref, loss_ref, got_ref, own_loss_ref):
    rows = loss_ref.shape[1]
    parts = got_ref[got_ref.shape[0] - 16 :, :rows].astype(F32)
    above = parts[0:1, :] + parts[1:2, :] + parts[2:3, :]
    own_loss_ref[...] = jnp.where(info_ref[2] == last, above, loss_ref[...])


def negative_kernel(seq_count, info_ref, neg_ref, neg_id_ref, loss_ref, *rest):
    *message_refs, keep_ref, send_ref, turned_ref, sum_ref = rest
    count, embed = neg_ref.shape
    rows = embed
    blocks = message_refs[0].shape[0] // rows
    tile = min(256, count)
    neg = neg_ref[...].astype(F32)
    norms = norm_of(neg)
    unit = neg / norms
    neg_hat = unit.astype(BF16)
    id_row = neg_id_ref[...].astype(F32)
    neg_id = column(id_row)
    for i, (message_ref, block) in enumerate(itertools.product(message_refs, range(blocks))):
        hats = message_ref[block * rows : (block + 1) * rows, :]
        parts = message_ref[blocks * rows :, :].astype(F32)[6 * block : 6 * block + 6, :]
        shifts = parts[0:1, :] + parts[1:2, :] + parts[2:3, :]
        ids = of_digits(parts[3:4, :], parts[4:5, :], parts[5:6, :])
        for start in range(0, count, tile):
            cut = slice(start, start + tile)
            scores = dot_t(neg_hat[cut, :], hats) * SCORE_SCALE - shifts
            weights = jnp.where(neg_id[cut, :] != ids, jnp.exp2(scores), 0.0)
            term = dot(weights.astype(BF16), hats)
            sum_ref[cut, :] = sum_ref[cut, :] + term if i else term
    neg_sum = sum_ref[...] * column(jnp.exp2(-LOG2E * log_sample_chance(id_row)) / SOFTMAX_WARMTH)
    grad = (neg_sum - unit * jnp.sum(unit * neg_sum, axis=-1, keepdims=True)) / norms
    turned_ref[...] = grad.T
    kept = keep_ref.shape[0]
    cols = kept // (seq_count // 2)
    for r in range(seq_count):
        at = part_at(lax.bitwise_xor(info_ref[2], r), cols)
        to_ref = send_ref if r % 2 else keep_ref
        to_ref[r // 2 * cols : (r // 2 + 1) * cols, :] = turned_ref[at, :].astype(to_ref.dtype)
    parts = split3(loss_ref[...])
    pad = jnp.zeros((16 - len(parts), loss_ref.shape[1]), F32)
    send_ref[kept:, :] = jnp.zeros((16, count), BF16)
    send_ref[kept:, : loss_ref.shape[1]] = jnp.concatenate(parts + [pad], axis=0).astype(BF16)


def call(kernel, ins, outs, scratch=(), limit=24, flops=0, moved=0, name=None):
    in_specs = [pl.BlockSpec(memory_space=pltpu.SMEM if x.ndim == 1 else pltpu.VMEM) for x in ins]
    many = isinstance(outs, (list, tuple))
    out_specs = jax.tree.map(lambda _: pl.BlockSpec(memory_space=pltpu.VMEM), outs)
    return pl.pallas_call(
        kernel,
        out_shape=list(outs) if many else outs,
        in_specs=in_specs,
        out_specs=list(out_specs) if many else out_specs,
        scratch_shapes=list(scratch),
        compiler_params=pltpu.CompilerParams(vmem_limit_bytes=limit * MIB),
        cost_estimate=pl.CostEstimate(flops=flops, bytes_accessed=moved, transcendentals=0),
        name=name,
    )(*ins)


def swap(x, axis, count, r):
    return lax.ppermute(x, axis, [(i, i ^ r) for i in range(count)])


def gather_step(blocks, axis, count):
    bit = count // (2 * len(blocks))
    return blocks + [swap(block, axis, count, bit) for block in blocks] if bit else blocks


def together(*trees):
    return lax.optimization_barrier(trees)


def struct(shape, kind):
    return jax.ShapeDtypeStruct(shape, kind)


def body(tokens, w_in, w_out, w_proj, pos_embed, pos_ids, lengths, neg_embed, neg_ids):
    rows, width = tokens.shape[1:]
    embed = w_proj.shape[1]
    seq_count = lax.axis_size("seq")
    pool_count = lax.axis_size("pool")
    plane = ("batch", "pool")
    plane_count = lax.axis_size("batch") * pool_count
    seq_at = lax.axis_index("seq")
    plane_at = lax.axis_index("batch") * pool_count + lax.axis_index("pool")
    own_end = jnp.where(seq_at == seq_count - 1, 0, lengths[0])
    guest_end = jnp.where(seq_at == seq_count - 2, lengths[0], 0)
    info = jnp.stack([seq_at * rows, lengths[0], seq_at, plane_at % 2, plane_at // 2, own_end, guest_end])
    info = info.astype(jnp.int32)
    own = tokens[0]
    local_neg = neg_embed.shape[1]

    up = [(i, i + 1) for i in range(seq_count - 2)]
    down = [(seq_count - 1, seq_count - 2)]
    block = lax.ppermute(own, "seq", up)
    guest = lax.ppermute(own, "seq", down)
    kind = struct((rows, width), BF16)
    wide = struct((rows, width), F32)
    gate, queries, keys, values, acc = call(
        own_kernel,
        [info, own, w_in],
        [kind, kind, kind, kind, wide],
        flops=2 * rows * width * (w_in.shape[1] + 2 * rows),
        moved=2 * w_in.size,
        name="own_block",
    )
    table_part, pos_part = call(
        table_kernel,
        [neg_embed[0], neg_ids, pos_embed[0], pos_ids],
        [
            struct((local_neg + padded_rows(6 * local_neg // embed), embed), BF16),
            struct((rows + 16, embed), BF16),
        ],
        name="table_part",
    )
    table_part, pos_part, acc = together(table_part, pos_part, acc)
    table = gather_step([table_part], "pool", pool_count)
    block, guest, acc = together(block, guest, acc)
    for step in range(1, seq_count - 2):
        following = lax.ppermute(block, "seq", up)
        if step == 1:
            guest_gate, guest_queries, guest_acc = call(
                guest_kernel, [info, guest, w_in, keys, values], [kind, kind, wide], name="guest_block"
            )
        acc, guest_acc = call(
            functools.partial(step_kernel, step * rows),
            [info, block, w_in, queries, guest_queries, acc, guest_acc],
            [wide, wide],
            name=f"earlier_block_{step}",
        )
        acc, table, pos_part = together(acc, table, pos_part)
        if step == 1:
            guest_pos = lax.ppermute(pos_part, "seq", down)
        table = gather_step(table, "pool", pool_count)
        block, acc = together(following, acc)
    while len(table) < pool_count:
        table = gather_step(table, "pool", pool_count)
    layer, out, hat = call(
        functools.partial(last_kernel, (seq_count - 2) * rows),
        [info, block, w_in, queries, guest_queries, acc, guest_acc, gate, guest_gate, own, guest, w_out, w_proj],
        [struct((2 * rows, width), BF16), struct((2 * rows, embed), F32), struct((2 * rows, embed), BF16)],
        scratch=[pltpu.VMEM((rows, width), F32)] * 2,
        flops=2 * rows * width * (4 * width + 4 * rows + 2 * embed),
        moved=6 * width * width,
        name="last_block",
    )

    half, chips = width // 2, plane_count // 2
    loss, guest_loss, message, keep, send = call(
        functools.partial(head_kernel, plane_count),
        [info, hat, out, layer, pos_embed[0], pos_ids, guest_pos, *table],
        [
            struct((1, rows), F32), struct((1, rows), F32), struct((2 * rows + 16, embed), BF16),
            struct((half, embed), F32), struct((half, embed), BF16),
        ],
        scratch=[pltpu.VMEM((width, embed), F32)],
        flops=8 * rows * local_neg * pool_count * embed,
        moved=2 * local_neg * pool_count * embed,
        name="head",
    )
    part = struct((half // chips, embed), BF16)
    cols = embed // seq_count
    def plane_swap(parts):
        return [swap(x, plane, plane_count, 2 * r) for r, x in enumerate(parts, 1)]

    got = swap(send, plane, plane_count, 1)
    messages = gather_step([message], "pool", pool_count)
    own_part, *sends = call(
        halved_kernel,
        [info, keep, got],
        [struct(part.shape, F32)] + [part] * (chips - 1),
        scratch=[pltpu.VMEM((half, embed), F32)],
        name="halved",
    )
    own_part, messages = together(own_part, messages)
    while len(messages) < pool_count:
        messages = gather_step(messages, "pool", pool_count)
    proj_parts = [own_part] + plane_swap(sends)
    keep, send = call(
        functools.partial(negative_kernel, seq_count),
        [info, neg_embed[0], neg_ids, guest_loss, *messages],
        [struct((embed // 2, local_neg), F32), struct((embed // 2 + 16, local_neg), BF16)],
        scratch=[pltpu.VMEM((embed, local_neg), F32), pltpu.VMEM((local_neg, embed), F32)],
        name="neg_grad",
    )
    proj_parts, keep, send = together(proj_parts, keep, send)
    proj_part = call(sum_kernel, proj_parts, part, name="plane_sum")
    bit = 1
    while bit < seq_count:
        if bit == 1:
            proj_part, send = together(proj_part, send)
        proj_got, got = swap(proj_part, "seq", seq_count, bit), swap(send, "seq", seq_count, bit)
        proj_part = call(sum_kernel, [proj_part, proj_got], part, name=f"seq_sum_{bit}")
        if 2 * bit < seq_count:
            if bit == 1:
                loss = call(
                    functools.partial(loss_kernel, seq_count - 1), [info, loss, got], struct((1, rows), F32), name="loss"
                )
            size = keep.shape[0] // 2
            keep, send = call(
                functools.partial(halving_kernel, cols),
                [keep, got],
                [struct((size, local_neg), F32), struct((size, local_neg), BF16)],
                name=f"neg_halved_{bit}",
            )
        bit *= 2
    proj_parts, got = together([proj_part] + plane_swap([proj_part] * (chips - 1)), got)
    proj_half = call(
        functools.partial(lay_kernel, 4), [info, *proj_parts], struct((half, embed), BF16), name="lay_half"
    )
    other_half = swap(proj_half, plane, plane_count, 1)
    d_neg = call(sum_kernel, [keep, got], struct((cols, local_neg), F32), name="neg_sum")
    d_proj = call(
        functools.partial(lay_kernel, 3), [info, proj_half, other_half], struct((width, embed), F32), name="lay_whole"
    )
    return (loss, d_neg.T[None], d_proj)


def solution(mesh):
    placed = (
        P(("batch", "pool"), "seq", None),
        P(),
        P(),
        P(),
        P(("batch", "pool"), "seq", None),
        P(("batch", "pool"), "seq"),
        P(("batch", "pool")),
        P("batch", "pool", None),
        P("batch", "pool"),
    )
    return jax.shard_map(
        body,
        mesh=mesh,
        in_specs=placed,
        out_specs=(P(("batch", "pool"), "seq"), P("batch", "pool", "seq"), P()),
        check_vma=False,
    )
```

```python
import functools
import itertools
import math

import jax
import jax.numpy as jnp
from jax import lax
from jax.experimental import pallas as pl
from jax.experimental.pallas import tpu as pltpu
from jax.sharding import PartitionSpec as P

HEADS = 8
ITEMS = 1048576

SOFTMAX_WARMTH = 0.02
NORM_EPSILON = 1e-05
UNIT_EPSILON = 1e-06
LOG2E = math.log2(math.e)
SCORE_SCALE = LOG2E / SOFTMAX_WARMTH
FAR = 10000.0

F32 = jnp.float32
BF16 = jnp.bfloat16
MIB = 1 << 20


def log_sample_chance(item_ids):
    x = 1.0 / (item_ids + 1.0)
    series = x * (1.0 - x * (1 / 2 - x * (1 / 3 - x * (1 / 4 - x * (1 / 5 - x * (1 / 6))))))
    return jnp.log(jnp.where(x > 1 / 16, jnp.log(1.0 + x), series)) - math.log(math.log(ITEMS + 1.0))


def column(row):
    return jnp.broadcast_to(row, (128, row.shape[1])).T[:, :1]


def dot(a, b):
    return jnp.dot(a, b, preferred_element_type=F32)


def dot_t(a, b):
    return lax.dot_general(a, b, (((1,), (1,)), ((), ())), preferred_element_type=F32)


def t_dot(a, b):
    return lax.dot_general(a, b, (((0,), (0,)), ((), ())), preferred_element_type=F32)


def silu(v):
    half = 0.5 * v
    return half + half * jnp.tanh(half)


def row_norm(x, keep=None):
    center = x - jnp.mean(x, axis=-1, keepdims=True)
    scale = lax.rsqrt(jnp.mean(center * center, axis=-1, keepdims=True) + NORM_EPSILON)
    if keep is not None:
        scale = jnp.where(keep, scale, 0.0)
    return center * scale


def norm_of(x):
    return jnp.sqrt(jnp.sum(x * x, axis=-1, keepdims=True) + UNIT_EPSILON)


def kept_rows(first, rows, length):
    return first + lax.broadcasted_iota(jnp.int32, (rows, 1), 0) < length


def attend(q_ref, keys, values, acc_ref, before_ref, causal=None):
    rows, width = q_ref.shape
    head = width // HEADS
    for h in range(HEADS):
        cols = slice(h * head, (h + 1) * head)
        half = dot_t(q_ref[:, cols], keys[:, cols]) * (0.5 / math.sqrt(head))
        weights = half + half * jnp.tanh(half)
        if causal is not None:
            weights = jnp.where(causal, weights, 0.0)
        part = dot(weights.astype(BF16), values[:, cols])
        acc_ref[:, cols] = part if before_ref is None else before_ref[:, cols] + part


def project(normed, w_ref, block):
    width = normed.shape[1]
    return silu(dot(normed, w_ref[:, block * width : (block + 1) * width])).astype(BF16)


def causal_mask(rows):
    return lax.broadcasted_iota(jnp.int32, (rows, rows), 0) >= lax.broadcasted_iota(jnp.int32, (rows, rows), 1)


def fetch(pairs, sems):
    copies = [pltpu.make_async_copy(src, dst, sems.at[i]) for i, (src, dst) in enumerate(pairs)]
    for copy in copies:
        copy.start()
    return copies


def own_kernel(info_ref, x_hbm, w_hbm, gate_ref, q_ref, k_ref, v_ref, acc_ref, x_ref, w_ref, sems):
    rows, width = x_ref.shape
    parts = [2, 3, 1, 0]
    pairs = [(w_hbm.at[:, i * width : (i + 1) * width], w_ref.at[i]) for i in parts]
    copies = fetch([(x_hbm, x_ref)] + pairs, sems)
    copies[0].wait()
    keep = kept_rows(info_ref[0], rows, info_ref[1])
    normed = row_norm(x_ref[...].astype(F32), keep).astype(BF16)
    for copy, i, to_ref in zip(copies[1:], parts, [q_ref, k_ref, v_ref, gate_ref]):
        copy.wait()
        to_ref[...] = silu(dot(normed, w_ref[i])).astype(BF16)
    attend(q_ref, k_ref, v_ref, acc_ref, None, causal_mask(rows))


def guest_kernel(
    info_ref, x_ref, w_ref, k_ref, v_ref, own_x_ref, own_gate_ref, own_q_ref, own_acc_ref,
    all_x_ref, all_gate_ref, all_q_ref, all_acc_ref, guest_k_ref, guest_v_ref,
):
    rows = x_ref.shape[0]
    own, guest = slice(0, rows), slice(rows, 2 * rows)
    keep = kept_rows(info_ref[0] + rows, rows, info_ref[1])
    normed = row_norm(x_ref[...].astype(F32), keep).astype(BF16)
    all_x_ref[own, :], all_x_ref[guest, :] = own_x_ref[...], x_ref[...]
    all_gate_ref[own, :], all_gate_ref[guest, :] = own_gate_ref[...], project(normed, w_ref, 0)
    all_q_ref[own, :], all_q_ref[guest, :] = own_q_ref[...], project(normed, w_ref, 2)
    all_acc_ref[own, :] = own_acc_ref[...]
    guest_k_ref[...] = project(normed, w_ref, 3)
    guest_v_ref[...] = project(normed, w_ref, 1)
    q_ref, acc_ref = all_q_ref.at[guest, :], all_acc_ref.at[guest, :]
    attend(q_ref, guest_k_ref, guest_v_ref, acc_ref, None, causal_mask(rows))
    attend(q_ref, k_ref, v_ref, acc_ref, acc_ref)


def add_block(info_ref, back, x_ref, w_ref, q_ref, acc_ref, before_ref):
    keep = kept_rows(info_ref[0] - back, x_ref.shape[0], info_ref[1])
    normed = row_norm(x_ref[...].astype(F32), keep).astype(BF16)
    attend(q_ref, project(normed, w_ref, 3), project(normed, w_ref, 1), acc_ref, before_ref)


def step_kernel(back, info_ref, x_ref, w_ref, q_ref, before_ref, acc_ref):
    add_block(info_ref, back, x_ref, w_ref, q_ref, acc_ref, before_ref)


def last_kernel(
    back, info_ref, x_ref, w_ref, q_ref, before_ref, gate_ref, own_ref, w_out_ref, w_proj_ref,
    layer_ref, out_ref, hat_ref, acc_ref,
):
    add_block(info_ref, back, x_ref, w_ref, q_ref, acc_ref, before_ref)
    gated = (row_norm(acc_ref[...]) * gate_ref[...].astype(F32)).astype(BF16)
    layer = (dot(gated, w_out_ref[...]) + own_ref[...].astype(F32)).astype(BF16)
    layer_ref[...] = layer
    out = dot(layer, w_proj_ref[...])
    out_ref[...] = out
    hat_ref[...] = (out / norm_of(out)).astype(BF16)


def split3(x):
    high = x.astype(BF16).astype(F32)
    mid = (x - high).astype(BF16).astype(F32)
    return [high, mid, x - high - mid]


def id_digits(ids):
    return [(ids >> 14).astype(F32), ((ids >> 7) & 127).astype(F32), (ids & 127).astype(F32)]


def of_digits(a, b, c):
    return a * 16384.0 + b * 128.0 + c


def padded_rows(count):
    return -(-count // 16) * 16


def table_kernel(
    x_hbm, ids_hbm, pos_hbm, pos_ids_hbm, table_ref, message_ref, x_ref, ids_ref, pos_ref, pos_ids_ref, sems
):
    pairs = [(x_hbm, x_ref), (ids_hbm, ids_ref), (pos_hbm, pos_ref), (pos_ids_hbm, pos_ids_ref)]
    for copy in fetch(pairs, sems):
        copy.wait()
    count, embed = x_ref.shape
    x = x_ref[...].astype(F32)
    table_ref[:count, :] = (x / norm_of(x)).astype(BF16)
    ids = jnp.concatenate([ids_ref[:, i : i + embed] for i in range(0, count, embed)], axis=0)
    parts = split3(log_sample_chance(ids.astype(F32)) * LOG2E) + id_digits(ids)
    used = len(parts) * ids.shape[0]
    pad = jnp.zeros((table_ref.shape[0] - count - used, embed), F32)
    table_ref[count:, :] = jnp.concatenate(parts + [pad], axis=0).astype(BF16)
    rows = pos_ref.shape[0]
    parts = id_digits(pos_ids_ref[...])
    pad = jnp.zeros((message_ref.shape[0] - rows - len(parts), embed), F32)
    message_ref[:rows, :] = pos_ref[...]
    message_ref[rows:, :] = jnp.concatenate(parts + [pad], axis=0).astype(BF16)


def head_kernel(
    hist_count, info_ref, hat_ref, out_ref, layer_ref, pos_ref, ids_ref, guest_ref, *rest
):
    *table_refs, loss_ref, guest_loss_ref, message_ref, keep_ref, send_ref, proj_ref, kept_ref = rest
    rows, embed = hat_ref.shape
    block = rows // 2
    chunks = table_refs[0].shape[0] // (embed + 6)
    count = chunks * embed
    hat = hat_ref[...]
    guest_parts = guest_ref[block:, :].astype(F32)
    id_rows = [id_digits(ids_ref[...]), [guest_parts[i : i + 1, :] for i in range(3)]]
    id_row = jnp.concatenate([of_digits(*digits) for digits in id_rows], axis=1)
    pos_id = column(id_row)
    pos = jnp.concatenate([pos_ref[...], guest_ref[:block, :]], axis=0).astype(F32)
    pos_unit = pos / norm_of(pos)
    pos_score = (
        jnp.sum(hat.astype(F32) * pos_unit, axis=-1, keepdims=True) / SOFTMAX_WARMTH - column(log_sample_chance(id_row))
    )
    lanes = jnp.zeros((rows, 128), F32)
    grads = jnp.zeros((rows, embed), F32)
    for table_ref in table_refs:
        parts = table_ref[count:, :].astype(F32)
        for chunk in range(chunks):
            bias, ids = (
                [parts[(g + j) * chunks + chunk : (g + j) * chunks + chunk + 1, :] for j in range(3)]
                for g in (0, 3)
            )
            cut = slice(chunk * embed, (chunk + 1) * embed)
            scores = dot_t(hat, table_ref[cut, :]) * SCORE_SCALE - (bias[0] + bias[1] + bias[2])
            kept = jnp.where(of_digits(*ids) != pos_id, jnp.exp2(scores), 0.0)
            for lane in range(0, embed, 128):
                lanes = lanes + kept[:, lane : lane + 128]
            kept_ref[:, cut] = kept.astype(BF16)
        grads = grads + dot(kept_ref[...], table_ref[:count, :])
    pos_part = jnp.exp(pos_score)
    total = pos_part + jnp.sum(lanes, axis=-1, keepdims=True)
    log_total = jnp.log(total)
    at = lax.broadcasted_iota(jnp.int32, (rows, 1), 0)
    valid = info_ref[0] + at < jnp.where(at < block, info_ref[5], info_ref[6])
    loss = jnp.where(valid, log_total - pos_score, 0.0)
    shift = jnp.where(valid, (log_total + math.log(hist_count)) * LOG2E, FAR)
    loss = jnp.broadcast_to(loss, (rows, 128)).T
    loss_ref[...] = loss[:1, :block]
    guest_loss_ref[...] = loss[:1, block:]
    shift = jnp.broadcast_to(shift, (rows, 128)).T
    parts = []
    for i in range(2):
        parts += split3(shift[:1, i * block : (i + 1) * block]) + id_rows[i]
    pad = jnp.zeros((message_ref.shape[0] - len(parts), embed), F32)
    message_ref[...] = jnp.concatenate(parts + [pad], axis=0).astype(BF16)
    share = jnp.where(valid, 1.0 / (total * hist_count), 0.0)
    pos_weight = jnp.where(valid, pos_part / total - 1.0, 0.0) / hist_count
    d_unit = (pos_weight * pos_unit + share * grads) / SOFTMAX_WARMTH
    out = out_ref[...]
    norms = norm_of(out)
    unit = out / norms
    d_out = ((d_unit - unit * jnp.sum(unit * d_unit, axis=-1, keepdims=True)) / norms).astype(BF16)
    proj_ref[...] = t_dot(layer_ref[...], d_out)
    half = keep_ref.shape[0]
    keep_ref[...] = proj_ref[part_at(info_ref[3], half), :]
    send_ref[...] = proj_ref[part_at(1 - info_ref[3], half), :].astype(BF16)


def part_at(index, rows):
    return pl.ds(pl.multiple_of(index * rows, rows), rows)


def halved_kernel(info_ref, keep_ref, got_ref, own_ref, *rest):
    *send_refs, sum_ref = rest
    rows = own_ref.shape[0]
    sum_ref[...] = keep_ref[...] + got_ref[...].astype(F32)
    own_ref[...] = sum_ref[part_at(info_ref[4], rows), :]
    for r, send_ref in enumerate(send_refs, 1):
        send_ref[...] = sum_ref[part_at(lax.bitwise_xor(info_ref[4], r), rows), :].astype(BF16)


def sum_kernel(*refs):
    parts = [ref[...].astype(F32) for ref in refs[:-1]]
    while len(parts) > 1:
        parts = [a + b for a, b in zip(parts[::2], parts[1::2])]
    refs[-1][...] = parts[0].astype(refs[-1].dtype)


def lay_kernel(slot, info_ref, *refs):
    *part_refs, out_ref = refs
    rows = part_refs[0].shape[0]
    for r, part_ref in enumerate(part_refs):
        at = part_at(lax.bitwise_xor(info_ref[slot], r), rows)
        out_ref[at, :] = part_ref[...].astype(out_ref.dtype)


def cut_blocks(values, keep_ref, send_ref, rows):
    for i in range(values.shape[0] // rows):
        to_ref = send_ref if i % 2 else keep_ref
        to_ref[i // 2 * rows : (i // 2 + 1) * rows, :] = values[i * rows : (i + 1) * rows, :].astype(to_ref.dtype)


def halving_kernel(rows, keep_ref, got_ref, next_keep_ref, next_send_ref):
    cut_blocks(keep_ref[...] + got_ref[: keep_ref.shape[0], :].astype(F32), next_keep_ref, next_send_ref, rows)


def loss_kernel(last, info_ref, loss_ref, got_ref, own_loss_ref):
    rows = loss_ref.shape[1]
    parts = got_ref[got_ref.shape[0] - 16 :, :rows].astype(F32)
    above = parts[0:1, :] + parts[1:2, :] + parts[2:3, :]
    own_loss_ref[...] = jnp.where(info_ref[2] == last, above, loss_ref[...])


def negative_kernel(seq_count, info_ref, neg_ref, neg_id_ref, loss_ref, *rest):
    *gathered, keep_ref, send_ref, turned_ref, sum_ref, weight_ref = rest
    pool_count = len(gathered) // 2
    count, embed = neg_ref.shape
    rows = embed
    blocks = gathered[0].shape[0] // rows
    tile = min(256, count)
    neg = neg_ref[...].astype(F32)
    norms = norm_of(neg)
    unit = neg / norms
    neg_hat = unit.astype(BF16)
    id_row = neg_id_ref[...].astype(F32)
    neg_id = column(id_row)
    for i, (hats_ref, message_ref) in enumerate(zip(gathered[:pool_count], gathered[pool_count:])):
        parts = message_ref[...].astype(F32)
        for block, start in itertools.product(range(blocks), range(0, count, tile)):
            own = slice(block * rows, (block + 1) * rows)
            cut = slice(start, start + tile)
            shift = [parts[6 * block + j : 6 * block + j + 1, :] for j in range(6)]
            scores = dot_t(neg_hat[cut, :], hats_ref[own, :]) * SCORE_SCALE - (shift[0] + shift[1] + shift[2])
            weights = jnp.where(neg_id[cut, :] != of_digits(*shift[3:]), jnp.exp2(scores), 0.0)
            weight_ref[cut, own] = weights.astype(BF16)
        for start in range(0, count, tile):
            cut = slice(start, start + tile)
            term = dot(weight_ref[cut, :], hats_ref[...])
            sum_ref[cut, :] = sum_ref[cut, :] + term if i else term
    neg_sum = sum_ref[...] * column(jnp.exp2(-LOG2E * log_sample_chance(id_row)) / SOFTMAX_WARMTH)
    grad = (neg_sum - unit * jnp.sum(unit * neg_sum, axis=-1, keepdims=True)) / norms
    turned_ref[...] = grad.T
    kept = keep_ref.shape[0]
    cols = kept // (seq_count // 2)
    for r in range(seq_count):
        at = part_at(lax.bitwise_xor(info_ref[2], r), cols)
        to_ref = send_ref if r % 2 else keep_ref
        to_ref[r // 2 * cols : (r // 2 + 1) * cols, :] = turned_ref[at, :].astype(to_ref.dtype)
    parts = split3(loss_ref[...])
    pad = jnp.zeros((16 - len(parts), loss_ref.shape[1]), F32)
    send_ref[kept:, :] = jnp.zeros((16, count), BF16)
    send_ref[kept:, : loss_ref.shape[1]] = jnp.concatenate(parts + [pad], axis=0).astype(BF16)


def call(kernel, ins, outs, scratch=(), limit=24, flops=0, moved=0, name=None, place=pltpu.VMEM):
    in_specs = [pl.BlockSpec(memory_space=pltpu.SMEM if x.ndim == 1 else place) for x in ins]
    many = isinstance(outs, (list, tuple))
    out_specs = jax.tree.map(lambda _: pl.BlockSpec(memory_space=pltpu.VMEM), outs)
    return pl.pallas_call(
        kernel,
        out_shape=list(outs) if many else outs,
        in_specs=in_specs,
        out_specs=list(out_specs) if many else out_specs,
        scratch_shapes=list(scratch),
        compiler_params=pltpu.CompilerParams(vmem_limit_bytes=limit * MIB),
        cost_estimate=pl.CostEstimate(flops=flops, bytes_accessed=moved, transcendentals=0),
        name=name,
    )(*ins)


def swap(x, axis, count, r):
    return lax.ppermute(x, axis, [(i, i ^ r) for i in range(count)])


def gather_step(blocks, axis, count):
    bit = count // (2 * len(blocks))
    return blocks + [swap(block, axis, count, bit) for block in blocks] if bit else blocks


def together(*trees):
    return lax.optimization_barrier(trees)


def struct(shape, kind):
    return jax.ShapeDtypeStruct(shape, kind)


def body(tokens, w_in, w_out, w_proj, pos_embed, pos_ids, lengths, neg_embed, neg_ids):
    rows, width = tokens.shape[1:]
    embed = w_proj.shape[1]
    seq_count = lax.axis_size("seq")
    pool_count = lax.axis_size("pool")
    plane = ("batch", "pool")
    plane_count = lax.axis_size("batch") * pool_count
    seq_at = lax.axis_index("seq")
    plane_at = lax.axis_index("batch") * pool_count + lax.axis_index("pool")
    own_end = jnp.where(seq_at == seq_count - 1, 0, lengths[0])
    guest_end = jnp.where(seq_at == seq_count - 2, lengths[0], 0)
    info = jnp.stack([seq_at * rows, lengths[0], seq_at, plane_at % 2, plane_at // 2, own_end, guest_end])
    info = info.astype(jnp.int32)
    own = tokens[0]
    local_neg = neg_embed.shape[1]

    up = [(i, i + 1) for i in range(seq_count - 2)]
    down = [(seq_count - 1, seq_count - 2)]
    block = lax.ppermute(own, "seq", up)
    guest = lax.ppermute(own, "seq", down)
    kind = struct((rows, width), BF16)
    wide = struct((rows, width), F32)
    gate, queries, keys, values, acc = call(
        own_kernel,
        [info, own, w_in],
        [kind, kind, kind, kind, wide],
        scratch=[pltpu.VMEM((rows, width), BF16), pltpu.VMEM((4, width, width), BF16), pltpu.SemaphoreType.DMA((5,))],
        place=pl.ANY,
        limit=44,
        name="own_block",
    )
    table_part, pos_part = call(
        table_kernel,
        [neg_embed[0], neg_ids, pos_embed[0], pos_ids],
        [
            struct((local_neg + padded_rows(6 * local_neg // embed), embed), BF16),
            struct((rows + 16, embed), BF16),
        ],
        scratch=[
            pltpu.VMEM((local_neg, embed), BF16), pltpu.VMEM((1, local_neg), jnp.int32),
            pltpu.VMEM((rows, embed), BF16), pltpu.VMEM((1, rows), jnp.int32), pltpu.SemaphoreType.DMA((4,)),
        ],
        place=pl.ANY,
        limit=24,
        name="table_part",
    )
    table_part, pos_part, acc = together(table_part, pos_part, acc)
    table = gather_step([table_part], "pool", pool_count)
    block, guest, acc = together(block, guest, acc)
    tall = struct((2 * rows, width), BF16)
    tall_wide = struct((2 * rows, width), F32)
    for step in range(1, seq_count - 2):
        following = lax.ppermute(block, "seq", up)
        if step == 1:
            own, gate, queries, acc = call(
                guest_kernel,
                [info, guest, w_in, keys, values, own, gate, queries, acc],
                [tall, tall, tall, tall_wide],
                scratch=[pltpu.VMEM((rows, width), BF16)] * 2,
                name="guest_block",
            )
        acc = call(
            functools.partial(step_kernel, step * rows),
            [info, block, w_in, queries, acc],
            tall_wide,
            name=f"earlier_block_{step}",
        )
        acc, table, pos_part = together(acc, table, pos_part)
        if step == 1:
            guest_pos = lax.ppermute(pos_part, "seq", down)
        table = gather_step(table, "pool", pool_count)
        block, acc = together(following, acc)
    while len(table) < pool_count:
        table = gather_step(table, "pool", pool_count)
    layer, out, hat = call(
        functools.partial(last_kernel, (seq_count - 2) * rows),
        [info, block, w_in, queries, acc, gate, own, w_out, w_proj],
        [tall, struct((2 * rows, embed), F32), struct((2 * rows, embed), BF16)],
        scratch=[pltpu.VMEM((2 * rows, width), F32)],
        name="last_block",
    )
    hats = gather_step([hat], "pool", pool_count)

    half, chips = width // 2, plane_count // 2
    loss, guest_loss, message, keep, send = call(
        functools.partial(head_kernel, plane_count),
        [info, hat, out, layer, pos_embed[0], pos_ids, guest_pos, *table],
        [
            struct((1, rows), F32), struct((1, rows), F32), struct((16, embed), BF16),
            struct((half, embed), F32), struct((half, embed), BF16),
        ],
        scratch=[pltpu.VMEM((width, embed), F32), pltpu.VMEM((2 * rows, local_neg), BF16)],
        name="head",
    )
    part = struct((half // chips, embed), BF16)
    cols = embed // seq_count
    def plane_swap(parts):
        return [swap(x, plane, plane_count, 2 * r) for r, x in enumerate(parts, 1)]

    got, messages = together(swap(send, plane, plane_count, 1), gather_step([message], "pool", pool_count))
    own_part, *sends = call(
        halved_kernel,
        [info, keep, got],
        [struct(part.shape, F32)] + [part] * (chips - 1),
        scratch=[pltpu.VMEM((half, embed), F32)],
        name="halved",
    )
    hats, _ = together(hats, own_part)
    while len(hats) < pool_count:
        hats = gather_step(hats, "pool", pool_count)
    while len(messages) < pool_count:
        messages = gather_step(messages, "pool", pool_count)
    proj_parts, messages = together([own_part] + plane_swap(sends), messages)
    proj_part = call(sum_kernel, proj_parts, part, name="plane_sum")
    bit = 1
    while 2 * bit < seq_count:
        got = swap(proj_part, "seq", seq_count, bit)
        proj_part = call(sum_kernel, [proj_part, got], part, name=f"seq_sum_{bit}")
        bit *= 2
    hats, messages, _ = together(hats, messages, proj_part)
    keep, send = call(
        functools.partial(negative_kernel, seq_count),
        [info, neg_embed[0], neg_ids, guest_loss, *hats, *messages],
        [struct((embed // 2, local_neg), F32), struct((embed // 2 + 16, local_neg), BF16)],
        scratch=[
            pltpu.VMEM((embed, local_neg), F32), pltpu.VMEM((local_neg, embed), F32),
            pltpu.VMEM((local_neg, 2 * rows), BF16),
        ],
        name="neg_grad",
    )
    got, keep, send = together(swap(proj_part, "seq", seq_count, bit), keep, send)
    proj_part = call(sum_kernel, [proj_part, got], part, name=f"seq_sum_{bit}")
    got = swap(send, "seq", seq_count, 1)
    got, _ = together(got, proj_part)
    loss = call(functools.partial(loss_kernel, seq_count - 1), [info, loss, got], struct((1, rows), F32), name="loss")
    bit = 2
    while bit < seq_count:
        size = keep.shape[0] // 2
        keep, send = call(
            functools.partial(halving_kernel, cols),
            [keep, got],
            [struct((size, local_neg), F32), struct((size, local_neg), BF16)],
            name=f"neg_halved_{bit}",
        )
        got = swap(send, "seq", seq_count, bit)
        bit *= 2
    proj_parts, send = together([proj_part] + plane_swap([proj_part] * (chips - 1)), send)
    proj_half = call(
        functools.partial(lay_kernel, 4), [info, *proj_parts], struct((half, embed), BF16), name="lay_half"
    )
    other_half = swap(proj_half, plane, plane_count, 1)
    d_neg = call(sum_kernel, [keep, got], struct((cols, local_neg), F32), name="neg_sum")
    d_proj = call(
        functools.partial(lay_kernel, 3), [info, proj_half, other_half], struct((width, embed), F32), name="lay_whole"
    )
    return (loss, d_neg.T[None], d_proj)


def solution(mesh):
    placed = (
        P(("batch", "pool"), "seq", None),
        P(),
        P(),
        P(),
        P(("batch", "pool"), "seq", None),
        P(("batch", "pool"), "seq"),
        P(("batch", "pool")),
        P("batch", "pool", None),
        P("batch", "pool"),
    )
    return jax.shard_map(
        body,
        mesh=mesh,
        in_specs=placed,
        out_specs=(P(("batch", "pool"), "seq"), P("batch", "pool", "seq"), P()),
        check_vma=False,
    )
```

```python
import functools
import itertools
import math

import jax
import jax.numpy as jnp
from jax import lax
from jax.experimental import pallas as pl
from jax.experimental.pallas import tpu as pltpu
from jax.sharding import PartitionSpec as P

HEADS = 8
ITEMS = 1048576

SOFTMAX_WARMTH = 0.02
NORM_EPSILON = 1e-05
UNIT_EPSILON = 1e-06
LOG2E = math.log2(math.e)
SCORE_SCALE = LOG2E / SOFTMAX_WARMTH
FAR = 10000.0

F32 = jnp.float32
BF16 = jnp.bfloat16
MIB = 1 << 20


def log_sample_chance(item_ids):
    x = 1.0 / (item_ids + 1.0)
    series = x * (1.0 - x * (1 / 2 - x * (1 / 3 - x * (1 / 4 - x * (1 / 5 - x * (1 / 6))))))
    return jnp.log(jnp.where(x > 1 / 16, jnp.log(1.0 + x), series)) - math.log(math.log(ITEMS + 1.0))


def column(row):
    return jnp.broadcast_to(row, (128, row.shape[1])).T[:, :1]


def dot(a, b):
    return jnp.dot(a, b, preferred_element_type=F32)


def dot_t(a, b):
    return lax.dot_general(a, b, (((1,), (1,)), ((), ())), preferred_element_type=F32)


def t_dot(a, b):
    return lax.dot_general(a, b, (((0,), (0,)), ((), ())), preferred_element_type=F32)


def silu(v):
    half = 0.5 * v
    return half + half * jnp.tanh(half)


def row_norm(x, keep=None):
    center = x - jnp.mean(x, axis=-1, keepdims=True)
    scale = lax.rsqrt(jnp.mean(center * center, axis=-1, keepdims=True) + NORM_EPSILON)
    if keep is not None:
        scale = jnp.where(keep, scale, 0.0)
    return center * scale


def norm_of(x):
    return jnp.sqrt(jnp.sum(x * x, axis=-1, keepdims=True) + UNIT_EPSILON)


def kept_rows(first, rows, length):
    return first + lax.broadcasted_iota(jnp.int32, (rows, 1), 0) < length


def attend(q_ref, keys, values, acc_ref, before_ref, causal=None):
    rows, width = q_ref.shape
    head = width // HEADS
    for h in range(HEADS):
        cols = slice(h * head, (h + 1) * head)
        half = dot_t(q_ref[:, cols], keys[:, cols]) * (0.5 / math.sqrt(head))
        weights = half + half * jnp.tanh(half)
        if causal is not None:
            weights = jnp.where(causal, weights, 0.0)
        part = dot(weights.astype(BF16), values[:, cols])
        acc_ref[:, cols] = part if before_ref is None else before_ref[:, cols] + part


def project(normed, w_ref, block):
    width = normed.shape[1]
    return silu(dot(normed, w_ref[:, block * width : (block + 1) * width])).astype(BF16)


def causal_mask(rows):
    return lax.broadcasted_iota(jnp.int32, (rows, rows), 0) >= lax.broadcasted_iota(jnp.int32, (rows, rows), 1)


def fetch(pairs, sems):
    copies = [pltpu.make_async_copy(src, dst, sems.at[i]) for i, (src, dst) in enumerate(pairs)]
    for copy in copies:
        copy.start()
    return copies


def own_kernel(info_ref, x_hbm, w_hbm, gate_ref, q_ref, k_ref, v_ref, acc_ref, x_ref, w_ref, sems):
    rows, width = x_ref.shape
    parts = [2, 3, 1, 0]
    pairs = [(w_hbm.at[:, i * width : (i + 1) * width], w_ref.at[i]) for i in parts]
    copies = fetch([(x_hbm, x_ref)] + pairs, sems)
    copies[0].wait()
    keep = kept_rows(info_ref[0], rows, info_ref[1])
    normed = row_norm(x_ref[...].astype(F32), keep).astype(BF16)
    for copy, i, to_ref in zip(copies[1:], parts, [q_ref, k_ref, v_ref, gate_ref]):
        copy.wait()
        to_ref[...] = silu(dot(normed, w_ref[i])).astype(BF16)
    attend(q_ref, k_ref, v_ref, acc_ref, None, causal_mask(rows))


def guest_kernel(
    info_ref, x_ref, w_ref, k_ref, v_ref, own_x_ref, own_gate_ref, own_q_ref, own_acc_ref,
    all_x_ref, all_gate_ref, all_q_ref, all_acc_ref, guest_k_ref, guest_v_ref,
):
    rows = x_ref.shape[0]
    own, guest = slice(0, rows), slice(rows, 2 * rows)
    keep = kept_rows(info_ref[0] + rows, rows, info_ref[1])
    normed = row_norm(x_ref[...].astype(F32), keep).astype(BF16)
    all_x_ref[own, :], all_x_ref[guest, :] = own_x_ref[...], x_ref[...]
    all_gate_ref[own, :], all_gate_ref[guest, :] = own_gate_ref[...], project(normed, w_ref, 0)
    all_q_ref[own, :], all_q_ref[guest, :] = own_q_ref[...], project(normed, w_ref, 2)
    all_acc_ref[own, :] = own_acc_ref[...]
    guest_k_ref[...] = project(normed, w_ref, 3)
    guest_v_ref[...] = project(normed, w_ref, 1)
    q_ref, acc_ref = all_q_ref.at[guest, :], all_acc_ref.at[guest, :]
    attend(q_ref, guest_k_ref, guest_v_ref, acc_ref, None, causal_mask(rows))
    attend(q_ref, k_ref, v_ref, acc_ref, acc_ref)


def add_block(info_ref, back, x_ref, w_ref, q_ref, acc_ref, before_ref):
    keep = kept_rows(info_ref[0] - back, x_ref.shape[0], info_ref[1])
    normed = row_norm(x_ref[...].astype(F32), keep).astype(BF16)
    attend(q_ref, project(normed, w_ref, 3), project(normed, w_ref, 1), acc_ref, before_ref)


def step_kernel(back, info_ref, x_ref, w_ref, q_ref, before_ref, acc_ref):
    add_block(info_ref, back, x_ref, w_ref, q_ref, acc_ref, before_ref)


def last_kernel(
    back, info_ref, x_ref, w_ref, q_ref, before_ref, gate_ref, own_ref, w_out_ref, w_proj_ref,
    layer_ref, out_ref, hat_ref, acc_ref,
):
    add_block(info_ref, back, x_ref, w_ref, q_ref, acc_ref, before_ref)
    gated = (row_norm(acc_ref[...]) * gate_ref[...].astype(F32)).astype(BF16)
    layer = (dot(gated, w_out_ref[...]) + own_ref[...].astype(F32)).astype(BF16)
    layer_ref[...] = layer
    out = dot(layer, w_proj_ref[...])
    out_ref[...] = out
    hat_ref[...] = (out / norm_of(out)).astype(BF16)


def split3(x):
    high = x.astype(BF16).astype(F32)
    mid = (x - high).astype(BF16).astype(F32)
    return [high, mid, x - high - mid]


def id_digits(ids):
    return [(ids >> 14).astype(F32), ((ids >> 7) & 127).astype(F32), (ids & 127).astype(F32)]


def of_digits(a, b, c):
    return a * 16384.0 + b * 128.0 + c


def padded_rows(count):
    return -(-count // 16) * 16


def table_kernel(
    x_hbm, ids_hbm, pos_hbm, pos_ids_hbm, table_ref, message_ref, x_ref, ids_ref, pos_ref, pos_ids_ref, sems
):
    pairs = [(x_hbm, x_ref), (ids_hbm, ids_ref), (pos_hbm, pos_ref), (pos_ids_hbm, pos_ids_ref)]
    for copy in fetch(pairs, sems):
        copy.wait()
    count, embed = x_ref.shape
    x = x_ref[...].astype(F32)
    table_ref[:count, :] = (x / norm_of(x)).astype(BF16)
    ids = jnp.concatenate([ids_ref[:, i : i + embed] for i in range(0, count, embed)], axis=0)
    parts = split3(log_sample_chance(ids.astype(F32)) * LOG2E) + id_digits(ids)
    used = len(parts) * ids.shape[0]
    pad = jnp.zeros((table_ref.shape[0] - count - used, embed), F32)
    table_ref[count:, :] = jnp.concatenate(parts + [pad], axis=0).astype(BF16)
    rows = pos_ref.shape[0]
    parts = id_digits(pos_ids_ref[...])
    pad = jnp.zeros((message_ref.shape[0] - rows - len(parts), embed), F32)
    message_ref[:rows, :] = pos_ref[...]
    message_ref[rows:, :] = jnp.concatenate(parts + [pad], axis=0).astype(BF16)


def head_kernel(
    hist_count, info_ref, hat_ref, out_ref, layer_ref, pos_ref, ids_ref, guest_ref, *rest
):
    *table_refs, loss_ref, guest_loss_ref, message_ref, keep_ref, send_ref, proj_ref, kept_ref = rest
    rows, embed = hat_ref.shape
    block = rows // 2
    chunks = table_refs[0].shape[0] // (embed + 6)
    count = chunks * embed
    hat = hat_ref[...]
    guest_parts = guest_ref[block:, :].astype(F32)
    id_rows = [id_digits(ids_ref[...]), [guest_parts[i : i + 1, :] for i in range(3)]]
    id_row = jnp.concatenate([of_digits(*digits) for digits in id_rows], axis=1)
    pos_id = column(id_row)
    pos = jnp.concatenate([pos_ref[...], guest_ref[:block, :]], axis=0).astype(F32)
    pos_unit = pos / norm_of(pos)
    pos_score = (
        jnp.sum(hat.astype(F32) * pos_unit, axis=-1, keepdims=True) / SOFTMAX_WARMTH - column(log_sample_chance(id_row))
    )
    lanes = jnp.zeros((rows, 128), F32)
    grads = jnp.zeros((rows, embed), F32)
    for table_ref in table_refs:
        parts = table_ref[count:, :].astype(F32)
        for chunk in range(chunks):
            bias, ids = (
                [parts[(g + j) * chunks + chunk : (g + j) * chunks + chunk + 1, :] for j in range(3)]
                for g in (0, 3)
            )
            cut = slice(chunk * embed, (chunk + 1) * embed)
            scores = dot_t(hat, table_ref[cut, :]) * SCORE_SCALE - (bias[0] + bias[1] + bias[2])
            kept = jnp.where(of_digits(*ids) != pos_id, jnp.exp2(scores), 0.0)
            for lane in range(0, embed, 128):
                lanes = lanes + kept[:, lane : lane + 128]
            kept_ref[:, cut] = kept.astype(BF16)
        grads = grads + dot(kept_ref[...], table_ref[:count, :])
    pos_part = jnp.exp(pos_score)
    total = pos_part + jnp.sum(lanes, axis=-1, keepdims=True)
    log_total = jnp.log(total)
    at = lax.broadcasted_iota(jnp.int32, (rows, 1), 0)
    valid = info_ref[0] + at < jnp.where(at < block, info_ref[5], info_ref[6])
    loss = jnp.where(valid, log_total - pos_score, 0.0)
    shift = jnp.where(valid, (log_total + math.log(hist_count)) * LOG2E, FAR)
    loss = jnp.broadcast_to(loss, (rows, 128)).T
    loss_ref[...] = loss[:1, :block]
    guest_loss_ref[...] = loss[:1, block:]
    shift = jnp.broadcast_to(shift, (rows, 128)).T
    parts = []
    for i in range(2):
        parts += split3(shift[:1, i * block : (i + 1) * block]) + id_rows[i]
    pad = jnp.zeros((message_ref.shape[0] - len(parts), embed), F32)
    message_ref[...] = jnp.concatenate(parts + [pad], axis=0).astype(BF16)
    share = jnp.where(valid, 1.0 / (total * hist_count), 0.0)
    pos_weight = jnp.where(valid, pos_part / total - 1.0, 0.0) / hist_count
    d_unit = (pos_weight * pos_unit + share * grads) / SOFTMAX_WARMTH
    out = out_ref[...]
    norms = norm_of(out)
    unit = out / norms
    d_out = ((d_unit - unit * jnp.sum(unit * d_unit, axis=-1, keepdims=True)) / norms).astype(BF16)
    proj_ref[...] = t_dot(layer_ref[...], d_out)
    half = keep_ref.shape[0]
    keep_ref[...] = proj_ref[part_at(info_ref[3], half), :]
    send_ref[...] = proj_ref[part_at(1 - info_ref[3], half), :].astype(BF16)


def part_at(index, rows):
    return pl.ds(pl.multiple_of(index * rows, rows), rows)


def halved_kernel(chip, info_ref, keep_ref, got_ref, message_ref, own_ref, *rest):
    *send_refs, sum_ref = rest
    rows = own_ref.shape[0]
    sum_ref[...] = keep_ref[...] + got_ref[...].astype(F32)
    own_ref[...] = sum_ref[part_at(info_ref[4], rows), :]
    for r, send_ref in enumerate(send_refs, 1):
        send_ref[:rows, :] = sum_ref[part_at(lax.bitwise_xor(info_ref[4], r), rows), :].astype(BF16)
        if r == chip:
            send_ref[rows:, :] = message_ref[...]


def sum_kernel(*refs):
    rows = refs[0].shape[0]
    parts = [ref[:rows, :].astype(F32) for ref in refs[:-1]]
    while len(parts) > 1:
        parts = [a + b for a, b in zip(parts[::2], parts[1::2])]
    refs[-1][...] = parts[0].astype(refs[-1].dtype)


def lay_kernel(info_ref, *refs):
    *part_refs, out_ref = refs
    rows = part_refs[0].shape[0]
    chips = len(part_refs) // 2
    for i, part_ref in enumerate(part_refs):
        core, r = divmod(i, chips)
        at = lax.bitwise_xor(info_ref[3], core) * chips + lax.bitwise_xor(info_ref[4], r)
        out_ref[part_at(at, rows), :] = part_ref[...].astype(out_ref.dtype)


def loss_kernel(last, info_ref, loss_ref, got_ref, own_loss_ref):
    rows = loss_ref.shape[1]
    parts = got_ref[got_ref.shape[0] - 16 :, :rows].astype(F32)
    above = parts[0:1, :] + parts[1:2, :] + parts[2:3, :]
    own_loss_ref[...] = jnp.where(info_ref[2] == last, above, loss_ref[...])


def negative_kernel(pool_count, info_ref, neg_ref, neg_id_ref, loss_ref, *rest):
    gathered, rest = rest[: 2 * pool_count], rest[2 * pool_count :]
    own_ref, *send_refs, turned_ref, sum_ref, weight_ref = rest
    count, embed = neg_ref.shape
    rows = embed
    blocks = gathered[0].shape[0] // rows
    tile = min(256, count)
    neg = neg_ref[...].astype(F32)
    norms = norm_of(neg)
    unit = neg / norms
    neg_hat = unit.astype(BF16)
    id_row = neg_id_ref[...].astype(F32)
    neg_id = column(id_row)
    for i, (hats_ref, message_ref) in enumerate(zip(gathered[:pool_count], gathered[pool_count:])):
        parts = message_ref[message_ref.shape[0] - 16 :, :].astype(F32)
        for block, start in itertools.product(range(blocks), range(0, count, tile)):
            own = slice(block * rows, (block + 1) * rows)
            cut = slice(start, start + tile)
            shift = [parts[6 * block + j : 6 * block + j + 1, :] for j in range(6)]
            scores = dot_t(neg_hat[cut, :], hats_ref[own, :]) * SCORE_SCALE - (shift[0] + shift[1] + shift[2])
            weights = jnp.where(neg_id[cut, :] != of_digits(*shift[3:]), jnp.exp2(scores), 0.0)
            weight_ref[cut, own] = weights.astype(BF16)
        for start in range(0, count, tile):
            cut = slice(start, start + tile)
            term = dot(weight_ref[cut, :], hats_ref[...])
            sum_ref[cut, :] = sum_ref[cut, :] + term if i else term
    neg_sum = sum_ref[...] * column(jnp.exp2(-LOG2E * log_sample_chance(id_row)) / SOFTMAX_WARMTH)
    grad = (neg_sum - unit * jnp.sum(unit * neg_sum, axis=-1, keepdims=True)) / norms
    turned_ref[...] = grad.T
    cols = own_ref.shape[0]
    own_ref[...] = turned_ref[part_at(info_ref[2], cols), :]
    for r, send_ref in enumerate(send_refs, 1):
        send_ref[:cols, :] = turned_ref[part_at(lax.bitwise_xor(info_ref[2], r), cols), :].astype(BF16)
    parts = split3(loss_ref[...])
    pad = jnp.zeros((16 - len(parts), loss_ref.shape[1]), F32)
    send_refs[0][cols:, :] = jnp.zeros((16, count), BF16)
    send_refs[0][cols:, : loss_ref.shape[1]] = jnp.concatenate(parts + [pad], axis=0).astype(BF16)


def call(kernel, ins, outs, scratch=(), limit=24, micros=0.5, name=None, place=pltpu.VMEM):
    in_specs = [pl.BlockSpec(memory_space=pltpu.SMEM if x.ndim == 1 else place) for x in ins]
    many = isinstance(outs, (list, tuple))
    out_specs = jax.tree.map(lambda _: pl.BlockSpec(memory_space=pltpu.VMEM), outs)
    return pl.pallas_call(
        kernel,
        out_shape=list(outs) if many else outs,
        in_specs=in_specs,
        out_specs=list(out_specs) if many else out_specs,
        scratch_shapes=list(scratch),
        compiler_params=pltpu.CompilerParams(vmem_limit_bytes=limit * MIB),
        cost_estimate=pl.CostEstimate(flops=int(micros * 5.75e8), bytes_accessed=0, transcendentals=0),
        name=name,
    )(*ins)


def swap(x, axis, count, r):
    return lax.ppermute(x, axis, [(i, i ^ r) for i in range(count)])


def gather_step(blocks, axis, count):
    bit = count // (2 * len(blocks))
    return blocks + [swap(block, axis, count, bit) for block in blocks] if bit else blocks


def together(*trees):
    return lax.optimization_barrier(trees)


def struct(shape, kind):
    return jax.ShapeDtypeStruct(shape, kind)


def body(tokens, w_in, w_out, w_proj, pos_embed, pos_ids, lengths, neg_embed, neg_ids):
    rows, width = tokens.shape[1:]
    embed = w_proj.shape[1]
    seq_count = lax.axis_size("seq")
    pool_count = lax.axis_size("pool")
    plane = ("batch", "pool")
    plane_count = lax.axis_size("batch") * pool_count
    seq_at = lax.axis_index("seq")
    plane_at = lax.axis_index("batch") * pool_count + lax.axis_index("pool")
    own_end = jnp.where(seq_at == seq_count - 1, 0, lengths[0])
    guest_end = jnp.where(seq_at == seq_count - 2, lengths[0], 0)
    info = jnp.stack([seq_at * rows, lengths[0], seq_at, plane_at % 2, plane_at // 2, own_end, guest_end])
    info = info.astype(jnp.int32)
    own = tokens[0]
    local_neg = neg_embed.shape[1]

    up = [(i, i + 1) for i in range(seq_count - 2)]
    down = [(seq_count - 1, seq_count - 2)]
    block = lax.ppermute(own, "seq", up)
    guest = lax.ppermute(own, "seq", down)
    kind = struct((rows, width), BF16)
    wide = struct((rows, width), F32)
    gate, queries, keys, values, acc = call(
        own_kernel,
        [info, own, w_in],
        [kind, kind, kind, kind, wide],
        scratch=[pltpu.VMEM((rows, width), BF16), pltpu.VMEM((4, width, width), BF16), pltpu.SemaphoreType.DMA((5,))],
        place=pl.ANY,
        limit=44,
        micros=6, name="own_block",
    )
    table_part, pos_part = call(
        table_kernel,
        [neg_embed[0], neg_ids, pos_embed[0], pos_ids],
        [
            struct((local_neg + padded_rows(6 * local_neg // embed), embed), BF16),
            struct((rows + 16, embed), BF16),
        ],
        scratch=[
            pltpu.VMEM((local_neg, embed), BF16), pltpu.VMEM((1, local_neg), jnp.int32),
            pltpu.VMEM((rows, embed), BF16), pltpu.VMEM((1, rows), jnp.int32), pltpu.SemaphoreType.DMA((4,)),
        ],
        place=pl.ANY,
        limit=24,
        micros=0.6, name="table_part",
    )
    table_part, pos_part, acc = together(table_part, pos_part, acc)
    table = gather_step([table_part], "pool", pool_count)
    block, guest, acc = together(block, guest, acc)
    tall = struct((2 * rows, width), BF16)
    tall_wide = struct((2 * rows, width), F32)
    for step in range(1, seq_count - 2):
        following = lax.ppermute(block, "seq", up)
        if step == 1:
            own, gate, queries, acc = call(
                guest_kernel,
                [info, guest, w_in, keys, values, own, gate, queries, acc],
                [tall, tall, tall, tall_wide],
                scratch=[pltpu.VMEM((rows, width), BF16)] * 2,
                micros=4.8, name="guest_block",
            )
        acc = call(
            functools.partial(step_kernel, step * rows),
            [info, block, w_in, queries, acc],
            tall_wide,
            micros=3.6, name=f"earlier_block_{step}",
        )
        acc, table, pos_part = together(acc, table, pos_part)
        if step == 1:
            guest_pos = lax.ppermute(pos_part, "seq", down)
        table = gather_step(table, "pool", pool_count)
        block, acc = together(following, acc)
    while len(table) < pool_count:
        table = gather_step(table, "pool", pool_count)
    layer, out, hat = call(
        functools.partial(last_kernel, (seq_count - 2) * rows),
        [info, block, w_in, queries, acc, gate, own, w_out, w_proj],
        [tall, struct((2 * rows, embed), F32), struct((2 * rows, embed), BF16)],
        scratch=[pltpu.VMEM((2 * rows, width), F32)],
        micros=6, name="last_block",
    )
    hats = gather_step([hat], "pool", pool_count)

    half, chips = width // 2, plane_count // 2
    loss, guest_loss, message, keep, send = call(
        functools.partial(head_kernel, plane_count),
        [info, hat, out, layer, pos_embed[0], pos_ids, guest_pos, *table],
        [
            struct((1, rows), F32), struct((1, rows), F32), struct((16, embed), BF16),
            struct((half, embed), F32), struct((half, embed), BF16),
        ],
        scratch=[pltpu.VMEM((width, embed), F32), pltpu.VMEM((2 * rows, local_neg), BF16)],
        micros=5, name="head",
    )
    part = struct((half // chips, embed), BF16)
    cols = embed // seq_count
    def plane_swap(parts):
        return [swap(x, plane, plane_count, 2 * r) for r, x in enumerate(parts, 1)]

    chip = pool_count // 4
    sizes = [part.shape[0] + 16 * (r == chip) for r in range(1, chips)]
    own_part, *sends = call(
        functools.partial(halved_kernel, chip),
        [info, keep, swap(send, plane, plane_count, 1), message],
        [struct(part.shape, F32)] + [struct((size, embed), BF16) for size in sizes],
        scratch=[pltpu.VMEM((half, embed), F32)],
        micros=0.6, name="halved",
    )
    proj_parts = plane_swap(sends)
    proj_part = call(sum_kernel, [own_part] + proj_parts, part, name="plane_sum")
    while len(hats) < pool_count:
        hats = gather_step(hats, "pool", pool_count)
    messages = [message, proj_parts[chip - 1]]
    while len(messages) < pool_count:
        messages = gather_step(messages, "pool", pool_count)
    hats, messages, _ = together(hats, messages, proj_part)
    d_part, *sends = call(
        functools.partial(negative_kernel, pool_count),
        [info, neg_embed[0], neg_ids, guest_loss, *hats, *messages],
        [struct((cols, local_neg), F32)]
        + [struct((cols + 16 * (r == 1), local_neg), BF16) for r in range(1, seq_count)],
        scratch=[
            pltpu.VMEM((embed, local_neg), F32), pltpu.VMEM((local_neg, embed), F32),
            pltpu.VMEM((local_neg, 2 * rows), BF16),
        ],
        micros=3.7, name="neg_grad",
    )
    got = swap(proj_part, "seq", seq_count, 1)
    got, sends = together(got, sends)
    proj_part = call(sum_kernel, [proj_part, got], part, name="seq_sum_1")
    bit = 2
    while bit < seq_count:
        proj_part = call(
            sum_kernel, [proj_part, swap(proj_part, "seq", seq_count, bit)], part, name=f"seq_sum_{bit}"
        )
        bit *= 2
    gots = [swap(x, "seq", seq_count, r) for r, x in enumerate(sends, 1)]
    others, gots = together(plane_swap([proj_part] * (chips - 1)), gots)
    proj_parts = [proj_part] + others
    proj_parts += [swap(x, plane, plane_count, 1) for x in proj_parts]
    d_proj = call(lay_kernel, [info, *proj_parts], struct((width, embed), F32), micros=0, name="lay_whole")
    loss = call(
        functools.partial(loss_kernel, seq_count - 1), [info, loss, gots[0]], struct((1, rows), F32),
        micros=1, name="loss",
    )
    d_neg = call(sum_kernel, [d_part, *gots], struct((cols, local_neg), F32), micros=0.7, name="neg_sum")
    return (loss, d_neg.T[None], d_proj)


def solution(mesh):
    placed = (
        P(("batch", "pool"), "seq", None),
        P(),
        P(),
        P(),
        P(("batch", "pool"), "seq", None),
        P(("batch", "pool"), "seq"),
        P(("batch", "pool")),
        P("batch", "pool", None),
        P("batch", "pool"),
    )
    return jax.shard_map(
        body,
        mesh=mesh,
        in_specs=placed,
        out_specs=(P(("batch", "pool"), "seq"), P("batch", "pool", "seq"), P()),
        check_vma=False,
    )
```

```python
import functools
import itertools
import math

import jax
import jax.numpy as jnp
from jax import lax
from jax.experimental import pallas as pl
from jax.experimental.pallas import tpu as pltpu
from jax.sharding import PartitionSpec as P

HEADS = 8
ITEMS = 1048576

SOFTMAX_WARMTH = 0.02
NORM_EPSILON = 1e-05
UNIT_EPSILON = 1e-06
LOG2E = math.log2(math.e)
SCORE_SCALE = LOG2E / SOFTMAX_WARMTH
FAR = 10000.0

F32 = jnp.float32
BF16 = jnp.bfloat16
MIB = 1 << 20


def log_sample_chance(item_ids):
    x = 1.0 / (item_ids + 1.0)
    series = x * (1.0 - x * (1 / 2 - x * (1 / 3 - x * (1 / 4 - x * (1 / 5 - x * (1 / 6))))))
    return jnp.log(jnp.where(x > 1 / 16, jnp.log(1.0 + x), series)) - math.log(math.log(ITEMS + 1.0))


def column(row):
    return jnp.broadcast_to(row, (128, row.shape[1])).T[:, :1]


def dot(a, b):
    return jnp.dot(a, b, preferred_element_type=F32)


def dot_t(a, b):
    return lax.dot_general(a, b, (((1,), (1,)), ((), ())), preferred_element_type=F32)


def t_dot(a, b):
    return lax.dot_general(a, b, (((0,), (0,)), ((), ())), preferred_element_type=F32)


def silu(v):
    half = 0.5 * v
    return half + half * jnp.tanh(half)


def row_norm(x, keep=None):
    center = x - jnp.mean(x, axis=-1, keepdims=True)
    scale = lax.rsqrt(jnp.mean(center * center, axis=-1, keepdims=True) + NORM_EPSILON)
    if keep is not None:
        scale = jnp.where(keep, scale, 0.0)
    return center * scale


def norm_of(x):
    return jnp.sqrt(jnp.sum(x * x, axis=-1, keepdims=True) + UNIT_EPSILON)


def kept_rows(first, rows, length):
    return first + lax.broadcasted_iota(jnp.int32, (rows, 1), 0) < length


def attend(q_ref, keys, values, acc_ref, before_ref, causal=None):
    rows, width = q_ref.shape
    head = width // HEADS
    spans = [slice(h * head, (h + 1) * head) for h in range(HEADS)]
    following = dot_t(q_ref[:, spans[0]], keys[:, spans[0]])
    for h, cols in enumerate(spans):
        half = following * (0.5 / math.sqrt(head))
        if h + 1 < HEADS:
            following = dot_t(q_ref[:, spans[h + 1]], keys[:, spans[h + 1]])
        weights = half + half * jnp.tanh(half)
        if causal is not None:
            weights = jnp.where(causal, weights, 0.0)
        part = dot(weights.astype(BF16), values[:, cols])
        acc_ref[:, cols] = part if before_ref is None else before_ref[:, cols] + part


def project(normed, w_ref, block):
    width = normed.shape[1]
    return silu(dot(normed, w_ref[:, block * width : (block + 1) * width])).astype(BF16)


def causal_mask(rows):
    return lax.broadcasted_iota(jnp.int32, (rows, rows), 0) >= lax.broadcasted_iota(jnp.int32, (rows, rows), 1)


def fetch(pairs, sems):
    copies = [pltpu.make_async_copy(src, dst, sems.at[i]) for i, (src, dst) in enumerate(pairs)]
    for copy in copies:
        copy.start()
    return copies


def own_kernel(info_ref, x_hbm, w_hbm, gate_ref, q_ref, k_ref, v_ref, acc_ref, x_ref, w_ref, sems):
    rows, width = x_ref.shape
    parts = [2, 3, 1, 0]
    pairs = [(w_hbm.at[:, i * width : (i + 1) * width], w_ref.at[i]) for i in parts]
    copies = fetch([(x_hbm, x_ref)] + pairs, sems)
    copies[0].wait()
    keep = kept_rows(info_ref[0], rows, info_ref[1])
    normed = row_norm(x_ref[...].astype(F32), keep).astype(BF16)
    for copy, i, to_ref in zip(copies[1:], parts, [q_ref, k_ref, v_ref, gate_ref]):
        copy.wait()
        to_ref[...] = silu(dot(normed, w_ref[i])).astype(BF16)
    attend(q_ref, k_ref, v_ref, acc_ref, None, causal_mask(rows))


def guest_kernel(
    info_ref, x_ref, w_ref, k_ref, v_ref, own_x_ref, own_gate_ref, own_q_ref, own_acc_ref,
    all_x_ref, all_gate_ref, all_q_ref, all_acc_ref, guest_k_ref, guest_v_ref,
):
    rows = x_ref.shape[0]
    own, guest = slice(0, rows), slice(rows, 2 * rows)
    keep = kept_rows(info_ref[0] + rows, rows, info_ref[1])
    normed = row_norm(x_ref[...].astype(F32), keep).astype(BF16)
    all_x_ref[own, :], all_x_ref[guest, :] = own_x_ref[...], x_ref[...]
    all_gate_ref[own, :], all_gate_ref[guest, :] = own_gate_ref[...], project(normed, w_ref, 0)
    all_q_ref[own, :], all_q_ref[guest, :] = own_q_ref[...], project(normed, w_ref, 2)
    all_acc_ref[own, :] = own_acc_ref[...]
    guest_k_ref[...] = project(normed, w_ref, 3)
    guest_v_ref[...] = project(normed, w_ref, 1)
    q_ref, acc_ref = all_q_ref.at[guest, :], all_acc_ref.at[guest, :]
    attend(q_ref, guest_k_ref, guest_v_ref, acc_ref, None, causal_mask(rows))
    attend(q_ref, k_ref, v_ref, acc_ref, acc_ref)


def add_block(info_ref, back, x_ref, w_ref, q_ref, acc_ref, before_ref):
    keep = kept_rows(info_ref[0] - back, x_ref.shape[0], info_ref[1])
    normed = row_norm(x_ref[...].astype(F32), keep).astype(BF16)
    attend(q_ref, project(normed, w_ref, 3), project(normed, w_ref, 1), acc_ref, before_ref)


def step_kernel(back, info_ref, x_ref, w_ref, q_ref, before_ref, acc_ref):
    add_block(info_ref, back, x_ref, w_ref, q_ref, acc_ref, before_ref)


def last_kernel(
    back, info_ref, x_ref, w_ref, q_ref, before_ref, gate_ref, own_ref, w_out_ref, w_proj_ref,
    layer_ref, out_ref, hat_ref, acc_ref,
):
    add_block(info_ref, back, x_ref, w_ref, q_ref, acc_ref, before_ref)
    gated = (row_norm(acc_ref[...]) * gate_ref[...].astype(F32)).astype(BF16)
    layer = (dot(gated, w_out_ref[...]) + own_ref[...].astype(F32)).astype(BF16)
    layer_ref[...] = layer
    out = dot(layer, w_proj_ref[...])
    out_ref[...] = out
    hat_ref[...] = (out / norm_of(out)).astype(BF16)


def split3(x):
    high = x.astype(BF16).astype(F32)
    mid = (x - high).astype(BF16).astype(F32)
    return [high, mid, x - high - mid]


def id_digits(ids):
    return [(ids >> 14).astype(F32), ((ids >> 7) & 127).astype(F32), (ids & 127).astype(F32)]


def of_digits(a, b, c):
    return a * 16384.0 + b * 128.0 + c


def padded_rows(count):
    return -(-count // 16) * 16


def table_kernel(
    x_hbm, ids_hbm, pos_hbm, pos_ids_hbm, table_ref, message_ref, x_ref, ids_ref, pos_ref, pos_ids_ref, sems
):
    pairs = [(x_hbm, x_ref), (ids_hbm, ids_ref), (pos_hbm, pos_ref), (pos_ids_hbm, pos_ids_ref)]
    for copy in fetch(pairs, sems):
        copy.wait()
    count, embed = x_ref.shape
    x = x_ref[...].astype(F32)
    table_ref[:count, :] = (x / norm_of(x)).astype(BF16)
    ids = jnp.concatenate([ids_ref[:, i : i + embed] for i in range(0, count, embed)], axis=0)
    parts = split3(log_sample_chance(ids.astype(F32)) * LOG2E) + id_digits(ids)
    used = len(parts) * ids.shape[0]
    pad = jnp.zeros((table_ref.shape[0] - count - used, embed), F32)
    table_ref[count:, :] = jnp.concatenate(parts + [pad], axis=0).astype(BF16)
    rows = pos_ref.shape[0]
    parts = id_digits(pos_ids_ref[...])
    pad = jnp.zeros((message_ref.shape[0] - rows - len(parts), embed), F32)
    message_ref[:rows, :] = pos_ref[...]
    message_ref[rows:, :] = jnp.concatenate(parts + [pad], axis=0).astype(BF16)


def head_kernel(
    hist_count, info_ref, hat_ref, out_ref, layer_ref, pos_ref, ids_ref, guest_ref, *rest
):
    *table_refs, loss_ref, guest_loss_ref, message_ref, keep_ref, send_ref, proj_ref, kept_ref = rest
    rows, embed = hat_ref.shape
    block = rows // 2
    chunks = table_refs[0].shape[0] // (embed + 6)
    count = chunks * embed
    hat = hat_ref[...]
    guest_parts = guest_ref[block:, :].astype(F32)
    id_rows = [id_digits(ids_ref[...]), [guest_parts[i : i + 1, :] for i in range(3)]]
    id_row = jnp.concatenate([of_digits(*digits) for digits in id_rows], axis=1)
    pos_id = column(id_row)
    pos = jnp.concatenate([pos_ref[...], guest_ref[:block, :]], axis=0).astype(F32)
    pos_unit = pos / norm_of(pos)
    pos_score = (
        jnp.sum(hat.astype(F32) * pos_unit, axis=-1, keepdims=True) / SOFTMAX_WARMTH - column(log_sample_chance(id_row))
    )
    lanes = jnp.zeros((rows, 128), F32)
    grads = jnp.zeros((rows, embed), F32)
    steps = [(table_ref, chunk) for table_ref in table_refs for chunk in range(chunks)]

    def table_scores(table_ref, chunk):
        return dot_t(hat, table_ref[chunk * embed : (chunk + 1) * embed, :])

    following = table_scores(*steps[0])
    for step, (table_ref, chunk) in enumerate(steps):
        scores = following * SCORE_SCALE
        if step + 1 < len(steps):
            following = table_scores(*steps[step + 1])
        row = [table_ref[count:, :][i : i + 1, :].astype(F32) for i in range(chunk, 6 * chunks, chunks)]
        kept = jnp.where(of_digits(*row[3:]) != pos_id, jnp.exp2(scores - (row[0] + row[1] + row[2])), 0.0)
        for lane in range(0, embed, 128):
            lanes = lanes + kept[:, lane : lane + 128]
        kept_ref[:, chunk * embed : (chunk + 1) * embed] = kept.astype(BF16)
        if chunk == chunks - 1:
            grads = grads + dot(kept_ref[...], table_ref[:count, :])
    pos_part = jnp.exp(pos_score)
    total = pos_part + jnp.sum(lanes, axis=-1, keepdims=True)
    log_total = jnp.log(total)
    at = lax.broadcasted_iota(jnp.int32, (rows, 1), 0)
    valid = info_ref[0] + at < jnp.where(at < block, info_ref[5], info_ref[6])
    loss = jnp.where(valid, log_total - pos_score, 0.0)
    shift = jnp.where(valid, (log_total + math.log(hist_count)) * LOG2E, FAR)
    loss = jnp.broadcast_to(loss, (rows, 128)).T
    loss_ref[...] = loss[:1, :block]
    guest_loss_ref[...] = loss[:1, block:]
    shift = jnp.broadcast_to(shift, (rows, 128)).T
    parts = []
    for i in range(2):
        parts += split3(shift[:1, i * block : (i + 1) * block]) + id_rows[i]
    pad = jnp.zeros((message_ref.shape[0] - len(parts), embed), F32)
    message_ref[...] = jnp.concatenate(parts + [pad], axis=0).astype(BF16)
    share = jnp.where(valid, 1.0 / (total * hist_count), 0.0)
    pos_weight = jnp.where(valid, pos_part / total - 1.0, 0.0) / hist_count
    d_unit = (pos_weight * pos_unit + share * grads) / SOFTMAX_WARMTH
    out = out_ref[...]
    norms = norm_of(out)
    unit = out / norms
    d_out = ((d_unit - unit * jnp.sum(unit * d_unit, axis=-1, keepdims=True)) / norms).astype(BF16)
    proj_ref[...] = t_dot(layer_ref[...], d_out)
    half = keep_ref.shape[0]
    keep_ref[...] = proj_ref[part_at(info_ref[3], half), :]
    send_ref[...] = proj_ref[part_at(1 - info_ref[3], half), :].astype(BF16)


def part_at(index, rows):
    return pl.ds(pl.multiple_of(index * rows, rows), rows)


def halved_kernel(chip, info_ref, keep_ref, got_ref, message_ref, own_ref, *rest):
    *send_refs, sum_ref = rest
    rows = own_ref.shape[0]
    sum_ref[...] = keep_ref[...] + got_ref[...].astype(F32)
    own_ref[...] = sum_ref[part_at(info_ref[4], rows), :]
    for r, send_ref in enumerate(send_refs, 1):
        send_ref[:rows, :] = sum_ref[part_at(lax.bitwise_xor(info_ref[4], r), rows), :].astype(BF16)
        if r == chip:
            send_ref[rows:, :] = message_ref[...]


def sum_kernel(*refs):
    rows = refs[-1].shape[0]
    parts = [ref[:rows, :].astype(F32) for ref in refs[:-1]]
    while len(parts) > 1:
        parts = [a + b for a, b in zip(parts[::2], parts[1::2])]
    refs[-1][...] = parts[0].astype(refs[-1].dtype)


def lay_kernel(info_ref, *refs):
    *part_refs, out_ref = refs
    rows = part_refs[0].shape[0]
    chips = len(part_refs) // 2
    for i, part_ref in enumerate(part_refs):
        core, r = divmod(i, chips)
        at = lax.bitwise_xor(info_ref[3], core) * chips + lax.bitwise_xor(info_ref[4], r)
        out_ref[part_at(at, rows), :] = part_ref[...].astype(out_ref.dtype)


def loss_sum_kernel(loss_ref, *refs):
    *part_refs, out_ref = refs
    rows, events = part_refs[0].shape[0], loss_ref.shape[1]
    sum_kernel(*part_refs, out_ref.at[:rows, :])
    parts = split3(loss_ref[...])
    pad = jnp.zeros((16 - len(parts), events), F32)
    out_ref[rows:, :] = jnp.concatenate(parts + [pad], axis=0).astype(BF16)


def last_sum_kernel(last, info_ref, loss_ref, got_ref, part_ref, *rest):
    *got_refs, own_loss_ref, sum_ref = rest
    parts = got_ref[got_ref.shape[0] - 16 :, :].astype(F32)
    above = parts[0:1, :] + parts[1:2, :] + parts[2:3, :]
    own_loss_ref[...] = jnp.where(info_ref[2] == last, above, loss_ref[...])
    sum_kernel(part_ref, *got_refs, sum_ref)


def negative_kernel(pool_count, info_ref, neg_ref, neg_id_ref, *rest):
    gathered, rest = rest[: 2 * pool_count], rest[2 * pool_count :]
    own_ref, *send_refs, turned_ref, sum_ref, weight_ref = rest
    count, embed = neg_ref.shape
    rows = embed
    blocks = gathered[0].shape[0] // rows
    tile = min(256, count)
    neg = neg_ref[...].astype(F32)
    norms = norm_of(neg)
    unit = neg / norms
    neg_hat = unit.astype(BF16)
    id_row = neg_id_ref[...].astype(F32)
    neg_id = column(id_row)
    for i, (hats_ref, message_ref) in enumerate(zip(gathered[:pool_count], gathered[pool_count:])):
        parts = message_ref[message_ref.shape[0] - 16 :, :].astype(F32)
        for block, start in itertools.product(range(blocks), range(0, count, tile)):
            own = slice(block * rows, (block + 1) * rows)
            cut = slice(start, start + tile)
            shift = [parts[6 * block + j : 6 * block + j + 1, :] for j in range(6)]
            scores = dot_t(neg_hat[cut, :], hats_ref[own, :]) * SCORE_SCALE - (shift[0] + shift[1] + shift[2])
            weights = jnp.where(neg_id[cut, :] != of_digits(*shift[3:]), jnp.exp2(scores), 0.0)
            weight_ref[cut, own] = weights.astype(BF16)
        for start in range(0, count, tile):
            cut = slice(start, start + tile)
            term = dot(weight_ref[cut, :], hats_ref[...])
            sum_ref[cut, :] = sum_ref[cut, :] + term if i else term
    neg_sum = sum_ref[...] * column(jnp.exp2(-LOG2E * log_sample_chance(id_row)) / SOFTMAX_WARMTH)
    grad = (neg_sum - unit * jnp.sum(unit * neg_sum, axis=-1, keepdims=True)) / norms
    turned_ref[...] = grad.T
    cols = own_ref.shape[0]
    own_ref[...] = turned_ref[part_at(info_ref[2], cols), :]
    for r, send_ref in enumerate(send_refs, 1):
        send_ref[...] = turned_ref[part_at(lax.bitwise_xor(info_ref[2], r), cols), :].astype(BF16)


def call(kernel, ins, outs, scratch=(), limit=24, micros=0.5, name=None, place=pltpu.VMEM):
    in_specs = [pl.BlockSpec(memory_space=pltpu.SMEM if x.ndim == 1 else place) for x in ins]
    many = isinstance(outs, (list, tuple))
    out_specs = jax.tree.map(lambda _: pl.BlockSpec(memory_space=pltpu.VMEM), outs)
    return pl.pallas_call(
        kernel,
        out_shape=list(outs) if many else outs,
        in_specs=in_specs,
        out_specs=list(out_specs) if many else out_specs,
        scratch_shapes=list(scratch),
        compiler_params=pltpu.CompilerParams(vmem_limit_bytes=limit * MIB),
        cost_estimate=pl.CostEstimate(flops=int(micros * 5.75e8), bytes_accessed=0, transcendentals=0),
        name=name,
    )(*ins)


def swap(x, axis, count, r):
    return lax.ppermute(x, axis, [(i, i ^ r) for i in range(count)])


def gather_step(blocks, axis, count):
    bit = count // (2 * len(blocks))
    return blocks + [swap(block, axis, count, bit) for block in blocks] if bit else blocks


def together(*trees):
    return lax.optimization_barrier(trees)


def struct(shape, kind):
    return jax.ShapeDtypeStruct(shape, kind)


def body(tokens, w_in, w_out, w_proj, pos_embed, pos_ids, lengths, neg_embed, neg_ids):
    rows, width = tokens.shape[1:]
    embed = w_proj.shape[1]
    seq_count = lax.axis_size("seq")
    pool_count = lax.axis_size("pool")
    plane = ("batch", "pool")
    plane_count = lax.axis_size("batch") * pool_count
    seq_at = lax.axis_index("seq")
    plane_at = lax.axis_index("batch") * pool_count + lax.axis_index("pool")
    own_end = jnp.where(seq_at == seq_count - 1, 0, lengths[0])
    guest_end = jnp.where(seq_at == seq_count - 2, lengths[0], 0)
    info = jnp.stack([seq_at * rows, lengths[0], seq_at, plane_at % 2, plane_at // 2, own_end, guest_end])
    info = info.astype(jnp.int32)
    own = tokens[0]
    local_neg = neg_embed.shape[1]

    ups = [[(i, i + 1) for i in range(hop, seq_count - 2)] for hop in range(seq_count - 2)]
    down = [(seq_count - 1, seq_count - 2)]
    block = lax.ppermute(own, "seq", ups[0])
    guest = lax.ppermute(own, "seq", down)
    kind = struct((rows, width), BF16)
    wide = struct((rows, width), F32)
    gate, queries, keys, values, acc = call(
        own_kernel,
        [info, own, w_in],
        [kind, kind, kind, kind, wide],
        scratch=[pltpu.VMEM((rows, width), BF16), pltpu.VMEM((4, width, width), BF16), pltpu.SemaphoreType.DMA((5,))],
        place=pl.ANY,
        limit=44,
        micros=6, name="own_block",
    )
    table_part, pos_part = call(
        table_kernel,
        [neg_embed[0], neg_ids, pos_embed[0], pos_ids],
        [
            struct((local_neg + padded_rows(6 * local_neg // embed), embed), BF16),
            struct((rows + 16, embed), BF16),
        ],
        scratch=[
            pltpu.VMEM((local_neg, embed), BF16), pltpu.VMEM((1, local_neg), jnp.int32),
            pltpu.VMEM((rows, embed), BF16), pltpu.VMEM((1, rows), jnp.int32), pltpu.SemaphoreType.DMA((4,)),
        ],
        place=pl.ANY,
        limit=24,
        micros=0.6, name="table_part",
    )
    table_part, pos_part, acc = together(table_part, pos_part, acc)
    table = gather_step([table_part], "pool", pool_count)
    block, guest, acc = together(block, guest, acc)
    tall = struct((2 * rows, width), BF16)
    tall_wide = struct((2 * rows, width), F32)
    for step in range(1, seq_count - 2):
        following = lax.ppermute(block, "seq", ups[step])
        if step == 1:
            own, gate, queries, acc = call(
                guest_kernel,
                [info, guest, w_in, keys, values, own, gate, queries, acc],
                [tall, tall, tall, tall_wide],
                scratch=[pltpu.VMEM((rows, width), BF16)] * 2,
                micros=4.8, name="guest_block",
            )
        acc = call(
            functools.partial(step_kernel, step * rows),
            [info, block, w_in, queries, acc],
            tall_wide,
            micros=3.6, name=f"earlier_block_{step}",
        )
        acc, table, pos_part = together(acc, table, pos_part)
        if step == 1:
            guest_pos = lax.ppermute(pos_part, "seq", down)
        table = gather_step(table, "pool", pool_count)
        block, acc = together(following, acc)
    while len(table) < pool_count:
        table = gather_step(table, "pool", pool_count)
    layer, out, hat = call(
        functools.partial(last_kernel, (seq_count - 2) * rows),
        [info, block, w_in, queries, acc, gate, own, w_out, w_proj],
        [tall, struct((2 * rows, embed), F32), struct((2 * rows, embed), BF16)],
        scratch=[pltpu.VMEM((2 * rows, width), F32)],
        micros=6, name="last_block",
    )
    hats = gather_step([hat], "pool", pool_count)

    half, chips = width // 2, plane_count // 2
    loss, guest_loss, message, keep, send = call(
        functools.partial(head_kernel, plane_count),
        [info, hat, out, layer, pos_embed[0], pos_ids, guest_pos, *table],
        [
            struct((1, rows), F32), struct((1, rows), F32), struct((16, embed), BF16),
            struct((half, embed), F32), struct((half, embed), BF16),
        ],
        scratch=[pltpu.VMEM((width, embed), F32), pltpu.VMEM((2 * rows, local_neg), BF16)],
        micros=5, name="head",
    )
    part = struct((half // chips, embed), BF16)
    cols = embed // seq_count
    def plane_swap(parts):
        return [swap(x, plane, plane_count, 2 * r) for r, x in enumerate(parts, 1)]

    chip = pool_count // 4
    sizes = [part.shape[0] + 16 * (r == chip) for r in range(1, chips)]
    own_part, *sends = call(
        functools.partial(halved_kernel, chip),
        [info, keep, swap(send, plane, plane_count, 1), message],
        [struct(part.shape, F32)] + [struct((size, embed), BF16) for size in sizes],
        scratch=[pltpu.VMEM((half, embed), F32)],
        micros=0.6, name="halved",
    )
    proj_parts = plane_swap(sends)
    proj_part = call(sum_kernel, [own_part] + proj_parts, part, name="plane_sum")
    while len(hats) < pool_count:
        hats = gather_step(hats, "pool", pool_count)
    messages = [message, proj_parts[chip - 1]]
    while len(messages) < pool_count:
        messages = gather_step(messages, "pool", pool_count)
    hats, messages, _ = together(hats, messages, proj_part)
    d_part, *sends = call(
        functools.partial(negative_kernel, pool_count),
        [info, neg_embed[0], neg_ids, *hats, *messages],
        [struct((cols, local_neg), F32)]
        + [struct((cols, local_neg), BF16)] * (seq_count - 1),
        scratch=[
            pltpu.VMEM((embed, local_neg), F32), pltpu.VMEM((local_neg, embed), F32),
            pltpu.VMEM((local_neg, 2 * rows), BF16),
        ],
        micros=3.7, name="neg_grad",
    )
    bit = seq_count // 2
    got, sends = together(swap(proj_part, "seq", seq_count, bit), sends)
    while bit > 2:
        proj_part = call(sum_kernel, [proj_part, got], part, name=f"seq_sum_{bit}")
        bit //= 2
        got = swap(proj_part, "seq", seq_count, bit)
    proj_part = call(
        loss_sum_kernel,
        [guest_loss, proj_part, got],
        struct((part.shape[0] + 16, embed), BF16),
        name="seq_sum_2",
    )
    loss_got = swap(proj_part, "seq", seq_count, 1)
    proj_part = call(sum_kernel, [proj_part, loss_got], part, name="seq_sum_1")
    gots = [swap(x, "seq", seq_count, r) for r, x in enumerate(sends[1:], 2)]
    others = plane_swap([proj_part] * (chips - 1))
    first, _ = together(sends[0], others)
    others, gots = together(others, gots)
    gots = [swap(first, "seq", seq_count, 1)] + gots
    proj_parts = [proj_part] + others
    proj_parts += [swap(x, plane, plane_count, 1) for x in proj_parts]
    d_proj = call(lay_kernel, [info, *proj_parts], struct((width, embed), F32), micros=0, name="lay_whole")
    loss, d_neg = call(
        functools.partial(last_sum_kernel, seq_count - 1),
        [info, loss, loss_got, d_part, *gots],
        [struct((1, rows), F32), struct((cols, local_neg), F32)],
        micros=0.9, name="neg_sum",
    )
    return (loss, d_neg.T[None], d_proj)


def solution(mesh):
    placed = (
        P(("batch", "pool"), "seq", None),
        P(),
        P(),
        P(),
        P(("batch", "pool"), "seq", None),
        P(("batch", "pool"), "seq"),
        P(("batch", "pool")),
        P("batch", "pool", None),
        P("batch", "pool"),
    )
    return jax.shard_map(
        body,
        mesh=mesh,
        in_specs=placed,
        out_specs=(P(("batch", "pool"), "seq"), P("batch", "pool", "seq"), P()),
        check_vma=False,
    )
```

```python
import functools
import itertools
import math

import jax
import jax.numpy as jnp
from jax import lax
from jax.experimental import pallas as pl
from jax.experimental.pallas import tpu as pltpu
from jax.sharding import PartitionSpec as P

HEADS = 8
ITEMS = 1048576

SOFTMAX_WARMTH = 0.02
NORM_EPSILON = 1e-05
UNIT_EPSILON = 1e-06
LOG2E = math.log2(math.e)
SCORE_SCALE = LOG2E / SOFTMAX_WARMTH
FAR = 10000.0

F32 = jnp.float32
BF16 = jnp.bfloat16
MIB = 1 << 20


def log_sample_chance(item_ids):
    x = 1.0 / (item_ids + 1.0)
    series = x * (1.0 - x * (1 / 2 - x * (1 / 3 - x * (1 / 4 - x * (1 / 5 - x * (1 / 6))))))
    return jnp.log(jnp.where(x > 1 / 16, jnp.log(1.0 + x), series)) - math.log(math.log(ITEMS + 1.0))


def column(row):
    return jnp.broadcast_to(row, (128, row.shape[1])).T[:, :1]


def dot(a, b):
    return jnp.dot(a, b, preferred_element_type=F32)


def dot_t(a, b):
    return lax.dot_general(a, b, (((1,), (1,)), ((), ())), preferred_element_type=F32)


def t_dot(a, b):
    return lax.dot_general(a, b, (((0,), (0,)), ((), ())), preferred_element_type=F32)


def silu(v):
    half = 0.5 * v
    return half + half * jnp.tanh(half)


def row_norm(x, keep=None):
    center = x - jnp.mean(x, axis=-1, keepdims=True)
    scale = lax.rsqrt(jnp.mean(center * center, axis=-1, keepdims=True) + NORM_EPSILON)
    if keep is not None:
        scale = jnp.where(keep, scale, 0.0)
    return center * scale


def norm_of(x):
    return jnp.sqrt(jnp.sum(x * x, axis=-1, keepdims=True) + UNIT_EPSILON)


def kept_rows(first, rows, length):
    return first + lax.broadcasted_iota(jnp.int32, (rows, 1), 0) < length


def attend(q_ref, keys, values, acc_ref, before_ref, causal=None):
    rows, width = q_ref.shape
    head = width // HEADS
    spans = [slice(h * head, (h + 1) * head) for h in range(HEADS)]
    following = dot_t(q_ref[:, spans[0]], keys[:, spans[0]])
    for h, cols in enumerate(spans):
        half = following * (0.5 / math.sqrt(head))
        if h + 1 < HEADS:
            following = dot_t(q_ref[:, spans[h + 1]], keys[:, spans[h + 1]])
        weights = half + half * jnp.tanh(half)
        if causal is not None:
            weights = jnp.where(causal, weights, 0.0)
        part = dot(weights.astype(BF16), values[:, cols])
        acc_ref[:, cols] = part if before_ref is None else before_ref[:, cols] + part


def project(normed, w_ref, block):
    width = normed.shape[1]
    return silu(dot(normed, w_ref[:, block * width : (block + 1) * width])).astype(BF16)


def causal_mask(rows):
    return lax.broadcasted_iota(jnp.int32, (rows, rows), 0) >= lax.broadcasted_iota(jnp.int32, (rows, rows), 1)


def fetch(pairs, sems):
    copies = [pltpu.make_async_copy(src, dst, sems.at[i]) for i, (src, dst) in enumerate(pairs)]
    for copy in copies:
        copy.start()
    return copies


def own_kernel(info_ref, x_hbm, w_hbm, gate_ref, q_ref, k_ref, v_ref, acc_ref, x_ref, w_ref, sems):
    rows, width = x_ref.shape
    parts = [2, 3, 1, 0]
    pairs = [(w_hbm.at[:, i * width : (i + 1) * width], w_ref.at[i]) for i in parts]
    copies = fetch([(x_hbm, x_ref)] + pairs, sems)
    copies[0].wait()
    keep = kept_rows(info_ref[0], rows, info_ref[1])
    normed = row_norm(x_ref[...].astype(F32), keep).astype(BF16)
    for copy, i, to_ref in zip(copies[1:], parts, [q_ref, k_ref, v_ref, gate_ref]):
        copy.wait()
        to_ref[...] = silu(dot(normed, w_ref[i])).astype(BF16)
    attend(q_ref, k_ref, v_ref, acc_ref, None, causal_mask(rows))


def guest_kernel(
    info_ref, x_ref, w_ref, k_ref, v_ref, own_x_ref, own_gate_ref, own_q_ref, own_acc_ref,
    all_x_ref, all_gate_ref, all_q_ref, all_acc_ref, guest_k_ref, guest_v_ref,
):
    rows = x_ref.shape[0]
    own, guest = slice(0, rows), slice(rows, 2 * rows)
    keep = kept_rows(info_ref[0] + rows, rows, info_ref[1])
    normed = row_norm(x_ref[...].astype(F32), keep).astype(BF16)
    all_x_ref[own, :], all_x_ref[guest, :] = own_x_ref[...], x_ref[...]
    all_gate_ref[own, :], all_gate_ref[guest, :] = own_gate_ref[...], project(normed, w_ref, 0)
    all_q_ref[own, :], all_q_ref[guest, :] = own_q_ref[...], project(normed, w_ref, 2)
    all_acc_ref[own, :] = own_acc_ref[...]
    guest_k_ref[...] = project(normed, w_ref, 3)
    guest_v_ref[...] = project(normed, w_ref, 1)
    q_ref, acc_ref = all_q_ref.at[guest, :], all_acc_ref.at[guest, :]
    attend(q_ref, guest_k_ref, guest_v_ref, acc_ref, None, causal_mask(rows))
    attend(q_ref, k_ref, v_ref, acc_ref, acc_ref)


def add_block(info_ref, back, x_ref, w_ref, q_ref, acc_ref, before_ref):
    keep = kept_rows(info_ref[0] - back, x_ref.shape[0], info_ref[1])
    normed = row_norm(x_ref[...].astype(F32), keep).astype(BF16)
    attend(q_ref, project(normed, w_ref, 3), project(normed, w_ref, 1), acc_ref, before_ref)


def step_kernel(back, info_ref, x_ref, w_ref, q_ref, before_ref, acc_ref):
    add_block(info_ref, back, x_ref, w_ref, q_ref, acc_ref, before_ref)


def last_kernel(
    back, info_ref, x_ref, w_ref, q_ref, before_ref, gate_ref, own_ref, w_out_ref, w_proj_ref,
    layer_ref, out_ref, hat_ref, acc_ref,
):
    add_block(info_ref, back, x_ref, w_ref, q_ref, acc_ref, before_ref)
    gated = (row_norm(acc_ref[...]) * gate_ref[...].astype(F32)).astype(BF16)
    layer = (dot(gated, w_out_ref[...]) + own_ref[...].astype(F32)).astype(BF16)
    layer_ref[...] = layer
    out = dot(layer, w_proj_ref[...])
    out_ref[...] = out
    hat_ref[...] = (out / norm_of(out)).astype(BF16)


def split3(x):
    high = x.astype(BF16).astype(F32)
    mid = (x - high).astype(BF16).astype(F32)
    return [high, mid, x - high - mid]


def id_digits(ids):
    return [(ids >> 14).astype(F32), ((ids >> 7) & 127).astype(F32), (ids & 127).astype(F32)]


def of_digits(a, b, c):
    return a * 16384.0 + b * 128.0 + c


def padded_rows(count):
    return -(-count // 16) * 16


def table_kernel(
    x_hbm, ids_hbm, pos_hbm, pos_ids_hbm, table_ref, message_ref, x_ref, ids_ref, pos_ref, pos_ids_ref, sems
):
    pairs = [(x_hbm, x_ref), (ids_hbm, ids_ref), (pos_hbm, pos_ref), (pos_ids_hbm, pos_ids_ref)]
    for copy in fetch(pairs, sems):
        copy.wait()
    count, embed = x_ref.shape
    x = x_ref[...].astype(F32)
    table_ref[:count, :] = (x / norm_of(x)).astype(BF16)
    ids = jnp.concatenate([ids_ref[:, i : i + embed] for i in range(0, count, embed)], axis=0)
    parts = split3(log_sample_chance(ids.astype(F32)) * LOG2E) + id_digits(ids)
    used = len(parts) * ids.shape[0]
    pad = jnp.zeros((table_ref.shape[0] - count - used, embed), F32)
    table_ref[count:, :] = jnp.concatenate(parts + [pad], axis=0).astype(BF16)
    rows = pos_ref.shape[0]
    parts = id_digits(pos_ids_ref[...])
    pad = jnp.zeros((message_ref.shape[0] - rows - len(parts), embed), F32)
    message_ref[:rows, :] = pos_ref[...]
    message_ref[rows:, :] = jnp.concatenate(parts + [pad], axis=0).astype(BF16)


def head_kernel(
    hist_count, info_ref, hat_ref, out_ref, layer_ref, pos_ref, ids_ref, guest_ref, *rest
):
    *table_refs, loss_ref, guest_loss_ref, message_ref, keep_ref, send_ref, proj_ref, kept_ref = rest
    rows, embed = hat_ref.shape
    block = rows // 2
    chunks = table_refs[0].shape[0] // (embed + 6)
    count = chunks * embed
    hat = hat_ref[...]
    guest_parts = guest_ref[block:, :].astype(F32)
    id_rows = [id_digits(ids_ref[...]), [guest_parts[i : i + 1, :] for i in range(3)]]
    id_row = jnp.concatenate([of_digits(*digits) for digits in id_rows], axis=1)
    pos_id = column(id_row)
    pos = jnp.concatenate([pos_ref[...], guest_ref[:block, :]], axis=0).astype(F32)
    pos_unit = pos / norm_of(pos)
    pos_score = (
        jnp.sum(hat.astype(F32) * pos_unit, axis=-1, keepdims=True) / SOFTMAX_WARMTH - column(log_sample_chance(id_row))
    )
    lanes = jnp.zeros((rows, 128), F32)
    grads = jnp.zeros((rows, embed), F32)
    steps = [(table_ref, chunk) for table_ref in table_refs for chunk in range(chunks)]

    def table_scores(table_ref, chunk):
        return dot_t(hat, table_ref[chunk * embed : (chunk + 1) * embed, :])

    following = table_scores(*steps[0])
    for step, (table_ref, chunk) in enumerate(steps):
        scores = following * SCORE_SCALE
        if step + 1 < len(steps):
            following = table_scores(*steps[step + 1])
        row = [table_ref[count:, :][i : i + 1, :].astype(F32) for i in range(chunk, 6 * chunks, chunks)]
        kept = jnp.where(of_digits(*row[3:]) != pos_id, jnp.exp2(scores - (row[0] + row[1] + row[2])), 0.0)
        for lane in range(0, embed, 128):
            lanes = lanes + kept[:, lane : lane + 128]
        kept_ref[:, chunk * embed : (chunk + 1) * embed] = kept.astype(BF16)
        if chunk == chunks - 1:
            grads = grads + dot(kept_ref[...], table_ref[:count, :])
    pos_part = jnp.exp(pos_score)
    total = pos_part + jnp.sum(lanes, axis=-1, keepdims=True)
    log_total = jnp.log(total)
    at = lax.broadcasted_iota(jnp.int32, (rows, 1), 0)
    valid = info_ref[0] + at < jnp.where(at < block, info_ref[5], info_ref[6])
    loss = jnp.where(valid, log_total - pos_score, 0.0)
    shift = jnp.where(valid, (log_total + math.log(hist_count)) * LOG2E, FAR)
    loss = jnp.broadcast_to(loss, (rows, 128)).T
    loss_ref[...] = loss[:1, :block]
    guest_loss_ref[...] = loss[:1, block:]
    shift = jnp.broadcast_to(shift, (rows, 128)).T
    parts = []
    for i in range(2):
        parts += split3(shift[:1, i * block : (i + 1) * block]) + id_rows[i]
    pad = jnp.zeros((message_ref.shape[0] - len(parts), embed), F32)
    message_ref[...] = jnp.concatenate(parts + [pad], axis=0).astype(BF16)
    share = jnp.where(valid, 1.0 / (total * hist_count), 0.0)
    pos_weight = jnp.where(valid, pos_part / total - 1.0, 0.0) / hist_count
    d_unit = (pos_weight * pos_unit + share * grads) / SOFTMAX_WARMTH
    out = out_ref[...]
    norms = norm_of(out)
    unit = out / norms
    d_out = ((d_unit - unit * jnp.sum(unit * d_unit, axis=-1, keepdims=True)) / norms).astype(BF16)
    proj_ref[...] = t_dot(layer_ref[...], d_out)
    half = keep_ref.shape[0]
    keep_ref[...] = proj_ref[part_at(info_ref[3], half), :]
    send_ref[...] = proj_ref[part_at(1 - info_ref[3], half), :].astype(BF16)


def part_at(index, rows):
    return pl.ds(pl.multiple_of(index * rows, rows), rows)


def halved_kernel(chip, info_ref, keep_ref, got_ref, message_ref, own_ref, *rest):
    *send_refs, sum_ref = rest
    rows = own_ref.shape[0]
    sum_ref[...] = keep_ref[...] + got_ref[...].astype(F32)
    own_ref[...] = sum_ref[part_at(info_ref[4], rows), :]
    for r, send_ref in enumerate(send_refs, 1):
        send_ref[:rows, :] = sum_ref[part_at(lax.bitwise_xor(info_ref[4], r), rows), :].astype(BF16)
        if r == chip:
            send_ref[rows:, :] = message_ref[...]


def sum_kernel(*refs):
    rows = refs[-1].shape[0]
    parts = [ref[:rows, :].astype(F32) for ref in refs[:-1]]
    while len(parts) > 1:
        parts = [a + b for a, b in zip(parts[::2], parts[1::2])]
    refs[-1][...] = parts[0].astype(refs[-1].dtype)


def lay_kernel(info_ref, *refs):
    *part_refs, out_ref = refs
    rows = part_refs[0].shape[0]
    chips = len(part_refs) // 2
    for i, part_ref in enumerate(part_refs):
        core, r = divmod(i, chips)
        at = lax.bitwise_xor(info_ref[3], core) * chips + lax.bitwise_xor(info_ref[4], r)
        out_ref[part_at(at, rows), :] = part_ref[...].astype(out_ref.dtype)


def loss_sum_kernel(loss_ref, *refs):
    *part_refs, out_ref = refs
    rows, events = part_refs[0].shape[0], loss_ref.shape[1]
    sum_kernel(*part_refs, out_ref.at[:rows, :])
    parts = split3(loss_ref[...])
    pad = jnp.zeros((16 - len(parts), events), F32)
    out_ref[rows:, :] = jnp.concatenate(parts + [pad], axis=0).astype(BF16)


def final_kernel(last, count, info_ref, loss_ref, loss_got_ref, *refs):
    proj_refs, (*part_refs, own_loss_ref, sum_ref, proj_ref) = refs[:count], refs[count:]
    parts = loss_got_ref[loss_got_ref.shape[0] - 16 :, :].astype(F32)
    above = parts[0:1, :] + parts[1:2, :] + parts[2:3, :]
    own_loss_ref[...] = jnp.where(info_ref[2] == last, above, loss_ref[...])
    lay_kernel(info_ref, *proj_refs, proj_ref)
    sum_kernel(*part_refs, sum_ref)


def negative_kernel(pool_count, info_ref, neg_ref, neg_id_ref, *rest):
    gathered, rest = rest[: 2 * pool_count], rest[2 * pool_count :]
    own_ref, *send_refs, turned_ref, sum_ref, weight_ref = rest
    count, embed = neg_ref.shape
    rows = embed
    blocks = gathered[0].shape[0] // rows
    tile = min(256, count)
    neg = neg_ref[...].astype(F32)
    norms = norm_of(neg)
    unit = neg / norms
    neg_hat = unit.astype(BF16)
    id_row = neg_id_ref[...].astype(F32)
    neg_id = column(id_row)
    for i, (hats_ref, message_ref) in enumerate(zip(gathered[:pool_count], gathered[pool_count:])):
        parts = message_ref[message_ref.shape[0] - 16 :, :].astype(F32)
        for block, start in itertools.product(range(blocks), range(0, count, tile)):
            own = slice(block * rows, (block + 1) * rows)
            cut = slice(start, start + tile)
            shift = [parts[6 * block + j : 6 * block + j + 1, :] for j in range(6)]
            scores = dot_t(neg_hat[cut, :], hats_ref[own, :]) * SCORE_SCALE - (shift[0] + shift[1] + shift[2])
            weights = jnp.where(neg_id[cut, :] != of_digits(*shift[3:]), jnp.exp2(scores), 0.0)
            weight_ref[cut, own] = weights.astype(BF16)
        for start in range(0, count, tile):
            cut = slice(start, start + tile)
            term = dot(weight_ref[cut, :], hats_ref[...])
            sum_ref[cut, :] = sum_ref[cut, :] + term if i else term
    neg_sum = sum_ref[...] * column(jnp.exp2(-LOG2E * log_sample_chance(id_row)) / SOFTMAX_WARMTH)
    grad = (neg_sum - unit * jnp.sum(unit * neg_sum, axis=-1, keepdims=True)) / norms
    turned_ref[...] = grad.T
    cols = own_ref.shape[0]
    own_ref[...] = turned_ref[part_at(info_ref[2], cols), :]
    for r, send_ref in enumerate(send_refs, 1):
        send_ref[...] = turned_ref[part_at(lax.bitwise_xor(info_ref[2], r), cols), :].astype(BF16)


def call(kernel, ins, outs, scratch=(), limit=24, micros=0.5, name=None, place=pltpu.VMEM):
    in_specs = [pl.BlockSpec(memory_space=pltpu.SMEM if x.ndim == 1 else place) for x in ins]
    many = isinstance(outs, (list, tuple))
    out_specs = jax.tree.map(lambda _: pl.BlockSpec(memory_space=pltpu.VMEM), outs)
    return pl.pallas_call(
        kernel,
        out_shape=list(outs) if many else outs,
        in_specs=in_specs,
        out_specs=list(out_specs) if many else out_specs,
        scratch_shapes=list(scratch),
        compiler_params=pltpu.CompilerParams(vmem_limit_bytes=limit * MIB),
        cost_estimate=pl.CostEstimate(flops=int(micros * 5.75e8), bytes_accessed=0, transcendentals=0),
        name=name,
    )(*ins)


def swap(x, axis, count, r):
    return lax.ppermute(x, axis, [(i, i ^ r) for i in range(count)])


def gather_step(blocks, axis, count):
    bit = count // (2 * len(blocks))
    return blocks + [swap(block, axis, count, bit) for block in blocks] if bit else blocks


def together(*trees):
    return lax.optimization_barrier(trees)


def struct(shape, kind):
    return jax.ShapeDtypeStruct(shape, kind)


def body(tokens, w_in, w_out, w_proj, pos_embed, pos_ids, lengths, neg_embed, neg_ids):
    rows, width = tokens.shape[1:]
    embed = w_proj.shape[1]
    seq_count = lax.axis_size("seq")
    pool_count = lax.axis_size("pool")
    plane = ("batch", "pool")
    plane_count = lax.axis_size("batch") * pool_count
    seq_at = lax.axis_index("seq")
    plane_at = lax.axis_index("batch") * pool_count + lax.axis_index("pool")
    own_end = jnp.where(seq_at == seq_count - 1, 0, lengths[0])
    guest_end = jnp.where(seq_at == seq_count - 2, lengths[0], 0)
    info = jnp.stack([seq_at * rows, lengths[0], seq_at, plane_at % 2, plane_at // 2, own_end, guest_end])
    info = info.astype(jnp.int32)
    own = tokens[0]
    local_neg = neg_embed.shape[1]

    ups = [[(i, i + 1) for i in range(hop, seq_count - 2)] for hop in range(seq_count - 2)]
    down = [(seq_count - 1, seq_count - 2)]
    block = lax.ppermute(own, "seq", ups[0])
    guest = lax.ppermute(own, "seq", down)
    kind = struct((rows, width), BF16)
    wide = struct((rows, width), F32)
    gate, queries, keys, values, acc = call(
        own_kernel,
        [info, own, w_in],
        [kind, kind, kind, kind, wide],
        scratch=[pltpu.VMEM((rows, width), BF16), pltpu.VMEM((4, width, width), BF16), pltpu.SemaphoreType.DMA((5,))],
        place=pl.ANY,
        limit=44,
        micros=6, name="own_block",
    )
    table_part, pos_part = call(
        table_kernel,
        [neg_embed[0], neg_ids, pos_embed[0], pos_ids],
        [
            struct((local_neg + padded_rows(6 * local_neg // embed), embed), BF16),
            struct((rows + 16, embed), BF16),
        ],
        scratch=[
            pltpu.VMEM((local_neg, embed), BF16), pltpu.VMEM((1, local_neg), jnp.int32),
            pltpu.VMEM((rows, embed), BF16), pltpu.VMEM((1, rows), jnp.int32), pltpu.SemaphoreType.DMA((4,)),
        ],
        place=pl.ANY,
        limit=24,
        micros=0.6, name="table_part",
    )
    table_part, pos_part, acc = together(table_part, pos_part, acc)
    table = gather_step([table_part], "pool", pool_count)
    block, guest, acc = together(block, guest, acc)
    tall = struct((2 * rows, width), BF16)
    tall_wide = struct((2 * rows, width), F32)
    for step in range(1, seq_count - 2):
        following = lax.ppermute(block, "seq", ups[step])
        if step == 1:
            own, gate, queries, acc = call(
                guest_kernel,
                [info, guest, w_in, keys, values, own, gate, queries, acc],
                [tall, tall, tall, tall_wide],
                scratch=[pltpu.VMEM((rows, width), BF16)] * 2,
                micros=4.8, name="guest_block",
            )
        acc = call(
            functools.partial(step_kernel, step * rows),
            [info, block, w_in, queries, acc],
            tall_wide,
            micros=3.6, name=f"earlier_block_{step}",
        )
        acc, table, pos_part = together(acc, table, pos_part)
        if step == 1:
            guest_pos = lax.ppermute(pos_part, "seq", down)
        table = gather_step(table, "pool", pool_count)
        block, acc = together(following, acc)
    while len(table) < pool_count:
        table = gather_step(table, "pool", pool_count)
    layer, out, hat = call(
        functools.partial(last_kernel, (seq_count - 2) * rows),
        [info, block, w_in, queries, acc, gate, own, w_out, w_proj],
        [tall, struct((2 * rows, embed), F32), struct((2 * rows, embed), BF16)],
        scratch=[pltpu.VMEM((2 * rows, width), F32)],
        micros=6, name="last_block",
    )
    hats = gather_step([hat], "pool", pool_count)

    half, chips = width // 2, plane_count // 2
    loss, guest_loss, message, keep, send = call(
        functools.partial(head_kernel, plane_count),
        [info, hat, out, layer, pos_embed[0], pos_ids, guest_pos, *table],
        [
            struct((1, rows), F32), struct((1, rows), F32), struct((16, embed), BF16),
            struct((half, embed), F32), struct((half, embed), BF16),
        ],
        scratch=[pltpu.VMEM((width, embed), F32), pltpu.VMEM((2 * rows, local_neg), BF16)],
        micros=5, name="head",
    )
    part = struct((half // chips, embed), BF16)
    cols = embed // seq_count
    def plane_swap(parts):
        return [swap(x, plane, plane_count, 2 * r) for r, x in enumerate(parts, 1)]

    chip = pool_count // 4
    sizes = [part.shape[0] + 16 * (r == chip) for r in range(1, chips)]
    own_part, *sends = call(
        functools.partial(halved_kernel, chip),
        [info, keep, swap(send, plane, plane_count, 1), message],
        [struct(part.shape, F32)] + [struct((size, embed), BF16) for size in sizes],
        scratch=[pltpu.VMEM((half, embed), F32)],
        micros=0.6, name="halved",
    )
    proj_parts = plane_swap(sends)
    proj_part = call(sum_kernel, [own_part] + proj_parts, part, name="plane_sum")
    while len(hats) < pool_count:
        hats = gather_step(hats, "pool", pool_count)
    messages = [message, proj_parts[chip - 1]]
    while len(messages) < pool_count:
        messages = gather_step(messages, "pool", pool_count)
    hats, messages, _ = together(hats, messages, proj_part)
    d_part, *sends = call(
        functools.partial(negative_kernel, pool_count),
        [info, neg_embed[0], neg_ids, *hats, *messages],
        [struct((cols, local_neg), F32)]
        + [struct((cols, local_neg), BF16)] * (seq_count - 1),
        scratch=[
            pltpu.VMEM((embed, local_neg), F32), pltpu.VMEM((local_neg, embed), F32),
            pltpu.VMEM((local_neg, 2 * rows), BF16),
        ],
        micros=3.7, name="neg_grad",
    )
    bit = seq_count // 2
    got, sends = together(swap(proj_part, "seq", seq_count, bit), sends)
    while bit > 2:
        proj_part = call(sum_kernel, [proj_part, got], part, name=f"seq_sum_{bit}")
        bit //= 2
        got = swap(proj_part, "seq", seq_count, bit)
    proj_part = call(
        loss_sum_kernel,
        [guest_loss, proj_part, got],
        struct((part.shape[0] + 16, embed), BF16),
        name="seq_sum_2",
    )
    loss_got = swap(proj_part, "seq", seq_count, 1)
    proj_part = call(sum_kernel, [proj_part, loss_got], part, name="seq_sum_1")
    gots = [swap(x, "seq", seq_count, r) for r, x in enumerate(sends[1:], 2)]
    others = plane_swap([proj_part] * (chips - 1))
    first, _ = together(sends[0], others[chip - 1])
    others, gots = together(others, gots)
    gots = [swap(first, "seq", seq_count, 1)] + gots
    proj_parts = [proj_part] + others
    proj_parts += [swap(x, plane, plane_count, 1) for x in proj_parts]
    loss, d_neg, d_proj = call(
        functools.partial(final_kernel, seq_count - 1, 2 * chips),
        [info, loss, loss_got, *proj_parts, d_part, *gots],
        [struct((1, rows), F32), struct((cols, local_neg), F32), struct((width, embed), F32)],
        micros=2, name="final",
    )
    return (loss, d_neg.T[None], d_proj)


def solution(mesh):
    placed = (
        P(("batch", "pool"), "seq", None),
        P(),
        P(),
        P(),
        P(("batch", "pool"), "seq", None),
        P(("batch", "pool"), "seq"),
        P(("batch", "pool")),
        P("batch", "pool", None),
        P("batch", "pool"),
    )
    return jax.shard_map(
        body,
        mesh=mesh,
        in_specs=placed,
        out_specs=(P(("batch", "pool"), "seq"), P("batch", "pool", "seq"), P()),
        check_vma=False,
    )
```

```python
import functools
import itertools
import math

import jax
import jax.numpy as jnp
from jax import lax
from jax.experimental import pallas as pl
from jax.experimental.pallas import tpu as pltpu
from jax.sharding import PartitionSpec as P

HEADS = 8
ITEMS = 1048576

SOFTMAX_WARMTH = 0.02
NORM_EPSILON = 1e-05
UNIT_EPSILON = 1e-06
LOG2E = math.log2(math.e)
SCORE_SCALE = LOG2E / SOFTMAX_WARMTH
FAR = 10000.0

F32 = jnp.float32
BF16 = jnp.bfloat16
MIB = 1 << 20


def log_sample_chance(item_ids):
    x = 1.0 / (item_ids + 1.0)
    series = x * (1.0 - x * (1 / 2 - x * (1 / 3 - x * (1 / 4 - x * (1 / 5 - x * (1 / 6))))))
    return jnp.log(jnp.where(x > 1 / 16, jnp.log(1.0 + x), series)) - math.log(math.log(ITEMS + 1.0))


def column(row):
    return jnp.broadcast_to(row, (128, row.shape[1])).T[:, :1]


def dot(a, b):
    return jnp.dot(a, b, preferred_element_type=F32)


def dot_t(a, b):
    return lax.dot_general(a, b, (((1,), (1,)), ((), ())), preferred_element_type=F32)


def t_dot(a, b):
    return lax.dot_general(a, b, (((0,), (0,)), ((), ())), preferred_element_type=F32)


def silu(v):
    half = 0.5 * v
    return half + half * jnp.tanh(half)


def row_norm(x, keep=None):
    center = x - jnp.mean(x, axis=-1, keepdims=True)
    scale = lax.rsqrt(jnp.mean(center * center, axis=-1, keepdims=True) + NORM_EPSILON)
    if keep is not None:
        scale = jnp.where(keep, scale, 0.0)
    return center * scale


def norm_of(x):
    return jnp.sqrt(jnp.sum(x * x, axis=-1, keepdims=True) + UNIT_EPSILON)


def kept_rows(first, rows, length):
    return first + lax.broadcasted_iota(jnp.int32, (rows, 1), 0) < length


def attend(q_ref, keys, values, acc_ref, before_ref, causal=None):
    rows, width = q_ref.shape
    head = width // HEADS
    spans = [slice(h * head, (h + 1) * head) for h in range(HEADS)]
    following = dot_t(q_ref[:, spans[0]], keys[:, spans[0]])
    for h, cols in enumerate(spans):
        half = following * (0.5 / math.sqrt(head))
        if h + 1 < HEADS:
            following = dot_t(q_ref[:, spans[h + 1]], keys[:, spans[h + 1]])
        weights = half + half * jnp.tanh(half)
        if causal is not None:
            weights = jnp.where(causal, weights, 0.0)
        part = dot(weights.astype(BF16), values[:, cols])
        acc_ref[:, cols] = part if before_ref is None else before_ref[:, cols] + part


def project(normed, w_ref, block):
    width = normed.shape[1]
    return silu(dot(normed, w_ref[:, block * width : (block + 1) * width])).astype(BF16)


def causal_mask(rows):
    return lax.broadcasted_iota(jnp.int32, (rows, rows), 0) >= lax.broadcasted_iota(jnp.int32, (rows, rows), 1)


def fetch(pairs, sems):
    copies = [pltpu.make_async_copy(src, dst, sems.at[i]) for i, (src, dst) in enumerate(pairs)]
    for copy in copies:
        copy.start()
    return copies


def own_kernel(info_ref, x_hbm, w_hbm, gate_ref, q_ref, k_ref, v_ref, acc_ref, x_ref, w_ref, sems):
    rows, width = x_ref.shape
    parts = [2, 3, 1, 0]
    pairs = [(w_hbm.at[:, i * width : (i + 1) * width], w_ref.at[i]) for i in parts]
    copies = fetch([(x_hbm, x_ref)] + pairs, sems)
    copies[0].wait()
    keep = kept_rows(info_ref[0], rows, info_ref[1])
    normed = row_norm(x_ref[...].astype(F32), keep).astype(BF16)
    for copy, i, to_ref in zip(copies[1:], parts, [q_ref, k_ref, v_ref, gate_ref]):
        copy.wait()
        to_ref[...] = silu(dot(normed, w_ref[i])).astype(BF16)
    attend(q_ref, k_ref, v_ref, acc_ref, None, causal_mask(rows))


def guest_kernel(
    info_ref, x_ref, w_ref, k_ref, v_ref, own_x_ref, own_gate_ref, own_q_ref, own_acc_ref,
    all_x_ref, all_gate_ref, all_q_ref, all_acc_ref, guest_k_ref, guest_v_ref,
):
    rows = x_ref.shape[0]
    own, guest = slice(0, rows), slice(rows, 2 * rows)
    keep = kept_rows(info_ref[0] + rows, rows, info_ref[1])
    normed = row_norm(x_ref[...].astype(F32), keep).astype(BF16)
    all_x_ref[own, :], all_x_ref[guest, :] = own_x_ref[...], x_ref[...]
    all_gate_ref[own, :], all_gate_ref[guest, :] = own_gate_ref[...], project(normed, w_ref, 0)
    all_q_ref[own, :], all_q_ref[guest, :] = own_q_ref[...], project(normed, w_ref, 2)
    all_acc_ref[own, :] = own_acc_ref[...]
    guest_k_ref[...] = project(normed, w_ref, 3)
    guest_v_ref[...] = project(normed, w_ref, 1)
    q_ref, acc_ref = all_q_ref.at[guest, :], all_acc_ref.at[guest, :]
    attend(q_ref, guest_k_ref, guest_v_ref, acc_ref, None, causal_mask(rows))
    attend(q_ref, k_ref, v_ref, acc_ref, acc_ref)


def add_block(info_ref, back, x_ref, w_ref, q_ref, acc_ref, before_ref):
    keep = kept_rows(info_ref[0] - back, x_ref.shape[0], info_ref[1])
    normed = row_norm(x_ref[...].astype(F32), keep).astype(BF16)
    attend(q_ref, project(normed, w_ref, 3), project(normed, w_ref, 1), acc_ref, before_ref)


def step_kernel(back, info_ref, x_ref, w_ref, q_ref, before_ref, acc_ref):
    add_block(info_ref, back, x_ref, w_ref, q_ref, acc_ref, before_ref)


def last_kernel(
    back, info_ref, x_ref, w_ref, q_ref, before_ref, gate_ref, own_ref, w_out_ref, w_proj_ref,
    layer_ref, out_ref, hat_ref, acc_ref,
):
    add_block(info_ref, back, x_ref, w_ref, q_ref, acc_ref, before_ref)
    gated = (row_norm(acc_ref[...]) * gate_ref[...].astype(F32)).astype(BF16)
    layer = (dot(gated, w_out_ref[...]) + own_ref[...].astype(F32)).astype(BF16)
    layer_ref[...] = layer
    out = dot(layer, w_proj_ref[...])
    out_ref[...] = out
    hat_ref[...] = (out / norm_of(out)).astype(BF16)


def split3(x):
    high = x.astype(BF16).astype(F32)
    mid = (x - high).astype(BF16).astype(F32)
    return [high, mid, x - high - mid]


def id_digits(ids):
    return [(ids >> 14).astype(F32), ((ids >> 7) & 127).astype(F32), (ids & 127).astype(F32)]


def of_digits(a, b, c):
    return a * 16384.0 + b * 128.0 + c


def padded_rows(count):
    return -(-count // 16) * 16


def table_kernel(
    x_hbm, ids_hbm, pos_hbm, pos_ids_hbm, table_ref, message_ref, x_ref, ids_ref, pos_ref, pos_ids_ref, sems
):
    pairs = [(x_hbm, x_ref), (ids_hbm, ids_ref), (pos_hbm, pos_ref), (pos_ids_hbm, pos_ids_ref)]
    for copy in fetch(pairs, sems):
        copy.wait()
    count, embed = x_ref.shape
    x = x_ref[...].astype(F32)
    table_ref[:count, :] = (x / norm_of(x)).astype(BF16)
    ids = jnp.concatenate([ids_ref[:, i : i + embed] for i in range(0, count, embed)], axis=0)
    parts = split3(log_sample_chance(ids.astype(F32)) * LOG2E) + id_digits(ids)
    used = len(parts) * ids.shape[0]
    pad = jnp.zeros((table_ref.shape[0] - count - used, embed), F32)
    table_ref[count:, :] = jnp.concatenate(parts + [pad], axis=0).astype(BF16)
    rows = pos_ref.shape[0]
    parts = id_digits(pos_ids_ref[...])
    pad = jnp.zeros((message_ref.shape[0] - rows - len(parts), embed), F32)
    message_ref[:rows, :] = pos_ref[...]
    message_ref[rows:, :] = jnp.concatenate(parts + [pad], axis=0).astype(BF16)


def head_kernel(
    hist_count, info_ref, hat_ref, out_ref, layer_ref, pos_ref, ids_ref, guest_ref, *rest
):
    *table_refs, loss_ref, guest_loss_ref, message_ref, keep_ref, send_ref, proj_ref, kept_ref = rest
    rows, embed = hat_ref.shape
    block = rows // 2
    chunks = table_refs[0].shape[0] // (embed + 6)
    count = chunks * embed
    hat = hat_ref[...]
    guest_parts = guest_ref[block:, :].astype(F32)
    id_rows = [id_digits(ids_ref[...]), [guest_parts[i : i + 1, :] for i in range(3)]]
    id_row = jnp.concatenate([of_digits(*digits) for digits in id_rows], axis=1)
    pos_id = column(id_row)
    pos = jnp.concatenate([pos_ref[...], guest_ref[:block, :]], axis=0).astype(F32)
    pos_unit = pos / norm_of(pos)
    pos_score = (
        jnp.sum(hat.astype(F32) * pos_unit, axis=-1, keepdims=True) / SOFTMAX_WARMTH - column(log_sample_chance(id_row))
    )
    lanes = jnp.zeros((rows, 128), F32)
    grads = jnp.zeros((rows, embed), F32)
    steps = [(table_ref, chunk) for table_ref in table_refs for chunk in range(chunks)]

    def table_scores(table_ref, chunk):
        return dot_t(hat, table_ref[chunk * embed : (chunk + 1) * embed, :])

    following = table_scores(*steps[0])
    for step, (table_ref, chunk) in enumerate(steps):
        scores = following * SCORE_SCALE
        if step + 1 < len(steps):
            following = table_scores(*steps[step + 1])
        row = [table_ref[count:, :][i : i + 1, :].astype(F32) for i in range(chunk, 6 * chunks, chunks)]
        kept = jnp.where(of_digits(*row[3:]) != pos_id, jnp.exp2(scores - (row[0] + row[1] + row[2])), 0.0)
        for lane in range(0, embed, 128):
            lanes = lanes + kept[:, lane : lane + 128]
        kept_ref[:, chunk * embed : (chunk + 1) * embed] = kept.astype(BF16)
        if chunk == chunks - 1:
            grads = grads + dot(kept_ref[...], table_ref[:count, :])
    pos_part = jnp.exp(pos_score)
    total = pos_part + jnp.sum(lanes, axis=-1, keepdims=True)
    log_total = jnp.log(total)
    at = lax.broadcasted_iota(jnp.int32, (rows, 1), 0)
    valid = info_ref[0] + at < jnp.where(at < block, info_ref[5], info_ref[6])
    loss = jnp.where(valid, log_total - pos_score, 0.0)
    shift = jnp.where(valid, (log_total + math.log(hist_count)) * LOG2E, FAR)
    loss = jnp.broadcast_to(loss, (rows, 128)).T
    loss_ref[...] = loss[:1, :block]
    guest_loss_ref[...] = loss[:1, block:]
    shift = jnp.broadcast_to(shift, (rows, 128)).T
    parts = []
    for i in range(2):
        parts += split3(shift[:1, i * block : (i + 1) * block]) + id_rows[i]
    pad = jnp.zeros((message_ref.shape[0] - len(parts), embed), F32)
    message_ref[...] = jnp.concatenate(parts + [pad], axis=0).astype(BF16)
    share = jnp.where(valid, 1.0 / (total * hist_count), 0.0)
    pos_weight = jnp.where(valid, pos_part / total - 1.0, 0.0) / hist_count
    d_unit = (pos_weight * pos_unit + share * grads) / SOFTMAX_WARMTH
    out = out_ref[...]
    norms = norm_of(out)
    unit = out / norms
    d_out = ((d_unit - unit * jnp.sum(unit * d_unit, axis=-1, keepdims=True)) / norms).astype(BF16)
    proj_ref[...] = t_dot(layer_ref[...], d_out)
    half = keep_ref.shape[0]
    keep_ref[...] = proj_ref[part_at(info_ref[3], half), :]
    send_ref[...] = proj_ref[part_at(1 - info_ref[3], half), :].astype(BF16)


def part_at(index, rows):
    return pl.ds(pl.multiple_of(index * rows, rows), rows)


def halved_kernel(chip, info_ref, keep_ref, got_ref, message_ref, own_ref, *rest):
    *send_refs, sum_ref = rest
    rows = own_ref.shape[0]
    sum_ref[...] = keep_ref[...] + got_ref[...].astype(F32)
    own_ref[...] = sum_ref[part_at(info_ref[4], rows), :]
    for r, send_ref in enumerate(send_refs, 1):
        send_ref[:rows, :] = sum_ref[part_at(lax.bitwise_xor(info_ref[4], r), rows), :].astype(BF16)
        if r == chip:
            send_ref[rows:, :] = message_ref[...]


def sum_kernel(*refs):
    rows = refs[-1].shape[0]
    parts = [ref[:rows, :].astype(F32) for ref in refs[:-1]]
    while len(parts) > 1:
        parts = [a + b for a, b in zip(parts[::2], parts[1::2])]
    refs[-1][...] = parts[0].astype(refs[-1].dtype)


def lay_kernel(info_ref, *refs):
    *part_refs, out_ref = refs
    rows = part_refs[0].shape[0]
    chips = len(part_refs) // 2
    for i, part_ref in enumerate(part_refs):
        core, r = divmod(i, chips)
        at = lax.bitwise_xor(info_ref[3], core) * chips + lax.bitwise_xor(info_ref[4], r)
        out_ref[part_at(at, rows), :] = part_ref[...].astype(out_ref.dtype)


def loss_sum_kernel(loss_ref, *refs):
    *part_refs, out_ref = refs
    rows, events = part_refs[0].shape[0], loss_ref.shape[1]
    sum_kernel(*part_refs, out_ref.at[:rows, :])
    parts = split3(loss_ref[...])
    pad = jnp.zeros((16 - len(parts), events), F32)
    out_ref[rows:, :] = jnp.concatenate(parts + [pad], axis=0).astype(BF16)


def final_kernel(last, count, info_ref, loss_ref, loss_got_ref, *refs):
    proj_refs, (*part_refs, own_loss_ref, sum_ref, proj_ref) = refs[:count], refs[count:]
    parts = loss_got_ref[loss_got_ref.shape[0] - 16 :, :].astype(F32)
    above = parts[0:1, :] + parts[1:2, :] + parts[2:3, :]
    own_loss_ref[...] = jnp.where(info_ref[2] == last, above, loss_ref[...])
    lay_kernel(info_ref, *proj_refs, proj_ref)
    sum_kernel(*part_refs, sum_ref)


def negative_kernel(pool_count, info_ref, neg_ref, neg_id_ref, *rest):
    gathered, rest = rest[: 2 * pool_count], rest[2 * pool_count :]
    own_ref, *send_refs, turned_ref, sum_ref, weight_ref = rest
    count, embed = neg_ref.shape
    rows = embed
    blocks = gathered[0].shape[0] // rows
    tile = min(256, count)
    neg = neg_ref[...].astype(F32)
    norms = norm_of(neg)
    unit = neg / norms
    neg_hat = unit.astype(BF16)
    id_row = neg_id_ref[...].astype(F32)
    neg_id = column(id_row)
    for i, (hats_ref, message_ref) in enumerate(zip(gathered[:pool_count], gathered[pool_count:])):
        parts = message_ref[message_ref.shape[0] - 16 :, :].astype(F32)
        for block, start in itertools.product(range(blocks), range(0, count, tile)):
            own = slice(block * rows, (block + 1) * rows)
            cut = slice(start, start + tile)
            shift = [parts[6 * block + j : 6 * block + j + 1, :] for j in range(6)]
            scores = dot_t(neg_hat[cut, :], hats_ref[own, :]) * SCORE_SCALE - (shift[0] + shift[1] + shift[2])
            weights = jnp.where(neg_id[cut, :] != of_digits(*shift[3:]), jnp.exp2(scores), 0.0)
            weight_ref[cut, own] = weights.astype(BF16)
        for start in range(0, count, tile):
            cut = slice(start, start + tile)
            term = dot(weight_ref[cut, :], hats_ref[...])
            sum_ref[cut, :] = sum_ref[cut, :] + term if i else term
    neg_sum = sum_ref[...] * column(jnp.exp2(-LOG2E * log_sample_chance(id_row)) / SOFTMAX_WARMTH)
    grad = (neg_sum - unit * jnp.sum(unit * neg_sum, axis=-1, keepdims=True)) / norms
    turned_ref[...] = grad.T
    cols = own_ref.shape[0]
    own_ref[...] = turned_ref[part_at(info_ref[2], cols), :]
    for r, send_ref in enumerate(send_refs, 1):
        send_ref[...] = turned_ref[part_at(lax.bitwise_xor(info_ref[2], r), cols), :].astype(BF16)


def call(kernel, ins, outs, scratch=(), limit=24, micros=0.5, name=None, place=pltpu.VMEM):
    in_specs = [pl.BlockSpec(memory_space=pltpu.SMEM if x.ndim == 1 else place) for x in ins]
    many = isinstance(outs, (list, tuple))
    out_specs = jax.tree.map(lambda _: pl.BlockSpec(memory_space=pltpu.VMEM), outs)
    return pl.pallas_call(
        kernel,
        out_shape=list(outs) if many else outs,
        in_specs=in_specs,
        out_specs=list(out_specs) if many else out_specs,
        scratch_shapes=list(scratch),
        compiler_params=pltpu.CompilerParams(vmem_limit_bytes=limit * MIB),
        cost_estimate=pl.CostEstimate(flops=int(micros * 5.75e8), bytes_accessed=0, transcendentals=0),
        name=name,
    )(*ins)


def swap(x, axis, count, r):
    return lax.ppermute(x, axis, [(i, i ^ r) for i in range(count)])


def gather_step(blocks, axis, count):
    bit = count // (2 * len(blocks))
    return blocks + [swap(block, axis, count, bit) for block in blocks] if bit else blocks


def together(*trees):
    return lax.optimization_barrier(trees)


def struct(shape, kind):
    return jax.ShapeDtypeStruct(shape, kind)


def body(tokens, w_in, w_out, w_proj, pos_embed, pos_ids, lengths, neg_embed, neg_ids):
    rows, width = tokens.shape[1:]
    embed = w_proj.shape[1]
    seq_count = lax.axis_size("seq")
    pool_count = lax.axis_size("pool")
    plane = ("batch", "pool")
    plane_count = lax.axis_size("batch") * pool_count
    seq_at = lax.axis_index("seq")
    plane_at = lax.axis_index("batch") * pool_count + lax.axis_index("pool")
    own_end = jnp.where(seq_at == seq_count - 1, 0, lengths[0])
    guest_end = jnp.where(seq_at == seq_count - 2, lengths[0], 0)
    info = jnp.stack([seq_at * rows, lengths[0], seq_at, plane_at % 2, plane_at // 2, own_end, guest_end])
    info = info.astype(jnp.int32)
    own = tokens[0]
    local_neg = neg_embed.shape[1]

    ups = [[(i, i + 1) for i in range(hop, seq_count - 2)] for hop in range(seq_count - 2)]
    down = [(seq_count - 1, seq_count - 2)]
    block = lax.ppermute(own, "seq", ups[0])
    guest = lax.ppermute(own, "seq", down)
    kind = struct((rows, width), BF16)
    wide = struct((rows, width), F32)
    gate, queries, keys, values, acc = call(
        own_kernel,
        [info, own, w_in],
        [kind, kind, kind, kind, wide],
        scratch=[pltpu.VMEM((rows, width), BF16), pltpu.VMEM((4, width, width), BF16), pltpu.SemaphoreType.DMA((5,))],
        place=pl.ANY,
        limit=44,
        micros=6, name="own_block",
    )
    table_part, pos_part = call(
        table_kernel,
        [neg_embed[0], neg_ids, pos_embed[0], pos_ids],
        [
            struct((local_neg + padded_rows(6 * local_neg // embed), embed), BF16),
            struct((rows + 16, embed), BF16),
        ],
        scratch=[
            pltpu.VMEM((local_neg, embed), BF16), pltpu.VMEM((1, local_neg), jnp.int32),
            pltpu.VMEM((rows, embed), BF16), pltpu.VMEM((1, rows), jnp.int32), pltpu.SemaphoreType.DMA((4,)),
        ],
        place=pl.ANY,
        limit=24,
        micros=0.6, name="table_part",
    )
    table_part, pos_part, acc = together(table_part, pos_part, acc)
    table = gather_step([table_part], "pool", pool_count)
    block, acc = together(block, acc)
    tall = struct((2 * rows, width), BF16)
    tall_wide = struct((2 * rows, width), F32)
    for step in range(1, seq_count - 2):
        following = lax.ppermute(block, "seq", ups[step])
        if step == 1:
            own, gate, queries, acc = call(
                guest_kernel,
                [info, guest, w_in, keys, values, own, gate, queries, acc],
                [tall, tall, tall, tall_wide],
                scratch=[pltpu.VMEM((rows, width), BF16)] * 2,
                micros=4.8, name="guest_block",
            )
        acc = call(
            functools.partial(step_kernel, step * rows),
            [info, block, w_in, queries, acc],
            tall_wide,
            micros=3.6, name=f"earlier_block_{step}",
        )
        acc, table, pos_part = together(acc, table, pos_part)
        if step == 1:
            guest_pos = lax.ppermute(pos_part, "seq", down)
        table = gather_step(table, "pool", pool_count)
        block, acc = together(following, acc)
    while len(table) < pool_count:
        table = gather_step(table, "pool", pool_count)
    layer, out, hat = call(
        functools.partial(last_kernel, (seq_count - 2) * rows),
        [info, block, w_in, queries, acc, gate, own, w_out, w_proj],
        [tall, struct((2 * rows, embed), F32), struct((2 * rows, embed), BF16)],
        scratch=[pltpu.VMEM((2 * rows, width), F32)],
        micros=6, name="last_block",
    )
    hats = gather_step([hat], "pool", pool_count)

    half, chips = width // 2, plane_count // 2
    loss, guest_loss, message, keep, send = call(
        functools.partial(head_kernel, plane_count),
        [info, hat, out, layer, pos_embed[0], pos_ids, guest_pos, *table],
        [
            struct((1, rows), F32), struct((1, rows), F32), struct((16, embed), BF16),
            struct((half, embed), F32), struct((half, embed), BF16),
        ],
        scratch=[pltpu.VMEM((width, embed), F32), pltpu.VMEM((2 * rows, local_neg), BF16)],
        micros=5, name="head",
    )
    part = struct((half // chips, embed), BF16)
    cols = embed // seq_count
    def plane_swap(parts):
        return [swap(x, plane, plane_count, 2 * r) for r, x in enumerate(parts, 1)]

    chip = pool_count // 4
    sizes = [part.shape[0] + 16 * (r == chip) for r in range(1, chips)]
    own_part, *sends = call(
        functools.partial(halved_kernel, chip),
        [info, keep, swap(send, plane, plane_count, 1), message],
        [struct(part.shape, F32)] + [struct((size, embed), BF16) for size in sizes],
        scratch=[pltpu.VMEM((half, embed), F32)],
        micros=0.6, name="halved",
    )
    proj_parts = plane_swap(sends)
    proj_part = call(sum_kernel, [own_part] + proj_parts, part, name="plane_sum")
    while len(hats) < pool_count:
        hats = gather_step(hats, "pool", pool_count)
    messages = [message, proj_parts[chip - 1]]
    while len(messages) < pool_count:
        messages = gather_step(messages, "pool", pool_count)
    hats, messages, _ = together(hats, messages, proj_part)
    d_part, *sends = call(
        functools.partial(negative_kernel, pool_count),
        [info, neg_embed[0], neg_ids, *hats, *messages],
        [struct((cols, local_neg), F32)]
        + [struct((cols, local_neg), BF16)] * (seq_count - 1),
        scratch=[
            pltpu.VMEM((embed, local_neg), F32), pltpu.VMEM((local_neg, embed), F32),
            pltpu.VMEM((local_neg, 2 * rows), BF16),
        ],
        micros=3.7, name="neg_grad",
    )
    bit = seq_count // 2
    got, sends = together(swap(proj_part, "seq", seq_count, bit), sends)
    while bit > 2:
        proj_part = call(sum_kernel, [proj_part, got], part, name=f"seq_sum_{bit}")
        bit //= 2
        got = swap(proj_part, "seq", seq_count, bit)
    proj_part = call(
        loss_sum_kernel,
        [guest_loss, proj_part, got],
        struct((part.shape[0] + 16, embed), BF16),
        name="seq_sum_2",
    )
    loss_got = swap(proj_part, "seq", seq_count, 1)
    proj_part = call(sum_kernel, [proj_part, loss_got], part, name="seq_sum_1")
    gots = [swap(x, "seq", seq_count, r) for r, x in enumerate(sends[1:], 2)]
    others = plane_swap([proj_part] * (chips - 1))
    first, _ = together(sends[0], others[chip - 1])
    others, gots = together(others, gots)
    gots = [swap(first, "seq", seq_count, 1)] + gots
    proj_parts = [proj_part] + others
    proj_parts += [swap(x, plane, plane_count, 1) for x in proj_parts]
    loss, d_neg, d_proj = call(
        functools.partial(final_kernel, seq_count - 1, 2 * chips),
        [info, loss, loss_got, *proj_parts, d_part, *gots],
        [struct((1, rows), F32), struct((cols, local_neg), F32), struct((width, embed), F32)],
        micros=2, name="final",
    )
    return (loss, d_neg.T[None], d_proj)


def solution(mesh):
    placed = (
        P(("batch", "pool"), "seq", None),
        P(),
        P(),
        P(),
        P(("batch", "pool"), "seq", None),
        P(("batch", "pool"), "seq"),
        P(("batch", "pool")),
        P("batch", "pool", None),
        P("batch", "pool"),
    )
    return jax.shard_map(
        body,
        mesh=mesh,
        in_specs=placed,
        out_specs=(P(("batch", "pool"), "seq"), P("batch", "pool", "seq"), P()),
        check_vma=False,
    )
```

```python
import functools
import itertools
import math

import jax
import jax.numpy as jnp
from jax import lax
from jax.experimental import pallas as pl
from jax.experimental.pallas import tpu as pltpu
from jax.sharding import PartitionSpec as P

HEADS = 8
ITEMS = 1048576

SOFTMAX_WARMTH = 0.02
NORM_EPSILON = 1e-05
UNIT_EPSILON = 1e-06
LOG2E = math.log2(math.e)
SCORE_SCALE = LOG2E / SOFTMAX_WARMTH
FAR = 10000.0

F32 = jnp.float32
BF16 = jnp.bfloat16
MIB = 1 << 20


def log_sample_chance(item_ids):
    x = 1.0 / (item_ids + 1.0)
    series = x * (1.0 - x * (1 / 2 - x * (1 / 3 - x * (1 / 4 - x * (1 / 5 - x * (1 / 6))))))
    return jnp.log(jnp.where(x > 1 / 16, jnp.log(1.0 + x), series)) - math.log(math.log(ITEMS + 1.0))


def column(row):
    return jnp.broadcast_to(row, (128, row.shape[1])).T[:, :1]


def dot(a, b):
    return jnp.dot(a, b, preferred_element_type=F32)


def dot_t(a, b):
    return lax.dot_general(a, b, (((1,), (1,)), ((), ())), preferred_element_type=F32)


def t_dot(a, b):
    return lax.dot_general(a, b, (((0,), (0,)), ((), ())), preferred_element_type=F32)


def silu(v):
    half = 0.5 * v
    return half + half * jnp.tanh(half)


def row_norm(x, keep=None):
    center = x - jnp.mean(x, axis=-1, keepdims=True)
    scale = lax.rsqrt(jnp.mean(center * center, axis=-1, keepdims=True) + NORM_EPSILON)
    if keep is not None:
        scale = jnp.where(keep, scale, 0.0)
    return center * scale


def norm_of(x):
    return jnp.sqrt(jnp.sum(x * x, axis=-1, keepdims=True) + UNIT_EPSILON)


def kept_rows(first, rows, length):
    return first + lax.broadcasted_iota(jnp.int32, (rows, 1), 0) < length


def attend(q_ref, keys, values, acc_ref, before_ref, causal=None):
    rows, width = q_ref.shape
    head = width // HEADS
    spans = [slice(h * head, (h + 1) * head) for h in range(HEADS)]
    following = dot_t(q_ref[:, spans[0]], keys[:, spans[0]])
    for h, cols in enumerate(spans):
        half = following * (0.5 / math.sqrt(head))
        if h + 1 < HEADS:
            following = dot_t(q_ref[:, spans[h + 1]], keys[:, spans[h + 1]])
        weights = half + half * jnp.tanh(half)
        if causal is not None:
            weights = jnp.where(causal, weights, 0.0)
        part = dot(weights.astype(BF16), values[:, cols])
        acc_ref[:, cols] = part if before_ref is None else before_ref[:, cols] + part


def project(normed, w_ref, block):
    width = normed.shape[1]
    return silu(dot(normed, w_ref[:, block * width : (block + 1) * width])).astype(BF16)


def causal_mask(rows):
    return lax.broadcasted_iota(jnp.int32, (rows, rows), 0) >= lax.broadcasted_iota(jnp.int32, (rows, rows), 1)


def fetch(pairs, sems):
    copies = [pltpu.make_async_copy(src, dst, sems.at[i]) for i, (src, dst) in enumerate(pairs)]
    for copy in copies:
        copy.start()
    return copies


def own_kernel(info_ref, x_hbm, w_hbm, gate_ref, q_ref, k_ref, v_ref, acc_ref, x_ref, w_ref, sems):
    rows, width = x_ref.shape
    parts = [2, 3, 1, 0]
    pairs = [(w_hbm.at[:, i * width : (i + 1) * width], w_ref.at[i]) for i in parts]
    copies = fetch([(x_hbm, x_ref)] + pairs, sems)
    copies[0].wait()
    keep = kept_rows(info_ref[0], rows, info_ref[1])
    normed = row_norm(x_ref[...].astype(F32), keep).astype(BF16)
    for copy, i, to_ref in zip(copies[1:], parts, [q_ref, k_ref, v_ref, gate_ref]):
        copy.wait()
        to_ref[...] = silu(dot(normed, w_ref[i])).astype(BF16)
    attend(q_ref, k_ref, v_ref, acc_ref, None, causal_mask(rows))


def guest_kernel(
    info_ref, x_ref, w_ref, k_ref, v_ref, own_x_ref, own_gate_ref, own_q_ref, own_acc_ref,
    all_x_ref, all_gate_ref, all_q_ref, all_acc_ref, guest_k_ref, guest_v_ref,
):
    rows = x_ref.shape[0]
    own, guest = slice(0, rows), slice(rows, 2 * rows)
    keep = kept_rows(info_ref[0] + rows, rows, info_ref[1])
    normed = row_norm(x_ref[...].astype(F32), keep).astype(BF16)
    all_x_ref[own, :], all_x_ref[guest, :] = own_x_ref[...], x_ref[...]
    all_gate_ref[own, :], all_gate_ref[guest, :] = own_gate_ref[...], project(normed, w_ref, 0)
    all_q_ref[own, :], all_q_ref[guest, :] = own_q_ref[...], project(normed, w_ref, 2)
    all_acc_ref[own, :] = own_acc_ref[...]
    guest_k_ref[...] = project(normed, w_ref, 3)
    guest_v_ref[...] = project(normed, w_ref, 1)
    q_ref, acc_ref = all_q_ref.at[guest, :], all_acc_ref.at[guest, :]
    attend(q_ref, guest_k_ref, guest_v_ref, acc_ref, None, causal_mask(rows))
    attend(q_ref, k_ref, v_ref, acc_ref, acc_ref)


def add_block(info_ref, back, x_ref, w_ref, q_ref, acc_ref, before_ref):
    keep = kept_rows(info_ref[0] - back, x_ref.shape[0], info_ref[1])
    normed = row_norm(x_ref[...].astype(F32), keep).astype(BF16)
    attend(q_ref, project(normed, w_ref, 3), project(normed, w_ref, 1), acc_ref, before_ref)


def step_kernel(back, info_ref, x_ref, w_ref, q_ref, before_ref, acc_ref):
    add_block(info_ref, back, x_ref, w_ref, q_ref, acc_ref, before_ref)


def last_kernel(
    back, info_ref, x_ref, w_ref, q_ref, before_ref, gate_ref, own_ref, w_out_ref, w_proj_ref,
    layer_ref, out_ref, hat_ref, acc_ref,
):
    add_block(info_ref, back, x_ref, w_ref, q_ref, acc_ref, before_ref)
    gated = (row_norm(acc_ref[...]) * gate_ref[...].astype(F32)).astype(BF16)
    layer = (dot(gated, w_out_ref[...]) + own_ref[...].astype(F32)).astype(BF16)
    layer_ref[...] = layer
    out = dot(layer, w_proj_ref[...])
    out_ref[...] = out
    hat_ref[...] = (out / norm_of(out)).astype(BF16)


def split3(x):
    high = x.astype(BF16).astype(F32)
    mid = (x - high).astype(BF16).astype(F32)
    return [high, mid, x - high - mid]


def id_digits(ids):
    return [(ids >> 14).astype(F32), ((ids >> 7) & 127).astype(F32), (ids & 127).astype(F32)]


def of_digits(a, b, c):
    return a * 16384.0 + b * 128.0 + c


def padded_rows(count):
    return -(-count // 16) * 16


def table_kernel(
    x_hbm, ids_hbm, pos_hbm, pos_ids_hbm, table_ref, message_ref, x_ref, ids_ref, pos_ref, pos_ids_ref, sems
):
    pairs = [(x_hbm, x_ref), (ids_hbm, ids_ref), (pos_hbm, pos_ref), (pos_ids_hbm, pos_ids_ref)]
    for copy in fetch(pairs, sems):
        copy.wait()
    count, embed = x_ref.shape
    x = x_ref[...].astype(F32)
    table_ref[:count, :] = (x / norm_of(x)).astype(BF16)
    ids = jnp.concatenate([ids_ref[:, i : i + embed] for i in range(0, count, embed)], axis=0)
    parts = split3(log_sample_chance(ids.astype(F32)) * LOG2E) + id_digits(ids)
    used = len(parts) * ids.shape[0]
    pad = jnp.zeros((table_ref.shape[0] - count - used, embed), F32)
    table_ref[count:, :] = jnp.concatenate(parts + [pad], axis=0).astype(BF16)
    rows = pos_ref.shape[0]
    parts = id_digits(pos_ids_ref[...])
    pad = jnp.zeros((message_ref.shape[0] - rows - len(parts), embed), F32)
    message_ref[:rows, :] = pos_ref[...]
    message_ref[rows:, :] = jnp.concatenate(parts + [pad], axis=0).astype(BF16)


def head_kernel(
    hist_count, info_ref, hat_ref, out_ref, layer_ref, pos_ref, ids_ref, guest_ref, *rest
):
    *table_refs, loss_ref, guest_loss_ref, message_ref, keep_ref, send_ref, proj_ref, kept_ref = rest
    rows, embed = hat_ref.shape
    block = rows // 2
    chunks = table_refs[0].shape[0] // (embed + 6)
    count = chunks * embed
    hat = hat_ref[...]
    guest_parts = guest_ref[block:, :].astype(F32)
    id_rows = [id_digits(ids_ref[...]), [guest_parts[i : i + 1, :] for i in range(3)]]
    id_row = jnp.concatenate([of_digits(*digits) for digits in id_rows], axis=1)
    pos_id = column(id_row)
    pos = jnp.concatenate([pos_ref[...], guest_ref[:block, :]], axis=0).astype(F32)
    pos_unit = pos / norm_of(pos)
    pos_score = (
        jnp.sum(hat.astype(F32) * pos_unit, axis=-1, keepdims=True) / SOFTMAX_WARMTH - column(log_sample_chance(id_row))
    )
    lanes = jnp.zeros((rows, 128), F32)
    grads = jnp.zeros((rows, embed), F32)
    steps = [(table_ref, chunk) for table_ref in table_refs for chunk in range(chunks)]

    def table_scores(table_ref, chunk):
        return dot_t(hat, table_ref[chunk * embed : (chunk + 1) * embed, :])

    following = table_scores(*steps[0])
    for step, (table_ref, chunk) in enumerate(steps):
        scores = following * SCORE_SCALE
        if step + 1 < len(steps):
            following = table_scores(*steps[step + 1])
        row = [table_ref[count:, :][i : i + 1, :].astype(F32) for i in range(chunk, 6 * chunks, chunks)]
        kept = jnp.where(of_digits(*row[3:]) != pos_id, jnp.exp2(scores - (row[0] + row[1] + row[2])), 0.0)
        for lane in range(0, embed, 128):
            lanes = lanes + kept[:, lane : lane + 128]
        kept_ref[:, chunk * embed : (chunk + 1) * embed] = kept.astype(BF16)
        if chunk == chunks - 1:
            grads = grads + dot(kept_ref[...], table_ref[:count, :])
    pos_part = jnp.exp(pos_score)
    total = pos_part + jnp.sum(lanes, axis=-1, keepdims=True)
    log_total = jnp.log(total)
    at = lax.broadcasted_iota(jnp.int32, (rows, 1), 0)
    valid = info_ref[0] + at < jnp.where(at < block, info_ref[5], info_ref[6])
    loss = jnp.where(valid, log_total - pos_score, 0.0)
    shift = jnp.where(valid, (log_total + math.log(hist_count)) * LOG2E, FAR)
    loss = jnp.broadcast_to(loss, (rows, 128)).T
    loss_ref[...] = loss[:1, :block]
    guest_loss_ref[...] = loss[:1, block:]
    shift = jnp.broadcast_to(shift, (rows, 128)).T
    parts = []
    for i in range(2):
        parts += split3(shift[:1, i * block : (i + 1) * block]) + id_rows[i]
    pad = jnp.zeros((message_ref.shape[0] - len(parts), embed), F32)
    message_ref[...] = jnp.concatenate(parts + [pad], axis=0).astype(BF16)
    share = jnp.where(valid, 1.0 / (total * hist_count), 0.0)
    pos_weight = jnp.where(valid, pos_part / total - 1.0, 0.0) / hist_count
    d_unit = (pos_weight * pos_unit + share * grads) / SOFTMAX_WARMTH
    out = out_ref[...]
    norms = norm_of(out)
    unit = out / norms
    d_out = ((d_unit - unit * jnp.sum(unit * d_unit, axis=-1, keepdims=True)) / norms).astype(BF16)
    proj_ref[...] = t_dot(layer_ref[...], d_out)
    half = keep_ref.shape[0]
    keep_ref[...] = proj_ref[part_at(info_ref[3], half), :]
    send_ref[...] = proj_ref[part_at(1 - info_ref[3], half), :].astype(BF16)


def part_at(index, rows):
    return pl.ds(pl.multiple_of(index * rows, rows), rows)


def halved_kernel(chip, info_ref, keep_ref, got_ref, message_ref, own_ref, *rest):
    *send_refs, sum_ref = rest
    rows = own_ref.shape[0]
    sum_ref[...] = keep_ref[...] + got_ref[...].astype(F32)
    own_ref[...] = sum_ref[part_at(info_ref[4], rows), :]
    for r, send_ref in enumerate(send_refs, 1):
        send_ref[:rows, :] = sum_ref[part_at(lax.bitwise_xor(info_ref[4], r), rows), :].astype(BF16)
        if r == chip:
            send_ref[rows:, :] = message_ref[...]


def sum_kernel(*refs):
    rows = refs[-1].shape[0]
    parts = [ref[:rows, :].astype(F32) for ref in refs[:-1]]
    while len(parts) > 1:
        parts = [a + b for a, b in zip(parts[::2], parts[1::2])]
    refs[-1][...] = parts[0].astype(refs[-1].dtype)


def lay_kernel(info_ref, *refs):
    *part_refs, out_ref = refs
    rows = part_refs[0].shape[0]
    chips = len(part_refs) // 2
    for i, part_ref in enumerate(part_refs):
        core, r = divmod(i, chips)
        at = lax.bitwise_xor(info_ref[3], core) * chips + lax.bitwise_xor(info_ref[4], r)
        out_ref[part_at(at, rows), :] = part_ref[...].astype(out_ref.dtype)


def loss_sum_kernel(loss_ref, *refs):
    *part_refs, out_ref = refs
    rows, events = part_refs[0].shape[0], loss_ref.shape[1]
    sum_kernel(*part_refs, out_ref.at[:rows, :])
    parts = split3(loss_ref[...])
    pad = jnp.zeros((16 - len(parts), events), F32)
    out_ref[rows:, :] = jnp.concatenate(parts + [pad], axis=0).astype(BF16)


def final_kernel(last, count, info_ref, loss_ref, loss_got_ref, *refs):
    proj_refs, (*part_refs, own_loss_ref, sum_ref, proj_ref) = refs[:count], refs[count:]
    parts = loss_got_ref[loss_got_ref.shape[0] - 16 :, :].astype(F32)
    above = parts[0:1, :] + parts[1:2, :] + parts[2:3, :]
    own_loss_ref[...] = jnp.where(info_ref[2] == last, above, loss_ref[...])
    lay_kernel(info_ref, *proj_refs, proj_ref)
    sum_kernel(*part_refs, sum_ref)


def negative_kernel(pool_count, info_ref, neg_ref, neg_id_ref, *rest):
    gathered, rest = rest[: 2 * pool_count], rest[2 * pool_count :]
    own_ref, *send_refs, turned_ref, sum_ref, weight_ref = rest
    count, embed = neg_ref.shape
    rows = embed
    blocks = gathered[0].shape[0] // rows
    tile = min(256, count)
    neg = neg_ref[...].astype(F32)
    norms = norm_of(neg)
    unit = neg / norms
    neg_hat = unit.astype(BF16)
    id_row = neg_id_ref[...].astype(F32)
    neg_id = column(id_row)
    for i, (hats_ref, message_ref) in enumerate(zip(gathered[:pool_count], gathered[pool_count:])):
        parts = message_ref[message_ref.shape[0] - 16 :, :].astype(F32)
        for block, start in itertools.product(range(blocks), range(0, count, tile)):
            own = slice(block * rows, (block + 1) * rows)
            cut = slice(start, start + tile)
            shift = [parts[6 * block + j : 6 * block + j + 1, :] for j in range(6)]
            scores = dot_t(neg_hat[cut, :], hats_ref[own, :]) * SCORE_SCALE - (shift[0] + shift[1] + shift[2])
            weights = jnp.where(neg_id[cut, :] != of_digits(*shift[3:]), jnp.exp2(scores), 0.0)
            weight_ref[cut, own] = weights.astype(BF16)
        for start in range(0, count, tile):
            cut = slice(start, start + tile)
            term = dot(weight_ref[cut, :], hats_ref[...])
            sum_ref[cut, :] = sum_ref[cut, :] + term if i else term
    neg_sum = sum_ref[...] * column(jnp.exp2(-LOG2E * log_sample_chance(id_row)) / SOFTMAX_WARMTH)
    grad = (neg_sum - unit * jnp.sum(unit * neg_sum, axis=-1, keepdims=True)) / norms
    turned_ref[...] = grad.T
    cols = own_ref.shape[0]
    own_ref[...] = turned_ref[part_at(info_ref[2], cols), :]
    for r, send_ref in enumerate(send_refs, 1):
        send_ref[...] = turned_ref[part_at(lax.bitwise_xor(info_ref[2], r), cols), :].astype(BF16)


def call(kernel, ins, outs, scratch=(), limit=24, micros=0.5, name=None, place=pltpu.VMEM):
    in_specs = [pl.BlockSpec(memory_space=pltpu.SMEM if x.ndim == 1 else place) for x in ins]
    many = isinstance(outs, (list, tuple))
    out_specs = jax.tree.map(lambda _: pl.BlockSpec(memory_space=pltpu.VMEM), outs)
    return pl.pallas_call(
        kernel,
        out_shape=list(outs) if many else outs,
        in_specs=in_specs,
        out_specs=list(out_specs) if many else out_specs,
        scratch_shapes=list(scratch),
        compiler_params=pltpu.CompilerParams(vmem_limit_bytes=limit * MIB),
        cost_estimate=pl.CostEstimate(flops=int(micros * 5.75e8), bytes_accessed=0, transcendentals=0),
        name=name,
    )(*ins)


def swap(x, axis, count, r):
    return lax.ppermute(x, axis, [(i, i ^ r) for i in range(count)])


def gather_step(blocks, axis, count):
    bit = count // (2 * len(blocks))
    return blocks + [swap(block, axis, count, bit) for block in blocks] if bit else blocks


def together(*trees):
    return lax.optimization_barrier(trees)


def struct(shape, kind):
    return jax.ShapeDtypeStruct(shape, kind)


def body(tokens, w_in, w_out, w_proj, pos_embed, pos_ids, lengths, neg_embed, neg_ids):
    rows, width = tokens.shape[1:]
    embed = w_proj.shape[1]
    seq_count = lax.axis_size("seq")
    pool_count = lax.axis_size("pool")
    plane = ("batch", "pool")
    plane_count = lax.axis_size("batch") * pool_count
    seq_at = lax.axis_index("seq")
    plane_at = lax.axis_index("batch") * pool_count + lax.axis_index("pool")
    own_end = jnp.where(seq_at == seq_count - 1, 0, lengths[0])
    guest_end = jnp.where(seq_at == seq_count - 2, lengths[0], 0)
    info = jnp.stack([seq_at * rows, lengths[0], seq_at, plane_at % 2, plane_at // 2, own_end, guest_end])
    info = info.astype(jnp.int32)
    own = tokens[0]
    local_neg = neg_embed.shape[1]

    ups = [[(i, i + 1) for i in range(hop, seq_count - 2)] for hop in range(seq_count - 2)]
    down = [(seq_count - 1, seq_count - 2)]
    block = lax.ppermute(own, "seq", ups[0])
    guest = lax.ppermute(own, "seq", down)
    kind = struct((rows, width), BF16)
    wide = struct((rows, width), F32)
    gate, queries, keys, values, acc = call(
        own_kernel,
        [info, own, w_in],
        [kind, kind, kind, kind, wide],
        scratch=[pltpu.VMEM((rows, width), BF16), pltpu.VMEM((4, width, width), BF16), pltpu.SemaphoreType.DMA((5,))],
        place=pl.ANY,
        limit=44,
        micros=6, name="own_block",
    )
    table_part, pos_part = call(
        table_kernel,
        [neg_embed[0], neg_ids, pos_embed[0], pos_ids],
        [
            struct((local_neg + padded_rows(6 * local_neg // embed), embed), BF16),
            struct((rows + 16, embed), BF16),
        ],
        scratch=[
            pltpu.VMEM((local_neg, embed), BF16), pltpu.VMEM((1, local_neg), jnp.int32),
            pltpu.VMEM((rows, embed), BF16), pltpu.VMEM((1, rows), jnp.int32), pltpu.SemaphoreType.DMA((4,)),
        ],
        place=pl.ANY,
        limit=24,
        micros=0.6, name="table_part",
    )
    table = gather_step([table_part], "pool", pool_count)
    block, acc = together(block, acc)
    tall = struct((2 * rows, width), BF16)
    tall_wide = struct((2 * rows, width), F32)
    for step in range(1, seq_count - 2):
        following = lax.ppermute(block, "seq", ups[step])
        if step == 1:
            own, gate, queries, acc = call(
                guest_kernel,
                [info, guest, w_in, keys, values, own, gate, queries, acc],
                [tall, tall, tall, tall_wide],
                scratch=[pltpu.VMEM((rows, width), BF16)] * 2,
                micros=4.8, name="guest_block",
            )
        acc = call(
            functools.partial(step_kernel, step * rows),
            [info, block, w_in, queries, acc],
            tall_wide,
            micros=3.6, name=f"earlier_block_{step}",
        )
        acc, table, pos_part = together(acc, table, pos_part)
        if step == 1:
            guest_pos = lax.ppermute(pos_part, "seq", down)
        table = gather_step(table, "pool", pool_count)
        block, acc = together(following, acc)
    while len(table) < pool_count:
        table = gather_step(table, "pool", pool_count)
    layer, out, hat = call(
        functools.partial(last_kernel, (seq_count - 2) * rows),
        [info, block, w_in, queries, acc, gate, own, w_out, w_proj],
        [tall, struct((2 * rows, embed), F32), struct((2 * rows, embed), BF16)],
        scratch=[pltpu.VMEM((2 * rows, width), F32)],
        micros=6, name="last_block",
    )
    hats = gather_step([hat], "pool", pool_count)

    half, chips = width // 2, plane_count // 2
    loss, guest_loss, message, keep, send = call(
        functools.partial(head_kernel, plane_count),
        [info, hat, out, layer, pos_embed[0], pos_ids, guest_pos, *table],
        [
            struct((1, rows), F32), struct((1, rows), F32), struct((16, embed), BF16),
            struct((half, embed), F32), struct((half, embed), BF16),
        ],
        scratch=[pltpu.VMEM((width, embed), F32), pltpu.VMEM((2 * rows, local_neg), BF16)],
        micros=5, name="head",
    )
    part = struct((half // chips, embed), BF16)
    cols = embed // seq_count
    def plane_swap(parts):
        return [swap(x, plane, plane_count, 2 * r) for r, x in enumerate(parts, 1)]

    chip = pool_count // 4
    sizes = [part.shape[0] + 16 * (r == chip) for r in range(1, chips)]
    own_part, *sends = call(
        functools.partial(halved_kernel, chip),
        [info, keep, swap(send, plane, plane_count, 1), message],
        [struct(part.shape, F32)] + [struct((size, embed), BF16) for size in sizes],
        scratch=[pltpu.VMEM((half, embed), F32)],
        micros=0.6, name="halved",
    )
    proj_parts = plane_swap(sends)
    proj_part = call(sum_kernel, [own_part] + proj_parts, part, name="plane_sum")
    while len(hats) < pool_count:
        hats = gather_step(hats, "pool", pool_count)
    messages = [message, proj_parts[chip - 1]]
    while len(messages) < pool_count:
        messages = gather_step(messages, "pool", pool_count)
    hats, messages, _ = together(hats, messages, proj_part)
    d_part, *sends = call(
        functools.partial(negative_kernel, pool_count),
        [info, neg_embed[0], neg_ids, *hats, *messages],
        [struct((cols, local_neg), F32)]
        + [struct((cols, local_neg), BF16)] * (seq_count - 1),
        scratch=[
            pltpu.VMEM((embed, local_neg), F32), pltpu.VMEM((local_neg, embed), F32),
            pltpu.VMEM((local_neg, 2 * rows), BF16),
        ],
        micros=3.7, name="neg_grad",
    )
    bit = seq_count // 2
    got, sends = together(swap(proj_part, "seq", seq_count, bit), sends)
    while bit > 2:
        proj_part = call(sum_kernel, [proj_part, got], part, name=f"seq_sum_{bit}")
        bit //= 2
        got = swap(proj_part, "seq", seq_count, bit)
    proj_part = call(
        loss_sum_kernel,
        [guest_loss, proj_part, got],
        struct((part.shape[0] + 16, embed), BF16),
        name="seq_sum_2",
    )
    loss_got = swap(proj_part, "seq", seq_count, 1)
    proj_part = call(sum_kernel, [proj_part, loss_got], part, name="seq_sum_1")
    gots = [swap(x, "seq", seq_count, r) for r, x in enumerate(sends[1:], 2)]
    others = plane_swap([proj_part] * (chips - 1))
    first, _ = together(sends[0], others[chip - 1])
    others, gots = together(others, gots)
    gots = [swap(first, "seq", seq_count, 1)] + gots
    proj_parts = [proj_part] + others
    proj_parts += [swap(x, plane, plane_count, 1) for x in proj_parts]
    loss, d_neg, d_proj = call(
        functools.partial(final_kernel, seq_count - 1, 2 * chips),
        [info, loss, loss_got, *proj_parts, d_part, *gots],
        [struct((1, rows), F32), struct((cols, local_neg), F32), struct((width, embed), F32)],
        micros=2, name="final",
    )
    return (loss, d_neg.T[None], d_proj)


def solution(mesh):
    placed = (
        P(("batch", "pool"), "seq", None),
        P(),
        P(),
        P(),
        P(("batch", "pool"), "seq", None),
        P(("batch", "pool"), "seq"),
        P(("batch", "pool")),
        P("batch", "pool", None),
        P("batch", "pool"),
    )
    return jax.shard_map(
        body,
        mesh=mesh,
        in_specs=placed,
        out_specs=(P(("batch", "pool"), "seq"), P("batch", "pool", "seq"), P()),
        check_vma=False,
    )
```

```python
import functools
import itertools
import math

import jax
import jax.numpy as jnp
from jax import lax
from jax.experimental import pallas as pl
from jax.experimental.pallas import tpu as pltpu
from jax.sharding import PartitionSpec as P

HEADS = 8
ITEMS = 1048576

SOFTMAX_WARMTH = 0.02
NORM_EPSILON = 1e-05
UNIT_EPSILON = 1e-06
LOG2E = math.log2(math.e)
SCORE_SCALE = LOG2E / SOFTMAX_WARMTH
FAR = 10000.0

F32 = jnp.float32
BF16 = jnp.bfloat16
MIB = 1 << 20


def log_sample_chance(item_ids):
    x = 1.0 / (item_ids + 1.0)
    series = x * (1.0 - x * (1 / 2 - x * (1 / 3 - x * (1 / 4 - x * (1 / 5 - x * (1 / 6))))))
    return jnp.log(jnp.where(x > 1 / 16, jnp.log(1.0 + x), series)) - math.log(math.log(ITEMS + 1.0))


def column(row):
    return jnp.broadcast_to(row, (128, row.shape[1])).T[:, :1]


def dot(a, b):
    return jnp.dot(a, b, preferred_element_type=F32)


def dot_t(a, b):
    return lax.dot_general(a, b, (((1,), (1,)), ((), ())), preferred_element_type=F32)


def t_dot(a, b):
    return lax.dot_general(a, b, (((0,), (0,)), ((), ())), preferred_element_type=F32)


def silu(v):
    half = 0.5 * v
    return half + half * jnp.tanh(half)


def row_norm(x, keep=None):
    center = x - jnp.mean(x, axis=-1, keepdims=True)
    scale = lax.rsqrt(jnp.mean(center * center, axis=-1, keepdims=True) + NORM_EPSILON)
    if keep is not None:
        scale = jnp.where(keep, scale, 0.0)
    return center * scale


def norm_of(x):
    return jnp.sqrt(jnp.sum(x * x, axis=-1, keepdims=True) + UNIT_EPSILON)


def kept_rows(first, rows, length):
    return first + lax.broadcasted_iota(jnp.int32, (rows, 1), 0) < length


def attend(q_ref, keys, values, acc_ref, before_ref, causal=None):
    rows, width = q_ref.shape
    head = width // HEADS
    spans = [slice(h * head, (h + 1) * head) for h in range(HEADS)]
    following = dot_t(q_ref[:, spans[0]], keys[:, spans[0]])
    for h, cols in enumerate(spans):
        half = following * (0.5 / math.sqrt(head))
        if h + 1 < HEADS:
            following = dot_t(q_ref[:, spans[h + 1]], keys[:, spans[h + 1]])
        weights = half + half * jnp.tanh(half)
        if causal is not None:
            weights = jnp.where(causal, weights, 0.0)
        part = dot(weights.astype(BF16), values[:, cols])
        acc_ref[:, cols] = part if before_ref is None else before_ref[:, cols] + part


def project(normed, w_ref, block):
    width = normed.shape[1]
    return silu(dot(normed, w_ref[:, block * width : (block + 1) * width])).astype(BF16)


def causal_mask(rows):
    return lax.broadcasted_iota(jnp.int32, (rows, rows), 0) >= lax.broadcasted_iota(jnp.int32, (rows, rows), 1)


def fetch(pairs, sems):
    copies = [pltpu.make_async_copy(src, dst, sems.at[i]) for i, (src, dst) in enumerate(pairs)]
    for copy in copies:
        copy.start()
    return copies


def own_kernel(info_ref, x_hbm, w_hbm, q_ref, k_ref, v_ref, acc_ref, x_ref, w_ref, sems):
    rows, width = x_ref.shape
    parts = [2, 3, 1]
    pairs = [(w_hbm.at[:, i * width : (i + 1) * width], w_ref.at[i - 1]) for i in parts]
    copies = fetch([(x_hbm, x_ref)] + pairs, sems)
    copies[0].wait()
    keep = kept_rows(info_ref[0], rows, info_ref[1])
    normed = row_norm(x_ref[...].astype(F32), keep).astype(BF16)
    for copy, i, to_ref in zip(copies[1:], parts, [q_ref, k_ref, v_ref]):
        copy.wait()
        to_ref[...] = silu(dot(normed, w_ref[i - 1])).astype(BF16)
    attend(q_ref, k_ref, v_ref, acc_ref, None, causal_mask(rows))


def guest_kernel(
    info_ref, x_ref, w_ref, k_ref, v_ref, own_x_ref, own_q_ref, own_acc_ref,
    all_x_ref, all_gate_ref, all_q_ref, all_acc_ref, guest_k_ref, guest_v_ref,
):
    rows = x_ref.shape[0]
    own, guest = slice(0, rows), slice(rows, 2 * rows)
    keep = kept_rows(info_ref[0] + rows, rows, info_ref[1])
    normed = row_norm(x_ref[...].astype(F32), keep).astype(BF16)
    all_x_ref[own, :], all_x_ref[guest, :] = own_x_ref[...], x_ref[...]
    own_keep = kept_rows(info_ref[0], rows, info_ref[1])
    own_normed = row_norm(own_x_ref[...].astype(F32), own_keep).astype(BF16)
    all_gate_ref[...] = project(jnp.concatenate([own_normed, normed], axis=0), w_ref, 0)
    all_q_ref[own, :], all_q_ref[guest, :] = own_q_ref[...], project(normed, w_ref, 2)
    all_acc_ref[own, :] = own_acc_ref[...]
    guest_k_ref[...] = project(normed, w_ref, 3)
    guest_v_ref[...] = project(normed, w_ref, 1)
    q_ref, acc_ref = all_q_ref.at[guest, :], all_acc_ref.at[guest, :]
    attend(q_ref, guest_k_ref, guest_v_ref, acc_ref, None, causal_mask(rows))
    attend(q_ref, k_ref, v_ref, acc_ref, acc_ref)


def add_block(info_ref, back, x_ref, w_ref, q_ref, acc_ref, before_ref):
    keep = kept_rows(info_ref[0] - back, x_ref.shape[0], info_ref[1])
    normed = row_norm(x_ref[...].astype(F32), keep).astype(BF16)
    attend(q_ref, project(normed, w_ref, 3), project(normed, w_ref, 1), acc_ref, before_ref)


def step_kernel(back, info_ref, x_ref, w_ref, q_ref, before_ref, acc_ref):
    add_block(info_ref, back, x_ref, w_ref, q_ref, acc_ref, before_ref)


def last_kernel(
    back, info_ref, x_ref, w_ref, q_ref, before_ref, gate_ref, own_ref, w_out_ref, w_proj_ref,
    layer_ref, out_ref, hat_ref, acc_ref,
):
    add_block(info_ref, back, x_ref, w_ref, q_ref, acc_ref, before_ref)
    gated = (row_norm(acc_ref[...]) * gate_ref[...].astype(F32)).astype(BF16)
    layer = (dot(gated, w_out_ref[...]) + own_ref[...].astype(F32)).astype(BF16)
    layer_ref[...] = layer
    out = dot(layer, w_proj_ref[...])
    out_ref[...] = out
    hat_ref[...] = (out / norm_of(out)).astype(BF16)


def split3(x):
    high = x.astype(BF16).astype(F32)
    mid = (x - high).astype(BF16).astype(F32)
    return [high, mid, x - high - mid]


def id_digits(ids):
    return [(ids >> 14).astype(F32), ((ids >> 7) & 127).astype(F32), (ids & 127).astype(F32)]


def of_digits(a, b, c):
    return a * 16384.0 + b * 128.0 + c


def padded_rows(count):
    return -(-count // 16) * 16


def table_kernel(
    x_hbm, ids_hbm, pos_hbm, pos_ids_hbm, table_ref, message_ref, x_ref, ids_ref, pos_ref, pos_ids_ref, sems
):
    pairs = [(x_hbm, x_ref), (ids_hbm, ids_ref), (pos_hbm, pos_ref), (pos_ids_hbm, pos_ids_ref)]
    for copy in fetch(pairs, sems):
        copy.wait()
    count, embed = x_ref.shape
    x = x_ref[...].astype(F32)
    table_ref[:count, :] = (x / norm_of(x)).astype(BF16)
    ids = jnp.concatenate([ids_ref[:, i : i + embed] for i in range(0, count, embed)], axis=0)
    parts = split3(log_sample_chance(ids.astype(F32)) * LOG2E) + id_digits(ids)
    used = len(parts) * ids.shape[0]
    pad = jnp.zeros((table_ref.shape[0] - count - used, embed), F32)
    table_ref[count:, :] = jnp.concatenate(parts + [pad], axis=0).astype(BF16)
    rows = pos_ref.shape[0]
    parts = id_digits(pos_ids_ref[...])
    pad = jnp.zeros((message_ref.shape[0] - rows - len(parts), embed), F32)
    message_ref[:rows, :] = pos_ref[...]
    message_ref[rows:, :] = jnp.concatenate(parts + [pad], axis=0).astype(BF16)


def head_kernel(
    hist_count, info_ref, hat_ref, out_ref, layer_ref, pos_ref, ids_ref, guest_ref, *rest
):
    *table_refs, loss_ref, guest_loss_ref, message_ref, keep_ref, send_ref, proj_ref, kept_ref = rest
    rows, embed = hat_ref.shape
    block = rows // 2
    chunks = table_refs[0].shape[0] // (embed + 6)
    count = chunks * embed
    hat = hat_ref[...]
    guest_parts = guest_ref[block:, :].astype(F32)
    id_rows = [id_digits(ids_ref[...]), [guest_parts[i : i + 1, :] for i in range(3)]]
    id_row = jnp.concatenate([of_digits(*digits) for digits in id_rows], axis=1)
    pos_id = column(id_row)
    pos = jnp.concatenate([pos_ref[...], guest_ref[:block, :]], axis=0).astype(F32)
    pos_unit = pos / norm_of(pos)
    pos_score = (
        jnp.sum(hat.astype(F32) * pos_unit, axis=-1, keepdims=True) / SOFTMAX_WARMTH - column(log_sample_chance(id_row))
    )
    lanes = jnp.zeros((rows, 128), F32)
    grads = jnp.zeros((rows, embed), F32)
    steps = [(table_ref, chunk) for table_ref in table_refs for chunk in range(chunks)]

    def table_scores(table_ref, chunk):
        return dot_t(hat, table_ref[chunk * embed : (chunk + 1) * embed, :])

    following = table_scores(*steps[0])
    for step, (table_ref, chunk) in enumerate(steps):
        scores = following * SCORE_SCALE
        if step + 1 < len(steps):
            following = table_scores(*steps[step + 1])
        row = [table_ref[count:, :][i : i + 1, :].astype(F32) for i in range(chunk, 6 * chunks, chunks)]
        kept = jnp.where(of_digits(*row[3:]) != pos_id, jnp.exp2(scores - (row[0] + row[1] + row[2])), 0.0)
        for lane in range(0, embed, 128):
            lanes = lanes + kept[:, lane : lane + 128]
        kept_ref[:, chunk * embed : (chunk + 1) * embed] = kept.astype(BF16)
        if chunk == chunks - 1:
            grads = grads + dot(kept_ref[...], table_ref[:count, :])
    pos_part = jnp.exp(pos_score)
    total = pos_part + jnp.sum(lanes, axis=-1, keepdims=True)
    log_total = jnp.log(total)
    at = lax.broadcasted_iota(jnp.int32, (rows, 1), 0)
    valid = info_ref[0] + at < jnp.where(at < block, info_ref[5], info_ref[6])
    loss = jnp.where(valid, log_total - pos_score, 0.0)
    shift = jnp.where(valid, (log_total + math.log(hist_count)) * LOG2E, FAR)
    loss = jnp.broadcast_to(loss, (rows, 128)).T
    loss_ref[...] = loss[:1, :block]
    guest_loss_ref[...] = loss[:1, block:]
    shift = jnp.broadcast_to(shift, (rows, 128)).T
    parts = []
    for i in range(2):
        parts += split3(shift[:1, i * block : (i + 1) * block]) + id_rows[i]
    pad = jnp.zeros((message_ref.shape[0] - len(parts), embed), F32)
    message_ref[...] = jnp.concatenate(parts + [pad], axis=0).astype(BF16)
    share = jnp.where(valid, 1.0 / (total * hist_count), 0.0)
    pos_weight = jnp.where(valid, pos_part / total - 1.0, 0.0) / hist_count
    d_unit = (pos_weight * pos_unit + share * grads) / SOFTMAX_WARMTH
    out = out_ref[...]
    norms = norm_of(out)
    unit = out / norms
    d_out = ((d_unit - unit * jnp.sum(unit * d_unit, axis=-1, keepdims=True)) / norms).astype(BF16)
    proj_ref[...] = t_dot(layer_ref[...], d_out)
    half = keep_ref.shape[0]
    keep_ref[...] = proj_ref[part_at(info_ref[3], half), :]
    send_ref[...] = proj_ref[part_at(1 - info_ref[3], half), :].astype(BF16)


def part_at(index, rows):
    return pl.ds(pl.multiple_of(index * rows, rows), rows)


def halved_kernel(chip, info_ref, keep_ref, got_ref, message_ref, own_ref, *rest):
    *send_refs, sum_ref = rest
    rows = own_ref.shape[0]
    sum_ref[...] = keep_ref[...] + got_ref[...].astype(F32)
    own_ref[...] = sum_ref[part_at(info_ref[4], rows), :]
    for r, send_ref in enumerate(send_refs, 1):
        send_ref[:rows, :] = sum_ref[part_at(lax.bitwise_xor(info_ref[4], r), rows), :].astype(BF16)
        if r == chip:
            send_ref[rows:, :] = message_ref[...]


def sum_kernel(*refs):
    rows = refs[-1].shape[0]
    parts = [ref[:rows, :].astype(F32) for ref in refs[:-1]]
    while len(parts) > 1:
        parts = [a + b for a, b in zip(parts[::2], parts[1::2])]
    refs[-1][...] = parts[0].astype(refs[-1].dtype)


def lay_kernel(info_ref, *refs):
    *part_refs, out_ref = refs
    rows = part_refs[0].shape[0]
    chips = len(part_refs) // 2
    for i, part_ref in enumerate(part_refs):
        core, r = divmod(i, chips)
        at = lax.bitwise_xor(info_ref[3], core) * chips + lax.bitwise_xor(info_ref[4], r)
        out_ref[part_at(at, rows), :] = part_ref[...].astype(out_ref.dtype)


def loss_sum_kernel(loss_ref, *refs):
    *part_refs, out_ref = refs
    rows, events = part_refs[0].shape[0], loss_ref.shape[1]
    sum_kernel(*part_refs, out_ref.at[:rows, :])
    parts = split3(loss_ref[...])
    pad = jnp.zeros((16 - len(parts), events), F32)
    out_ref[rows:, :] = jnp.concatenate(parts + [pad], axis=0).astype(BF16)


def final_kernel(last, count, info_ref, loss_ref, loss_got_ref, *refs):
    proj_refs, (*part_refs, own_loss_ref, sum_ref, proj_ref) = refs[:count], refs[count:]
    parts = loss_got_ref[loss_got_ref.shape[0] - 16 :, :].astype(F32)
    above = parts[0:1, :] + parts[1:2, :] + parts[2:3, :]
    own_loss_ref[...] = jnp.where(info_ref[2] == last, above, loss_ref[...])
    lay_kernel(info_ref, *proj_refs, proj_ref)
    sum_kernel(*part_refs, sum_ref)


def negative_kernel(pool_count, info_ref, neg_ref, neg_id_ref, *rest):
    gathered, rest = rest[: 2 * pool_count], rest[2 * pool_count :]
    own_ref, *send_refs, turned_ref, sum_ref, weight_ref = rest
    count, embed = neg_ref.shape
    rows = embed
    blocks = gathered[0].shape[0] // rows
    tile = min(256, count)
    neg = neg_ref[...].astype(F32)
    norms = norm_of(neg)
    unit = neg / norms
    neg_hat = unit.astype(BF16)
    id_row = neg_id_ref[...].astype(F32)
    neg_id = column(id_row)
    for i, (hats_ref, message_ref) in enumerate(zip(gathered[:pool_count], gathered[pool_count:])):
        parts = message_ref[message_ref.shape[0] - 16 :, :].astype(F32)
        for block, start in itertools.product(range(blocks), range(0, count, tile)):
            own = slice(block * rows, (block + 1) * rows)
            cut = slice(start, start + tile)
            shift = [parts[6 * block + j : 6 * block + j + 1, :] for j in range(6)]
            scores = dot_t(neg_hat[cut, :], hats_ref[own, :]) * SCORE_SCALE - (shift[0] + shift[1] + shift[2])
            weights = jnp.where(neg_id[cut, :] != of_digits(*shift[3:]), jnp.exp2(scores), 0.0)
            weight_ref[cut, own] = weights.astype(BF16)
        for start in range(0, count, tile):
            cut = slice(start, start + tile)
            term = dot(weight_ref[cut, :], hats_ref[...])
            sum_ref[cut, :] = sum_ref[cut, :] + term if i else term
    neg_sum = sum_ref[...] * column(jnp.exp2(-LOG2E * log_sample_chance(id_row)) / SOFTMAX_WARMTH)
    grad = (neg_sum - unit * jnp.sum(unit * neg_sum, axis=-1, keepdims=True)) / norms
    turned_ref[...] = grad.T
    cols = own_ref.shape[0]
    own_ref[...] = turned_ref[part_at(info_ref[2], cols), :]
    for r, send_ref in enumerate(send_refs, 1):
        send_ref[...] = turned_ref[part_at(lax.bitwise_xor(info_ref[2], r), cols), :].astype(BF16)


def call(kernel, ins, outs, scratch=(), limit=24, micros=0.5, name=None, place=pltpu.VMEM):
    in_specs = [pl.BlockSpec(memory_space=pltpu.SMEM if x.ndim == 1 else place) for x in ins]
    many = isinstance(outs, (list, tuple))
    out_specs = jax.tree.map(lambda _: pl.BlockSpec(memory_space=pltpu.VMEM), outs)
    return pl.pallas_call(
        kernel,
        out_shape=list(outs) if many else outs,
        in_specs=in_specs,
        out_specs=list(out_specs) if many else out_specs,
        scratch_shapes=list(scratch),
        compiler_params=pltpu.CompilerParams(vmem_limit_bytes=limit * MIB),
        cost_estimate=pl.CostEstimate(flops=int(micros * 5.75e8), bytes_accessed=0, transcendentals=0),
        name=name,
    )(*ins)


def swap(x, axis, count, r):
    return lax.ppermute(x, axis, [(i, i ^ r) for i in range(count)])


def gather_step(blocks, axis, count):
    bit = count // (2 * len(blocks))
    return blocks + [swap(block, axis, count, bit) for block in blocks] if bit else blocks


def together(*trees):
    return lax.optimization_barrier(trees)


def struct(shape, kind):
    return jax.ShapeDtypeStruct(shape, kind)


def body(tokens, w_in, w_out, w_proj, pos_embed, pos_ids, lengths, neg_embed, neg_ids):
    rows, width = tokens.shape[1:]
    embed = w_proj.shape[1]
    seq_count = lax.axis_size("seq")
    pool_count = lax.axis_size("pool")
    plane = ("batch", "pool")
    plane_count = lax.axis_size("batch") * pool_count
    seq_at = lax.axis_index("seq")
    plane_at = lax.axis_index("batch") * pool_count + lax.axis_index("pool")
    own_end = jnp.where(seq_at == seq_count - 1, 0, lengths[0])
    guest_end = jnp.where(seq_at == seq_count - 2, lengths[0], 0)
    info = jnp.stack([seq_at * rows, lengths[0], seq_at, plane_at % 2, plane_at // 2, own_end, guest_end])
    info = info.astype(jnp.int32)
    own = tokens[0]
    local_neg = neg_embed.shape[1]

    ups = [[(i, i + 1) for i in range(hop, seq_count - 2)] for hop in range(seq_count - 2)]
    down = [(seq_count - 1, seq_count - 2)]
    block = lax.ppermute(own, "seq", ups[0])
    guest = lax.ppermute(own, "seq", down)
    kind = struct((rows, width), BF16)
    wide = struct((rows, width), F32)
    queries, keys, values, acc = call(
        own_kernel,
        [info, own, w_in],
        [kind, kind, kind, wide],
        scratch=[pltpu.VMEM((rows, width), BF16), pltpu.VMEM((3, width, width), BF16), pltpu.SemaphoreType.DMA((4,))],
        place=pl.ANY,
        limit=44,
        micros=6, name="own_block",
    )
    table_part, pos_part = call(
        table_kernel,
        [neg_embed[0], neg_ids, pos_embed[0], pos_ids],
        [
            struct((local_neg + padded_rows(6 * local_neg // embed), embed), BF16),
            struct((rows + 16, embed), BF16),
        ],
        scratch=[
            pltpu.VMEM((local_neg, embed), BF16), pltpu.VMEM((1, local_neg), jnp.int32),
            pltpu.VMEM((rows, embed), BF16), pltpu.VMEM((1, rows), jnp.int32), pltpu.SemaphoreType.DMA((4,)),
        ],
        place=pl.ANY,
        limit=24,
        micros=0.6, name="table_part",
    )
    table = gather_step([table_part], "pool", pool_count)
    block, acc = together(block, acc)
    tall = struct((2 * rows, width), BF16)
    tall_wide = struct((2 * rows, width), F32)
    for step in range(1, seq_count - 2):
        following = lax.ppermute(block, "seq", ups[step])
        if step == 1:
            own, gate, queries, acc = call(
                guest_kernel,
                [info, guest, w_in, keys, values, own, queries, acc],
                [tall, tall, tall, tall_wide],
                scratch=[pltpu.VMEM((rows, width), BF16)] * 2,
                micros=4.8, name="guest_block",
            )
        acc = call(
            functools.partial(step_kernel, step * rows),
            [info, block, w_in, queries, acc],
            tall_wide,
            micros=3.6, name=f"earlier_block_{step}",
        )
        acc, table, pos_part = together(acc, table, pos_part)
        if step == 1:
            guest_pos = lax.ppermute(pos_part, "seq", down)
        table = gather_step(table, "pool", pool_count)
        block, acc = together(following, acc)
    while len(table) < pool_count:
        table = gather_step(table, "pool", pool_count)
    layer, out, hat = call(
        functools.partial(last_kernel, (seq_count - 2) * rows),
        [info, block, w_in, queries, acc, gate, own, w_out, w_proj],
        [tall, struct((2 * rows, embed), F32), struct((2 * rows, embed), BF16)],
        scratch=[pltpu.VMEM((2 * rows, width), F32)],
        micros=6, name="last_block",
    )
    hats = gather_step([hat], "pool", pool_count)

    half, chips = width // 2, plane_count // 2
    loss, guest_loss, message, keep, send = call(
        functools.partial(head_kernel, plane_count),
        [info, hat, out, layer, pos_embed[0], pos_ids, guest_pos, *table],
        [
            struct((1, rows), F32), struct((1, rows), F32), struct((16, embed), BF16),
            struct((half, embed), F32), struct((half, embed), BF16),
        ],
        scratch=[pltpu.VMEM((width, embed), F32), pltpu.VMEM((2 * rows, local_neg), BF16)],
        micros=5, name="head",
    )
    part = struct((half // chips, embed), BF16)
    cols = embed // seq_count
    def plane_swap(parts):
        return [swap(x, plane, plane_count, 2 * r) for r, x in enumerate(parts, 1)]

    chip = pool_count // 4
    sizes = [part.shape[0] + 16 * (r == chip) for r in range(1, chips)]
    own_part, *sends = call(
        functools.partial(halved_kernel, chip),
        [info, keep, swap(send, plane, plane_count, 1), message],
        [struct(part.shape, F32)] + [struct((size, embed), BF16) for size in sizes],
        scratch=[pltpu.VMEM((half, embed), F32)],
        micros=0.6, name="halved",
    )
    proj_parts = plane_swap(sends)
    proj_part = call(sum_kernel, [own_part] + proj_parts, part, name="plane_sum")
    while len(hats) < pool_count:
        hats = gather_step(hats, "pool", pool_count)
    messages = [message, proj_parts[chip - 1]]
    while len(messages) < pool_count:
        messages = gather_step(messages, "pool", pool_count)
    hats, messages, _ = together(hats, messages, proj_part)
    d_part, *sends = call(
        functools.partial(negative_kernel, pool_count),
        [info, neg_embed[0], neg_ids, *hats, *messages],
        [struct((cols, local_neg), F32)]
        + [struct((cols, local_neg), BF16)] * (seq_count - 1),
        scratch=[
            pltpu.VMEM((embed, local_neg), F32), pltpu.VMEM((local_neg, embed), F32),
            pltpu.VMEM((local_neg, 2 * rows), BF16),
        ],
        micros=3.7, name="neg_grad",
    )
    bit = seq_count // 2
    got, sends = together(swap(proj_part, "seq", seq_count, bit), sends)
    while bit > 2:
        proj_part = call(sum_kernel, [proj_part, got], part, name=f"seq_sum_{bit}")
        bit //= 2
        got = swap(proj_part, "seq", seq_count, bit)
    proj_part = call(
        loss_sum_kernel,
        [guest_loss, proj_part, got],
        struct((part.shape[0] + 16, embed), BF16),
        name="seq_sum_2",
    )
    loss_got = swap(proj_part, "seq", seq_count, 1)
    proj_part = call(sum_kernel, [proj_part, loss_got], part, name="seq_sum_1")
    gots = [swap(x, "seq", seq_count, r) for r, x in enumerate(sends[1:], 2)]
    others = plane_swap([proj_part] * (chips - 1))
    first, _ = together(sends[0], others[chip - 1])
    others, gots = together(others, gots)
    gots = [swap(first, "seq", seq_count, 1)] + gots
    proj_parts = [proj_part] + others
    proj_parts += [swap(x, plane, plane_count, 1) for x in proj_parts]
    loss, d_neg, d_proj = call(
        functools.partial(final_kernel, seq_count - 1, 2 * chips),
        [info, loss, loss_got, *proj_parts, d_part, *gots],
        [struct((1, rows), F32), struct((cols, local_neg), F32), struct((width, embed), F32)],
        micros=2, name="final",
    )
    return (loss, d_neg.T[None], d_proj)


def solution(mesh):
    placed = (
        P(("batch", "pool"), "seq", None),
        P(),
        P(),
        P(),
        P(("batch", "pool"), "seq", None),
        P(("batch", "pool"), "seq"),
        P(("batch", "pool")),
        P("batch", "pool", None),
        P("batch", "pool"),
    )
    return jax.shard_map(
        body,
        mesh=mesh,
        in_specs=placed,
        out_specs=(P(("batch", "pool"), "seq"), P("batch", "pool", "seq"), P()),
        check_vma=False,
    )
```
